256 devices in a mesh: gx: 128 (over z, y_hi, x, core), gz: 2 (over y_lo).
Axes of the slice: x: 4, y: 4 (y_hi: 2, y_lo: 2; y = y_hi * 2 + y_lo), z: 8, core: 2. Of those that a mesh axis runs over, the one named last changes fastest.
Arguments:
- thermal_anomaly: float32 [128, 768, 512], P('gz', 'gx'), may hold values from -6 to 6
- saltiness_anomaly: float32 [128, 768, 512], P('gz', 'gx'), may hold values from -6 to 6
- eastward_flow: float32 [128, 768, 512], P('gz', 'gx'), may hold values from -6 to 6
- advective_ratio: float32 [128, 768, 512], P('gz', 'gx'), may hold values from -0.8 to 0.8
- dual_thermal_final: float32 [128, 768, 512], P('gz', 'gx'), may hold values from -6 to 6
- dual_saltiness_final: float32 [128, 768, 512], P('gz', 'gx'), may hold values from -6 to 6
- dual_flow_final: float32 [128, 768, 512], P('gz', 'gx'), may hold values from -6 to 6
- dual_kinematic_head: float32 [128, 768, 512], P('gz', 'gx'), may hold values from -6 to 6
- depth_into_eigenbasis: float32 [128, 128], replicated, may hold values from -1 to 1.25
- eigenbasis_into_depth: float32 [128, 128], replicated, may hold values from -1 to 1.25
- spectral_magnitudes: float32 [128], replicated, may hold values from 0.003 to 1
Outputs:
- dual_thermal_initial: float32 [128, 768, 512], P('gz', 'gx')
- dual_saltiness_initial: float32 [128, 768, 512], P('gz', 'gx')
- dual_flow_initial: float32 [128, 768, 512], P('gz', 'gx')
- dual_interface_ratio: float32 [128, 768, 512], P('gz', 'gx')
- dual_poisson_forcing: float32 [128, 768, 512], P('gz', 'gx')
The draws below stay inside these ranges and needn't reach their ends.
All inputs are finite; a program needn't handle non-finite values.
Results may differ from the reference program's by a relative error of at most 0.0003.
Values sent between devices are 32-bit elements; how exact they have to be, the bound alone decides.
No kernel may reach another device: no remote copies, remote signals or barrier semaphores. Data moves between devices by JAX's collectives and lax.ppermute only.
A program may use at most 192 MiB of HBM per device.

```python
import math
import jax
import jax.numpy as jnp
from jax import lax

EASTWARD_COUNT = 768
NORTHWARD_COUNT = 512
DEPTH_LAYERS = 128


def mode_matrix(key, offdiag):
    diagonal = jax.random.uniform(key, (DEPTH_LAYERS,), jnp.float32, 0.8, 1.2)
    identity = jnp.eye(DEPTH_LAYERS, dtype=jnp.float32)
    return identity * diagonal[None, :] + (1.0 - identity) * offdiag * (0.4 / math.sqrt(DEPTH_LAYERS))


def draw_dual_kinematic_head(key, part):
    key = jax.random.fold_in(key, 11)
    return jnp.clip(jax.random.normal(key, (DEPTH_LAYERS, EASTWARD_COUNT, NORTHWARD_COUNT), jnp.float32), -6.0, 6.0)


def draw_depth_into_eigenbasis(key, part):
    key = jax.random.fold_in(key, 21)
    spread_key = jax.random.fold_in(key, 5)
    offdiag = jnp.clip(jax.random.normal(spread_key, (DEPTH_LAYERS, DEPTH_LAYERS), jnp.float32), -4.0, 4.0)
    return mode_matrix(key, offdiag)


def draw_eigenbasis_into_depth(key, part):
    key = jax.random.fold_in(key, 22)
    spread_key = jax.random.fold_in(key, 5)
    offdiag = jnp.clip(jax.random.normal(spread_key, (DEPTH_LAYERS, DEPTH_LAYERS), jnp.float32), -4.0, 4.0)
    return mode_matrix(key, offdiag)


def shard_levels(own_key, shape, cuts, low, largest):
    factor_of, own = 1.0, jax.random.fold_in(own_key, 6)
    for axis_at, parts in cuts:
        draws = jnp.exp(jax.random.uniform(jax.random.fold_in(own, axis_at), (parts,), jnp.float32, low / len(cuts), largest / len(cuts)))
        factor_of = factor_of * jnp.repeat(draws, shape[axis_at] // parts).reshape([-1 if axis == axis_at else 1 for axis in range(len(shape))])
    return factor_of


def noise(stream_key, shape, deviation, most, shards=(), held_as=jnp.bfloat16):
    drawn = deviation * jax.random.normal(stream_key, shape, jnp.float32)
    if shards:
        drawn = drawn * shard_levels(stream_key, shape, shards, -0.22, 0.18)
    return jnp.clip(drawn, -most, most).astype(held_as)


def setup_inputs(seed: int = 0) -> dict:
    keys = jax.random.split(jax.random.key(seed), 12)
    return {
        "thermal_anomaly": noise(keys[0], (DEPTH_LAYERS, EASTWARD_COUNT, NORTHWARD_COUNT), 1.0, 6.0, ((0, 2), (1, 128)), jnp.float32),
        "saltiness_anomaly": noise(keys[1], (DEPTH_LAYERS, EASTWARD_COUNT, NORTHWARD_COUNT), 1.0, 6.0, ((0, 2), (1, 128)), jnp.float32),
        "eastward_flow": noise(keys[2], (DEPTH_LAYERS, EASTWARD_COUNT, NORTHWARD_COUNT), 1.0, 6.0, ((0, 2), (1, 128)), jnp.float32),
        "advective_ratio": jnp.clip(jax.random.uniform(keys[3], (DEPTH_LAYERS, EASTWARD_COUNT, NORTHWARD_COUNT), jnp.float32, -0.8, 0.8) * shard_levels(keys[3], (DEPTH_LAYERS, EASTWARD_COUNT, NORTHWARD_COUNT), ((0, 2), (1, 128)), -0.4, 0.0), -0.8, 0.8),
        "dual_thermal_final": noise(keys[4], (DEPTH_LAYERS, EASTWARD_COUNT, NORTHWARD_COUNT), 1.0, 6.0, ((0, 2), (1, 128)), jnp.float32),
        "dual_saltiness_final": noise(keys[5], (DEPTH_LAYERS, EASTWARD_COUNT, NORTHWARD_COUNT), 1.0, 6.0, ((0, 2), (1, 128)), jnp.float32),
        "dual_flow_final": noise(keys[6], (DEPTH_LAYERS, EASTWARD_COUNT, NORTHWARD_COUNT), 1.0, 6.0, ((0, 2), (1, 128)), jnp.float32),
        "dual_kinematic_head": draw_dual_kinematic_head(jax.random.fold_in(keys[11], 71), 0),
        "depth_into_eigenbasis": draw_depth_into_eigenbasis(jax.random.fold_in(keys[11], 71), 0),
        "eigenbasis_into_depth": draw_eigenbasis_into_depth(jax.random.fold_in(keys[11], 71), 0),
        "spectral_magnitudes": jnp.clip(jnp.exp(jax.random.uniform(keys[10], (DEPTH_LAYERS,), jnp.float32, math.log(0.003), math.log(1.0))), 0.003, 1.0),
    }


smooth_floor = 0.01
highest = lax.Precision.HIGHEST

def reconstruct(far_left, near_left, center, near_right, far_right):
    first_poly = (2.0 * far_left - 7.0 * near_left + 11.0 * center) / 6.0
    second_poly = (-near_left + 5.0 * center + 2.0 * near_right) / 6.0
    third_poly = (2.0 * center + 5.0 * near_right - far_right) / 6.0
    first_smooth = 13.0 / 12.0 * (far_left - 2.0 * near_left + center) ** 2 + 0.25 * (far_left - 4.0 * near_left + 3.0 * center) ** 2
    second_smooth = 13.0 / 12.0 * (near_left - 2.0 * center + near_right) ** 2 + 0.25 * (near_left - near_right) ** 2
    third_smooth = 13.0 / 12.0 * (center - 2.0 * near_right + far_right) ** 2 + 0.25 * (3.0 * center - 4.0 * near_right + far_right) ** 2
    first_alpha = 0.1 / (smooth_floor + first_smooth) ** 2
    second_alpha = 0.6 / (smooth_floor + second_smooth) ** 2
    third_alpha = 0.3 / (smooth_floor + third_smooth) ** 2
    total = first_alpha + second_alpha + third_alpha
    return (first_alpha * first_poly + second_alpha * second_poly + third_alpha * third_poly) / total

def face_flux(minus_three, minus_two, minus_one, middle, plus_one, plus_two, advective_ratio):
    upwind_left = reconstruct(minus_three, minus_two, minus_one, middle, plus_one)
    upwind_right = reconstruct(plus_two, plus_one, middle, minus_one, minus_two)
    return advective_ratio * jnp.where(advective_ratio >= 0.0, upwind_left, upwind_right)

def advect(stored_numbers_array, advective_ratio):
    shifted = [jnp.roll(stored_numbers_array, offset, axis=0) for offset in (3, 2, 1, 0, -1, -2)]
    fluxes = face_flux(shifted[0], shifted[1], shifted[2], shifted[3], shifted[4], shifted[5], advective_ratio)
    return stored_numbers_array - jnp.roll(fluxes, -1, axis=0) + fluxes

def dual_by_depth_layer(lone_depth_sheet):
    thermal_anomaly, saltiness_anomaly, eastward_flow, advective_ratio, dual_thermal_final, dual_saltiness_final, tentative_flow_speed = lone_depth_sheet
    courant_total = jnp.zeros_like(advective_ratio)
    results = []
    for stored_numbers_array, upstream_sensitivity in ((thermal_anomaly, dual_thermal_final), (saltiness_anomaly, dual_saltiness_final), (eastward_flow, tentative_flow_speed)):
        unused, pullback = jax.vjp(advect, stored_numbers_array, advective_ratio)
        values_bar, courant_bar = pullback(upstream_sensitivity)
        results.append(values_bar)
        courant_total = courant_total + courant_bar
    return (results[0], results[1], results[2], courant_total)

def hartley(stored_numbers_array, dimension):
    transform = jnp.fft.fft(stored_numbers_array, axis=dimension)
    return jnp.real(transform) - jnp.imag(transform)

def reference(thermal_anomaly, saltiness_anomaly, eastward_flow, advective_ratio, dual_thermal_final, dual_saltiness_final, dual_flow_final, dual_kinematic_head, depth_into_eigenbasis, eigenbasis_into_depth, spectral_magnitudes):
    spectrum = hartley(hartley(dual_kinematic_head, 2), 1)
    projected = jnp.einsum('mz,zxy->mxy', depth_into_eigenbasis, spectrum, precision=highest)
    wave_x = 2.0 - 2.0 * jnp.cos(jnp.arange(EASTWARD_COUNT, dtype=jnp.float32) * (2.0 * math.pi / EASTWARD_COUNT))
    wave_y = 2.0 - 2.0 * jnp.cos(jnp.arange(NORTHWARD_COUNT, dtype=jnp.float32) * (2.0 * math.pi / NORTHWARD_COUNT))
    divisor = spectral_magnitudes[:, None, None] + wave_x[None, :, None] + wave_y[None, None, :]
    scaled = -projected / (divisor * (EASTWARD_COUNT * NORTHWARD_COUNT))
    restored = jnp.einsum('zm,mxy->zxy', eigenbasis_into_depth, scaled, precision=highest)
    dual_poisson_forcing = hartley(hartley(restored, 2), 1)
    tentative_flow_speed = dual_flow_final + jnp.roll(dual_poisson_forcing, 1, axis=1) - dual_poisson_forcing
    dual_thermal_initial, dual_saltiness_initial, dual_flow_initial, dual_interface_ratio = lax.map(dual_by_depth_layer, (thermal_anomaly, saltiness_anomaly, eastward_flow, advective_ratio, dual_thermal_final, dual_saltiness_final, tentative_flow_speed))
    return (dual_thermal_initial, dual_saltiness_initial, dual_flow_initial, dual_interface_ratio, dual_poisson_forcing)
```

```python
import math

import jax
import jax.numpy as jnp
import numpy as np
from jax import lax
from jax.experimental import pallas as pl
from jax.experimental.pallas import tpu as pltpu
from jax.sharding import Mesh, PartitionSpec as P

f32 = jnp.float32
bf16 = jnp.bfloat16
highest = lax.Precision.HIGHEST
LANES = 128
ROWS = 8
SPLIT = {128: (8, 2, 4, 2)}
ALONG = ("z", "yh", "x", "c")
GROUP = ("yh", "x", "c")
GROUP_ALL = ("yh", "x", "c", "gz")


def hartley_table(length):
    numbers = np.arange(length)
    angle = (numbers[:, None] * numbers[None, :] % length) * (2.0 * math.pi / length)
    return np.cos(angle) + np.sin(angle)


def halves(value):
    upper = value.astype(bf16)
    return upper, (value - upper.astype(f32)).astype(bf16)


def exact_dot(a, b):
    return jnp.dot(a, b, precision=highest, preferred_element_type=f32)


def split_dot(a, b):
    (a_hi, a_lo), (b_hi, b_lo) = a, b

    def dot(p, q):
        return jnp.dot(p, q, preferred_element_type=f32)

    return dot(a_hi, b_hi) + (dot(a_hi, b_lo) + dot(a_lo, b_hi))


def inverse(value):
    guess = pl.reciprocal(value, approx=True)
    return guess * (2.0 - value * guess)


def face_terms(edges, ratio):
    positive = ratio >= 0.0
    d1 = jnp.where(positive, edges[0], edges[4])
    d2 = jnp.where(positive, edges[1], edges[3])
    d3 = edges[2]
    d4 = jnp.where(positive, edges[3], edges[1])
    s1, s2, s3 = d2 - d1, d3 - d2, d4 - d3
    e0, e1, e2 = (d2 + d2) + s1, d2 + d3, (d3 + d3) - s3
    t0, t1, t2 = (13.0 / 3.0) * s1, (13.0 / 3.0) * s2, (13.0 / 3.0) * s3
    r0 = inverse(t0 * s1 + (e0 * e0 + 0.04))
    r1 = inverse(t1 * s2 + (e1 * e1 + 0.04))
    r2 = inverse(t2 * s3 + (e2 * e2 + 0.04))
    u0, u1, u2 = (1.0 / 6.0) * (r0 * r0), r1 * r1, 0.5 * (r2 * r2)
    norm = inverse(u0 + u1 + u2)
    w0, w1, w2 = u0 * norm, u1 * norm, u2 * norm
    bend = s1 - s2
    a2, cc = bend + bend, s2 - s3
    z = w0 * a2 + w2 * cc
    total = (e1 + d3) + z
    n0, n1, n2 = w0 * r0 * (z - a2), w1 * r1 * z, w2 * r2 * (z - cc)
    p0, q0 = n0 * t0, n0 * e0
    p1, q1 = n1 * t1, n1 * e1
    p2, q2 = n2 * t2, n2 * e2
    left, right = p0 + q0, q2 - p2
    g1 = -(0.5 * w0 + left)
    g2 = (1.25 * w0 + 0.25 * w1) + (left + (q0 + q0)) + (q1 - p1)
    g3 = (0.5 * w1 + w2) + (right + (q2 + q2)) + (p1 + q1)
    g4 = -(0.25 * w2 + right)
    return positive, total, (g1, g2, g3, g4)


def weno_tile(field, ratio, cotangent, faces, cells, owned):
    edge_of, edge_bar, cell_bar, ratio_bar = {}, {}, {}, {}

    def edge(x):
        if x not in edge_of:
            edge_of[x] = field(x + 1) - field(x)
        return edge_of[x]

    def add(store, key, value):
        store[key] = store[key] + value if key in store else value

    for f in faces:
        c, e = ratio(f), cotangent(f)
        positive, total, (g1, g2, g3, g4) = face_terms([edge(f - 3 + k) for k in range(5)], c)
        gain = (2.0 / 3.0) * (jnp.abs(c) * e)
        g1, g2, g3, g4 = gain * g1, gain * g2, gain * g3, gain * g4
        zero = jnp.zeros_like(g1)
        add(edge_bar, f - 3, jnp.where(positive, g1, zero))
        add(edge_bar, f - 2, jnp.where(positive, g2, g4))
        add(edge_bar, f - 1, g3)
        add(edge_bar, f, jnp.where(positive, g4, g2))
        add(edge_bar, f + 1, jnp.where(positive, zero, g1))
        add(cell_bar, f - 1, jnp.maximum(c, 0.0) * e)
        add(cell_bar, f, jnp.minimum(c, 0.0) * e)
        if f in owned:
            center = jnp.where(positive, field(f - 1), field(f))
            sixth = total * (1.0 / 6.0)
            ratio_bar[f] = e * (center + jnp.where(positive, sixth, -sixth))
    bars = {}
    for x in cells:
        parts = []
        if x - 1 in edge_bar:
            parts.append(edge_bar[x - 1])
        if x in edge_bar:
            parts.append(-edge_bar[x])
        if x in cell_bar:
            parts.append(cell_bar[x])
        bars[x] = sum(parts[1:], parts[0])
    return bars, ratio_bar


def planes(own, before, after, own_count, before_at, before_count, after_at, lanes):
    def read(x):
        if x < 0:
            return before[before_at + before_count + x, :, lanes]
        if x >= own_count:
            return after[after_at + x - own_count, :, lanes]
        return own[x, :, lanes]

    return read


def tracer_kernel(t, s, c, lt, ls, before, after, t_out, s_out, c_out, left_out, right_out):
    n, _, width = t.shape

    def tile(l, carry):
        lanes = pl.ds(pl.multiple_of(l * LANES, LANES), LANES)
        sums = {}
        for k, (own, dual, out) in enumerate(((t, lt, t_out), (s, ls, s_out))):
            field = planes(own, before, after, n, 3 * k, 3, 2 * k, lanes)
            lam = planes(dual, before, after, n, 6 + k, 1, 0, lanes)
            bars, ratio_bar = weno_tile(
                field,
                lambda f: c[f, :, lanes],
                lambda f: lam(f) - lam(f - 1),
                range(n),
                range(-3, n + 2),
                range(n),
            )
            for x in range(n):
                out[x, :, lanes] = dual[x, :, lanes] + bars[x]
                sums[x] = sums[x] + ratio_bar[x] if x in sums else ratio_bar[x]
            for x in range(3):
                left_out[3 * k + x, :, lanes] = bars[x - 3]
            for x in range(2):
                right_out[2 * k + x, :, lanes] = bars[n + x]
        for x in range(n):
            c_out[x, :, lanes] = sums[x]
        return carry

    lax.fori_loop(0, width // LANES, tile, 0)


def flow_kernel(
    u, c, df, before, after, phi, phi_edge, t_in, s_in, c_in, from_left, from_right,
    t_out, s_out, u_out, c_out,
):
    n, _, width = u.shape

    def tile(l, carry):
        lanes = pl.ds(pl.multiple_of(l * LANES, LANES), LANES)
        field = planes(u, before, after, n, 0, 5, 0, lanes)
        ratio = planes(c, before, after, n, 5, 2, 5, lanes)
        dual = planes(df, before, after, n, 7, 3, 8, lanes)
        head = planes(phi, phi_edge, phi_edge, n, 0, 3, 3, lanes)
        step = {x: head(x) - head(x - 1) for x in range(-2, n + 2)}

        def bend(x):
            if x == -3:
                return phi_edge[5, :, lanes]
            if x == n + 1:
                return phi_edge[6, :, lanes]
            return step[x] - step[x + 1]

        bars, ratio_bar = weno_tile(
            field,
            ratio,
            lambda f: (dual(f) - dual(f - 1)) + bend(f - 1),
            range(-2, n + 3),
            range(n),
            range(n),
        )
        for x in range(n):
            u_out[x, :, lanes] = (df[x, :, lanes] - step[x]) + bars[x]
            c_out[x, :, lanes] = c_in[x, :, lanes] + ratio_bar[x]
        for k, (base, out) in enumerate(((t_in, t_out), (s_in, s_out))):
            for x in range(n):
                value = base[x, :, lanes]
                if x < 2:
                    value = value + from_left[2 * k + x, :, lanes]
                if x >= n - 3:
                    value = value + from_right[3 * k + x - (n - 3), :, lanes]
                out[x, :, lanes] = value
        return carry

    lax.fori_loop(0, width // LANES, tile, 0)


def moments_kernel(rows, blocks, head, table, depth, rates, waves, spec, coeff, sums, a_acc, b_acc, power):
    j, last = pl.program_id(0), pl.num_programs(0) - 1
    half = depth.shape[1] // 2
    columns = table.shape[1]
    width = columns // blocks

    @pl.when(j == 0)
    def _():
        a = rates[...] + waves[...]
        root = jnp.sqrt(a * (1.0 + 0.25 * a))
        rho = 1.0 / ((1.0 + 0.5 * a) + root)
        coeff[0] = rho
        coeff[1] = 0.5 / root
        coeff[2] = a
        a_acc[...] = jnp.zeros_like(a_acc)
        b_acc[...] = jnp.zeros_like(b_acc)
        power[...] = jnp.ones_like(power)

    values = exact_dot(head[0], table[...])
    spec[0] = values
    first = lax.axis_index("gz") == 0
    share = jnp.where(first, depth[:, :half], depth[:, half:])
    part = exact_dot(share * (-1.0 / columns), values)
    rho = coeff[0]
    a_acc[...] = a_acc[...] * rho + part
    b_acc[...] = b_acc[...] + power[...] * part
    power[...] = power[...] * rho

    @pl.when(j == last)
    def _():
        for n in range(sums.shape[0]):
            m, r = n // blocks * rows, n % blocks * width
            sums[n, 0] = a_acc[m : m + rows, r : r + width]
            sums[n, 1] = b_acc[m : m + rows, r : r + width]


def halo_kernel(left, right, table, spec):
    value = jnp.concatenate([left[...], right[...]], axis=0)
    count, levels, columns = value.shape
    spec[...] = exact_dot(value.reshape(count * levels, columns), table[...]).reshape(value.shape)


def chunk_decay(rows, blocks, coeff, sheets):
    n = lax.axis_index("yh")
    for name in GROUP_ALL[1:]:
        n = n * lax.axis_size(name) + lax.axis_index(name)
    width = coeff.shape[2] // blocks
    m = pl.multiple_of(n // blocks * rows, rows)
    r = pl.multiple_of(n % blocks * width, width)
    rho = coeff[0, pl.ds(m, rows), pl.ds(r, width)]
    square = rho * rho
    result = jnp.ones_like(rho)
    for _ in range(sheets // 2):
        result = result * square
    return result * rho if sheets % 2 else result


def repeated(value, times):
    result, power = None, value
    while times:
        if times & 1:
            result = power if result is None else result * power
        power, times = power * power, times >> 1
    return result


def group_kernel(rows, blocks, sheets, got, coeff, out):
    decay = chunk_decay(rows, blocks, coeff, sheets)
    places, rings = got.shape[0], out.shape[0]
    forward, backward = None, None
    for p in range(places):
        a, b = got[p, 0, 0] + got[p, 1, 0], got[places - 1 - p, 0, 1] + got[places - 1 - p, 1, 1]
        forward = a if forward is None else forward * decay + a
        backward = b if backward is None else backward * decay + b
    mine = lax.axis_index("z")
    factor = repeated(decay, places)
    for k in range(rings):
        out[lax.rem(mine + 1 + k, rings), 0] = forward
        out[lax.rem(mine + 2 * rings - 1 - k, rings), 1] = backward
        forward, backward = forward * factor, backward * factor


def carry_kernel(rows, blocks, sheets, got, rings, coeff, out):
    decay = chunk_decay(rows, blocks, coeff, sheets)
    places, around = got.shape[0], rings.shape[0]
    closing = 1.0 / (1.0 - repeated(decay, places * around))
    left, right = rings[0, 0], rings[0, 1]
    for k in range(1, around):
        left, right = left + rings[k, 0], right + rings[k, 1]
    left, right = left * closing, right * closing
    for p in range(places):
        q = places - 1 - p
        for g in range(2):
            out[p, g, 0] = left
            out[q, g, 1] = right
        left = left * decay + (got[p, 0, 0] + got[p, 1, 0])
        right = right * decay + (got[q, 0, 1] + got[q, 1, 1])


def source_kernel(own, edge, own_other, edge_other, depth, out, full):
    half = own.shape[1]
    mine = lax.axis_index("gz")
    here = pl.ds(pl.multiple_of(mine * half, half), half)
    there = pl.ds(pl.multiple_of((1 - mine) * half, half), half)
    scale = -1.0 / own.shape[2]
    matrix = depth[...] * scale
    n = own.shape[0]

    def inner(j, carry):
        full[here, :] = own[j]
        full[there, :] = own_other[j]
        out[3 + j] = exact_dot(matrix, full[...])
        return carry

    def outer(j, carry):
        full[here, :] = edge[j]
        full[there, :] = edge_other[j]
        out[jnp.where(j < 3, j, j + n)] = exact_dot(matrix, full[...])
        return carry

    lax.fori_loop(0, n, inner, 0)
    lax.fori_loop(0, edge.shape[0], outer, 0)


def solve_kernel(rows, blocks, source, carries, coeff, basis, table_hi, table_lo, phi, phi_edge, solved, levels_hi, levels_lo):
    count = source.shape[0]
    n = count - 5
    columns = source.shape[2]
    width = columns // blocks
    half = basis.shape[0] // 2

    def chunk(i, carry):
        m = pl.ds(pl.multiple_of(i // blocks * rows, rows), rows)
        r = pl.ds(pl.multiple_of(i % blocks * width, width), width)
        rho, kappa, a = coeff[0, m, r], coeff[1, m, r], coeff[2, m, r]
        growth = (2.0 + a) - rho
        f = [source[j, m, r] for j in range(count)]
        c, b = [None] * count, [None] * count
        c[2] = carries[i, 0]
        c[1] = (c[2] - f[2]) * growth
        c[0] = (c[1] - f[1]) * growth
        for j in range(3, count):
            c[j] = f[j] + rho * c[j - 1]
        b[n + 3] = carries[i, 1]
        b[n + 4] = (b[n + 3] - f[n + 3]) * growth
        for j in range(n + 2, -1, -1):
            b[j] = f[j] + rho * b[j + 1]
        values = [kappa * ((c[j] - f[j]) + b[j]) for j in range(count)]
        values.append(f[0] - a * values[0])
        values.append(f[count - 1] - a * values[count - 1])
        for j, value in enumerate(values):
            solved[j, m, r] = value
        return carry

    lax.fori_loop(0, carries.shape[0], chunk, 0)
    first = lax.axis_index("gz") == 0
    share = halves(jnp.where(first, basis[:half, :], basis[half:, :]))

    def plane(j, carry):
        value = split_dot(share, halves(solved[j]))
        here = pl.ds(pl.multiple_of(j * half, half), half)
        levels_hi[here, :], levels_lo[here, :] = halves(value)
        return carry

    lax.fori_loop(0, count + 2, plane, 0)
    result = split_dot((levels_hi[...], levels_lo[...]), (table_hi[...], table_lo[...]))
    result = result.reshape(count + 2, half, columns)
    phi[...] = result[3 : 3 + n]
    phi_edge[0:3] = result[0:3]
    phi_edge[3:7] = result[3 + n :]


WHOLE = pl.BlockSpec(memory_space=pltpu.VMEM)


def params():
    return pltpu.CompilerParams(vmem_limit_bytes=48 * 1024 * 1024)


def cost(us):
    return pl.CostEstimate(flops=int(us * 1e6), bytes_accessed=int(us * 3e6), transcendentals=0)


def call(kernel, outs, *args, scratch=(), us=2.0, name):
    many = isinstance(outs, (list, tuple))
    return pl.pallas_call(
        kernel,
        out_shape=outs,
        in_specs=[WHOLE] * len(args),
        out_specs=[WHOLE] * len(outs) if many else WHOLE,
        scratch_shapes=list(scratch),
        compiler_params=params(),
        cost_estimate=cost(us),
        name=name,
    )(*args)


def by_rows(kernel, outs, *args, us, name):
    levels, columns = args[0].shape[1:]

    def spec(a):
        return pl.BlockSpec((a.shape[0], ROWS, columns), lambda i: (0, i, 0))

    return pl.pallas_call(
        kernel,
        grid=(levels // ROWS,),
        out_shape=outs,
        in_specs=[spec(a) for a in args],
        out_specs=[spec(o) for o in outs],
        compiler_params=params(),
        cost_estimate=cost(us),
        name=name,
    )(*args)


def shards(
    thermal_anomaly,
    saltiness_anomaly,
    eastward_flow,
    advective_ratio,
    dual_thermal_final,
    dual_saltiness_final,
    dual_flow_final,
    dual_kinematic_head,
    depth_into_eigenbasis,
    eigenbasis_into_depth,
    spectral_magnitudes,
):
    t, s, u, c, lt, ls, df, head = (
        jnp.transpose(a, (1, 0, 2))
        for a in (
            thermal_anomaly,
            saltiness_anomaly,
            eastward_flow,
            advective_ratio,
            dual_thermal_final,
            dual_saltiness_final,
            dual_flow_final,
            dual_kinematic_head,
        )
    )
    n, levels, columns = t.shape
    modes = depth_into_eigenbasis.shape[0]
    across = lax.axis_size(ALONG)
    places = lax.axis_size(GROUP)
    rings = lax.axis_size("z")
    chunks = places * lax.axis_size("gz")
    rows = max(ROWS, modes // chunks)
    blocks = chunks * rows // modes
    width = columns // blocks

    def to_right(block):
        return lax.ppermute(block, ALONG, [(i, (i + 1) % across) for i in range(across)])

    def to_left(block):
        return lax.ppermute(block, ALONG, [((i + 1) % across, i) for i in range(across)])

    def other_half(block):
        return lax.ppermute(block, "gz", [(0, 1), (1, 0)])

    def like(*shape):
        return jax.ShapeDtypeStruct(shape, f32)

    exact = hartley_table(columns)
    table = jnp.asarray(exact.astype(np.float32))
    upper = exact.astype(np.float32).astype(jnp.bfloat16)
    table_hi = jnp.asarray(upper)
    table_lo = jnp.asarray((exact - upper.astype(np.float64)).astype(jnp.bfloat16))
    waves = jnp.asarray(
        (2.0 - 2.0 * np.cos(np.arange(columns) * (2.0 * math.pi / columns))).astype(np.float32)
    ).reshape(1, columns)

    head_left = to_right(head[n - 3 :])
    head_right = to_left(head[:2])
    tracer_before = to_right(jnp.concatenate([t[n - 3 :], s[n - 3 :], lt[n - 1 :], ls[n - 1 :]]))
    tracer_after = to_left(jnp.concatenate([t[:2], s[:2]]))
    flow_before = to_right(jnp.concatenate([u[n - 5 :], c[n - 2 :], df[n - 3 :]]))
    flow_after = to_left(jnp.concatenate([u[:5], c[:3], df[:3]]))

    whole = lambda *shape: pl.BlockSpec(shape, lambda j: (0,) * len(shape))
    spec, coeff, sums = pl.pallas_call(
        lambda *refs: moments_kernel(rows, blocks, *refs),
        grid=(n,),
        out_shape=[
            like(n, levels, columns),
            like(3, modes, columns),
            like(chunks, 2, rows, width),
        ],
        in_specs=[
            pl.BlockSpec((1, levels, columns), lambda j: (j, 0, 0)),
            whole(columns, columns),
            whole(modes, modes),
            whole(modes, 1),
            whole(1, columns),
        ],
        out_specs=[
            pl.BlockSpec((1, levels, columns), lambda j: (j, 0, 0)),
            whole(3, modes, columns),
            whole(chunks, 2, rows, width),
        ],
        scratch_shapes=[pltpu.VMEM((modes, columns), f32)] * 3,
        compiler_params=params(),
        cost_estimate=cost(4.0),
        name="block_moments",
    )(head, table, depth_into_eigenbasis, spectral_magnitudes.reshape(modes, 1), waves)
    gathered = lax.all_to_all(sums, GROUP_ALL, 0, 0, tiled=True)
    gathered = gathered.reshape(places, chunks // places, 2, rows, width)
    spec_other = other_half(spec)
    edge = call(halo_kernel, like(5, levels, columns), head_left, head_right, table, us=3.0, name="edge_spectrum")
    edge_other = other_half(edge)

    t_base, s_base, c_base, to_left_part, to_right_part = by_rows(
        tracer_kernel,
        [like(n, levels, columns)] * 3 + [like(6, levels, columns), like(4, levels, columns)],
        t, s, c, lt, ls, tracer_before, tracer_after,
        us=10.0,
        name="tracers",
    )
    from_right = to_left(to_left_part)
    from_left = to_right(to_right_part)

    ring = call(
        lambda *refs: group_kernel(rows, blocks, n, *refs),
        like(rings, 2, rows, width),
        gathered, coeff,
        us=1.0,
        name="group_moments",
    )
    ring = lax.all_to_all(ring, "z", 0, 0, tiled=True)
    carries = call(
        lambda *refs: carry_kernel(rows, blocks, n, *refs),
        like(places, chunks // places, 2, rows, width),
        gathered, ring, coeff,
        us=1.0,
        name="group_carries",
    )
    carries = lax.all_to_all(carries.reshape(chunks, 2, rows, width), GROUP_ALL, 0, 0, tiled=True)

    source = call(
        source_kernel,
        like(n + 5, modes, columns),
        spec, edge, spec_other, edge_other, depth_into_eigenbasis,
        scratch=[pltpu.VMEM((modes, columns), f32)],
        us=4.0,
        name="mode_source",
    )
    phi, phi_edge = call(
        lambda *refs: solve_kernel(rows, blocks, *refs),
        [like(n, levels, columns), like(7, levels, columns)],
        source, carries, coeff, eigenbasis_into_depth, table_hi, table_lo,
        scratch=[pltpu.VMEM((n + 7, modes, columns), f32)]
        + [pltpu.VMEM(((n + 7) * levels, columns), bf16)] * 2,
        us=7.0,
        name="pressure",
    )
    t_bar, s_bar, u_bar, c_bar = by_rows(
        flow_kernel,
        [like(n, levels, columns)] * 4,
        u, c, df, flow_before, flow_after, phi, phi_edge,
        t_base, s_base, c_base, from_left, from_right,
        us=7.0,
        name="flow",
    )
    return tuple(jnp.transpose(a, (1, 0, 2)) for a in (t_bar, s_bar, u_bar, c_bar, phi))


def solution(mesh):
    gx, gz = mesh.shape["gx"], mesh.shape["gz"]
    inner = Mesh(mesh.devices.reshape(SPLIT[gx] + (gz,)), ALONG + ("gz",))
    field = P("gz", ALONG, None)
    return jax.shard_map(
        shards,
        mesh=inner,
        in_specs=(field,) * 8 + (P(),) * 3,
        out_specs=(field,) * 5,
        check_vma=False,
    )
```

```python
import math

import jax
import jax.numpy as jnp
import numpy as np
from jax import lax
from jax.experimental import pallas as pl
from jax.experimental.pallas import tpu as pltpu
from jax.sharding import Mesh, PartitionSpec as P

f32 = jnp.float32
bf16 = jnp.bfloat16
LANES = 128
ROWS = 8
SPLIT = {128: (8, 2, 4, 2)}
ALONG = ("z", "yh", "x", "c")
GROUP = ("yh", "x", "c")
GROUP_ALL = ("yh", "x", "c", "gz")


def hartley_table(length):
    numbers = np.arange(length)
    angle = (numbers[:, None] * numbers[None, :] % length) * (2.0 * math.pi / length)
    return np.cos(angle) + np.sin(angle)


def halves(value):
    upper = value.astype(bf16)
    return upper, (value - upper.astype(f32)).astype(bf16)


def thrice_left(pair):
    return jnp.concatenate([pair[0], pair[0], pair[1]], axis=1)


def thrice_right(pair):
    return jnp.concatenate([pair[0], pair[1], pair[0]], axis=0)


def split_dot(a, b):
    (a_hi, a_lo), (b_hi, b_lo) = a, b

    def dot(p, q):
        return jnp.dot(p, q, preferred_element_type=f32)

    return dot(a_hi, b_hi) + (dot(a_hi, b_lo) + dot(a_lo, b_hi))


def face_terms(edges, ratio):
    positive = ratio >= 0.0
    d1 = jnp.where(positive, edges[0], edges[4])
    d2 = jnp.where(positive, edges[1], edges[3])
    d3 = edges[2]
    d4 = jnp.where(positive, edges[3], edges[1])
    s1, s2, s3 = d2 - d1, d3 - d2, d4 - d3
    e0, e1, e2 = (d2 + d2) + s1, d2 + d3, (d3 + d3) - s3
    t0, t1, t2 = (13.0 / 3.0) * s1, (13.0 / 3.0) * s2, (13.0 / 3.0) * s3
    r0 = 1.0 / (t0 * s1 + (e0 * e0 + 0.04))
    r1 = 1.0 / (t1 * s2 + (e1 * e1 + 0.04))
    r2 = 1.0 / (t2 * s3 + (e2 * e2 + 0.04))
    u0, u1, u2 = (1.0 / 6.0) * (r0 * r0), r1 * r1, 0.5 * (r2 * r2)
    norm = 1.0 / (u0 + u1 + u2)
    w0, w1, w2 = u0 * norm, u1 * norm, u2 * norm
    bend = s1 - s2
    a2, cc = bend + bend, s2 - s3
    z = w0 * a2 + w2 * cc
    total = (e1 + d3) + z
    n0, n1, n2 = w0 * r0 * (z - a2), w1 * r1 * z, w2 * r2 * (z - cc)
    p0, q0 = n0 * t0, n0 * e0
    p1, q1 = n1 * t1, n1 * e1
    p2, q2 = n2 * t2, n2 * e2
    h0, h2 = 0.5 * w0, 0.25 * w2
    lean = h0 - h2
    m1, m4 = h0 + (p0 + q0), h2 + (q2 - p2)
    g2 = ((0.25 + lean) + m1) + ((q0 + q0) + (q1 - p1))
    g3 = ((0.5 - lean) + m4) + ((q2 + q2) + (p1 + q1))
    return positive, total, (m1, g2, g3, m4)


def weno_tile(field, ratio, cotangent, faces, cells, owned):
    edge_of, edge_bar, cell_bar, ratio_bar = {}, {}, {}, {}

    def edge(x):
        if x not in edge_of:
            edge_of[x] = field(x + 1) - field(x)
        return edge_of[x]

    def add(store, key, value, less=False):
        if key in store:
            store[key] = store[key] - value if less else store[key] + value
        else:
            store[key] = -value if less else value

    for f in faces:
        c, e = ratio(f), cotangent(f)
        positive, total, (m1, g2, g3, m4) = face_terms([edge(f - 3 + k) for k in range(5)], c)
        gain = (2.0 / 3.0) * (jnp.abs(c) * e)
        m1, g2, g3, m4 = gain * m1, gain * g2, gain * g3, gain * m4
        zero = jnp.zeros_like(m1)
        add(edge_bar, f - 3, jnp.where(positive, m1, zero), True)
        add(edge_bar, f - 2, jnp.where(positive, g2, -m4))
        add(edge_bar, f - 1, g3)
        add(edge_bar, f, jnp.where(positive, -m4, g2))
        add(edge_bar, f + 1, jnp.where(positive, zero, m1), True)
        add(cell_bar, f - 1, jnp.maximum(c, 0.0) * e)
        add(cell_bar, f, jnp.minimum(c, 0.0) * e)
        if f in owned:
            center = jnp.where(positive, field(f - 1), field(f))
            sixth = total * (1.0 / 6.0)
            ratio_bar[f] = e * (center + jnp.where(positive, sixth, -sixth))
    bars = {}
    for x in cells:
        parts = []
        if x - 1 in edge_bar:
            parts.append(edge_bar[x - 1])
        if x in edge_bar:
            parts.append(-edge_bar[x])
        if x in cell_bar:
            parts.append(cell_bar[x])
        bars[x] = sum(parts[1:], parts[0])
    return bars, ratio_bar


def planes(own, before, after, own_count, before_at, before_count, after_at, lanes):
    def read(x):
        if x < 0:
            return before[before_at + before_count + x, :, lanes]
        if x >= own_count:
            return after[after_at + x - own_count, :, lanes]
        return own[x, :, lanes]

    return read


def tracer_kernel(t, s, c, lt, ls, before, after, t_out, s_out, c_out, left_out, right_out):
    n, _, width = t.shape

    def tile(l, carry):
        lanes = pl.ds(pl.multiple_of(l * LANES, LANES), LANES)
        sums = {}
        for k, (own, dual, out) in enumerate(((t, lt, t_out), (s, ls, s_out))):
            field = planes(own, before, after, n, 3 * k, 3, 2 * k, lanes)
            lam = planes(dual, before, after, n, 6 + k, 1, 0, lanes)
            bars, ratio_bar = weno_tile(
                field,
                lambda f: c[f, :, lanes],
                lambda f: lam(f) - lam(f - 1),
                range(n),
                range(-3, n + 2),
                range(n),
            )
            for x in range(n):
                out[x, :, lanes] = dual[x, :, lanes] + bars[x]
                sums[x] = sums[x] + ratio_bar[x] if x in sums else ratio_bar[x]
            for x in range(3):
                left_out[3 * k + x, :, lanes] = bars[x - 3]
            for x in range(2):
                right_out[2 * k + x, :, lanes] = bars[n + x]
        for x in range(n):
            c_out[x, :, lanes] = sums[x]
        return carry

    lax.fori_loop(0, width // LANES, tile, 0)


def flow_kernel(
    u, c, df, before, after, phi, phi_edge, t_in, s_in, c_in, from_left, from_right,
    t_out, s_out, u_out, c_out,
):
    n, _, width = u.shape

    def tile(l, carry):
        lanes = pl.ds(pl.multiple_of(l * LANES, LANES), LANES)
        field = planes(u, before, after, n, 0, 5, 0, lanes)
        ratio = planes(c, before, after, n, 5, 2, 5, lanes)
        dual = planes(df, before, after, n, 7, 3, 8, lanes)
        head = planes(phi, phi_edge, phi_edge, n, 0, 3, 3, lanes)
        step = {x: head(x) - head(x - 1) for x in range(-2, n + 2)}

        def bend(x):
            if x == -3:
                return phi_edge[5, :, lanes]
            if x == n + 1:
                return phi_edge[6, :, lanes]
            return step[x] - step[x + 1]

        bars, ratio_bar = weno_tile(
            field,
            ratio,
            lambda f: (dual(f) - dual(f - 1)) + bend(f - 1),
            range(-2, n + 3),
            range(n),
            range(n),
        )
        for x in range(n):
            u_out[x, :, lanes] = (df[x, :, lanes] - step[x]) + bars[x]
            c_out[x, :, lanes] = c_in[x, :, lanes] + ratio_bar[x]
        for k, (base, out) in enumerate(((t_in, t_out), (s_in, s_out))):
            for x in range(n):
                value = base[x, :, lanes]
                if x < 2:
                    value = value + from_left[2 * k + x, :, lanes]
                if x >= n - 3:
                    value = value + from_right[3 * k + x - (n - 3), :, lanes]
                out[x, :, lanes] = value
        return carry

    lax.fori_loop(0, width // LANES, tile, 0)


def moments_kernel(rows, blocks, head, table_hi, table_lo, depth, rates, waves, u, c, df, spec, coeff, sums, flow_right, flow_left, sems):
    n, levels, columns = head.shape
    width = columns // blocks
    copies = [
        pltpu.make_async_copy(source, target, sems.at[k])
        for k, (source, target) in enumerate(
            (
                (u.at[n - 5 : n], flow_right.at[0:5]),
                (c.at[n - 2 : n], flow_right.at[5:7]),
                (df.at[n - 3 : n], flow_right.at[7:10]),
                (u.at[0:5], flow_left.at[0:5]),
                (c.at[0:3], flow_left.at[5:8]),
                (df.at[0:3], flow_left.at[8:11]),
            )
        )
    ]
    for copy in copies:
        copy.start()
    a = jnp.transpose(jnp.broadcast_to(rates[...], (columns, rates.shape[1]))) + waves[...]
    root = jnp.sqrt(a * (1.0 + 0.25 * a))
    rho = 1.0 / ((1.0 + 0.5 * a) + root)
    coeff[0] = rho
    coeff[1] = 0.5 / root
    coeff[2] = a
    values = head[...].reshape(n * levels, columns)
    values = split_dot(halves(values), (table_hi[...], table_lo[...]))
    spec[...] = values.reshape(n, levels, columns)
    first = lax.axis_index("gz") == 0
    share = jnp.where(first, depth[:, :levels], depth[:, levels:])
    share = thrice_left(halves(share * (-1.0 / columns)))
    for j in range(n):
        part = jnp.dot(share, thrice_right(halves(spec[j])), preferred_element_type=f32)
        if j == 0:
            forward, backward, power = part, part, coeff[0]
        else:
            forward = forward * coeff[0] + part
            backward = backward + power * part
            power = power * coeff[0]
    for i in range(sums.shape[0]):
        m, r = i // blocks * rows, i % blocks * width
        sums[i, 0] = forward[m : m + rows, r : r + width]
        sums[i, 1] = backward[m : m + rows, r : r + width]
    for copy in copies:
        copy.wait()


def pack_kernel(head, t, s, lt, ls, right, left, sems):
    n = head.shape[0]
    copies = [
        pltpu.make_async_copy(source, target, sems.at[k])
        for k, (source, target) in enumerate(
            (
                (t.at[n - 3 : n], right.at[0:3]),
                (s.at[n - 3 : n], right.at[3:6]),
                (lt.at[n - 1 : n], right.at[6:7]),
                (ls.at[n - 1 : n], right.at[7:8]),
                (head.at[n - 3 : n], right.at[8:11]),
                (t.at[0:2], left.at[0:2]),
                (s.at[0:2], left.at[2:4]),
                (head.at[0:2], left.at[4:6]),
            )
        )
    ]
    for copy in copies:
        copy.start()
    for copy in copies:
        copy.wait()


def halo_kernel(before, after, table_hi, table_lo, spec, planes, sems):
    copies = [
        pltpu.make_async_copy(before.at[8:11], planes.at[0:3], sems.at[0]),
        pltpu.make_async_copy(after.at[4:6], planes.at[3:5], sems.at[1]),
    ]
    for copy in copies:
        copy.start()
    for copy in copies:
        copy.wait()
    count, levels, columns = planes.shape
    value = planes[...].reshape(count * levels, columns)
    spec[...] = split_dot(halves(value), (table_hi[...], table_lo[...])).reshape(planes.shape)


def chunk_decay(rows, blocks, coeff, sheets):
    n = lax.axis_index("yh")
    for name in GROUP_ALL[1:]:
        n = n * lax.axis_size(name) + lax.axis_index(name)
    width = coeff.shape[2] // blocks
    m = pl.multiple_of(n // blocks * rows, rows)
    r = pl.multiple_of(n % blocks * width, width)
    rho = coeff[0, pl.ds(m, rows), pl.ds(r, width)]
    square = rho * rho
    result = jnp.ones_like(rho)
    for _ in range(sheets // 2):
        result = result * square
    return result * rho if sheets % 2 else result


def repeated(value, times):
    result, power = None, value
    while times:
        if times & 1:
            result = power if result is None else result * power
        power, times = power * power, times >> 1
    return result


def group_kernel(rows, blocks, sheets, got, coeff, out):
    decay = chunk_decay(rows, blocks, coeff, sheets)
    places, rings = got.shape[0], out.shape[0]
    forward, backward = None, None
    for p in range(places):
        a, b = got[p, 0, 0] + got[p, 1, 0], got[places - 1 - p, 0, 1] + got[places - 1 - p, 1, 1]
        forward = a if forward is None else forward * decay + a
        backward = b if backward is None else backward * decay + b
    mine = lax.axis_index("z")
    factor = repeated(decay, places)
    for k in range(rings):
        out[lax.rem(mine + 1 + k, rings), 0] = forward
        out[lax.rem(mine + 2 * rings - 1 - k, rings), 1] = backward
        forward, backward = forward * factor, backward * factor


def carry_kernel(rows, blocks, sheets, got, rings, coeff, out):
    decay = chunk_decay(rows, blocks, coeff, sheets)
    places, around = got.shape[0], rings.shape[0]
    closing = 1.0 / (1.0 - repeated(decay, places * around))
    left, right = rings[0, 0], rings[0, 1]
    for k in range(1, around):
        left, right = left + rings[k, 0], right + rings[k, 1]
    left, right = left * closing, right * closing
    for p in range(places):
        q = places - 1 - p
        for g in range(2):
            out[p, g, 0] = left
            out[q, g, 1] = right
        left = left * decay + (got[p, 0, 0] + got[p, 1, 0])
        right = right * decay + (got[q, 0, 1] + got[q, 1, 1])


def source_kernel(own, edge, own_other, edge_other, depth, out):
    half = own.shape[1]
    n = own.shape[0]
    first = lax.axis_index("gz") == 0
    matrix = depth[...] * (-1.0 / own.shape[2])
    here = jnp.where(first, matrix[:, :half], matrix[:, half:])
    there = jnp.where(first, matrix[:, half:], matrix[:, :half])
    matrix = thrice_left(halves(jnp.concatenate([here, there], axis=1)))

    def product(mine, other):
        full = halves(jnp.concatenate([mine, other], axis=0))
        return jnp.dot(matrix, thrice_right(full), preferred_element_type=f32)

    for j in range(n):
        out[3 + j] = product(own[j], own_other[j])
    for j in range(5):
        out[j if j < 3 else j + n] = product(edge[j], edge_other[j])


def solve_kernel(rows, blocks, source, carries, coeff, basis, table_hi, table_lo, phi, phi_edge, solved, levels_hi, levels_lo):
    count = source.shape[0]
    n = count - 5
    columns = source.shape[2]
    width = columns // blocks
    half = basis.shape[0] // 2

    def chunk(i, carry):
        m = pl.ds(pl.multiple_of(i // blocks * rows, rows), rows)
        r = pl.ds(pl.multiple_of(i % blocks * width, width), width)
        rho, kappa, a = coeff[0, m, r], coeff[1, m, r], coeff[2, m, r]
        growth = (2.0 + a) - rho
        f = [source[j, m, r] for j in range(count)]
        c, b = [None] * count, [None] * count
        c[2] = carries[i, 0]
        c[1] = (c[2] - f[2]) * growth
        c[0] = (c[1] - f[1]) * growth
        for j in range(3, count):
            c[j] = f[j] + rho * c[j - 1]
        b[n + 3] = carries[i, 1]
        b[n + 4] = (b[n + 3] - f[n + 3]) * growth
        for j in range(n + 2, -1, -1):
            b[j] = f[j] + rho * b[j + 1]
        values = [kappa * ((c[j] - f[j]) + b[j]) for j in range(count)]
        values.append(f[0] - a * values[0])
        values.append(f[count - 1] - a * values[count - 1])
        for j, value in enumerate(values):
            solved[j, m, r] = value
        return carry

    lax.fori_loop(0, carries.shape[0], chunk, 0)
    first = lax.axis_index("gz") == 0
    share = thrice_left(halves(jnp.where(first, basis[:half, :], basis[half:, :])))

    def plane(j, carry):
        value = jnp.dot(share, thrice_right(halves(solved[j])), preferred_element_type=f32)
        here = pl.ds(pl.multiple_of(j * half, half), half)
        levels_hi[here, :], levels_lo[here, :] = halves(value)
        return carry

    lax.fori_loop(0, count + 2, plane, 0)
    result = split_dot((levels_hi[...], levels_lo[...]), (table_hi[...], table_lo[...]))
    result = result.reshape(count + 2, half, columns)
    phi[...] = result[3 : 3 + n]
    phi_edge[0:3] = result[0:3]
    phi_edge[3:7] = result[3 + n :]


AWAY = pl.BlockSpec(memory_space=pl.ANY)


def params():
    return pltpu.CompilerParams(vmem_limit_bytes=63 * 1024 * 1024)


def cost(us):
    return pl.CostEstimate(flops=int(us * 1e6), bytes_accessed=int(us * 3e6), transcendentals=0)


def call(kernel, outs, *args, scratch=(), us=2.0, name, away=(), out_away=()):
    many = isinstance(outs, (list, tuple))

    def whole(a):
        return pl.BlockSpec(a.shape, lambda i: (0,) * len(a.shape), pipeline_mode=pl.Buffered(1))

    return pl.pallas_call(
        kernel,
        grid=(1,),
        out_shape=outs,
        in_specs=[AWAY if k in away else whole(a) for k, a in enumerate(args)],
        out_specs=[AWAY if k in out_away else whole(a) for k, a in enumerate(outs)]
        if many
        else whole(outs),
        scratch_shapes=list(scratch),
        compiler_params=params(),
        cost_estimate=cost(us),
        name=name,
    )(*args)


def by_rows(kernel, outs, *args, us, name, counts={}):
    levels, columns = args[0].shape[1:]

    def spec(a, count=None):
        return pl.BlockSpec((count or a.shape[0], ROWS, columns), lambda i: (0, i, 0))

    return pl.pallas_call(
        kernel,
        grid=(levels // ROWS,),
        out_shape=outs,
        in_specs=[spec(a, counts.get(k)) for k, a in enumerate(args)],
        out_specs=[spec(o) for o in outs],
        compiler_params=params(),
        cost_estimate=cost(us),
        name=name,
    )(*args)


def shards(
    thermal_anomaly,
    saltiness_anomaly,
    eastward_flow,
    advective_ratio,
    dual_thermal_final,
    dual_saltiness_final,
    dual_flow_final,
    dual_kinematic_head,
    depth_into_eigenbasis,
    eigenbasis_into_depth,
    spectral_magnitudes,
):
    t, s, u, c, lt, ls, df, head = (
        jnp.transpose(a, (1, 0, 2))
        for a in (
            thermal_anomaly,
            saltiness_anomaly,
            eastward_flow,
            advective_ratio,
            dual_thermal_final,
            dual_saltiness_final,
            dual_flow_final,
            dual_kinematic_head,
        )
    )
    n, levels, columns = t.shape
    modes = depth_into_eigenbasis.shape[0]
    across = lax.axis_size(ALONG)
    places = lax.axis_size(GROUP)
    rings = lax.axis_size("z")
    chunks = places * lax.axis_size("gz")
    rows = max(ROWS, modes // chunks)
    blocks = chunks * rows // modes
    width = columns // blocks

    def to_right(block):
        return lax.ppermute(block, ALONG, [(i, (i + 1) % across) for i in range(across)])

    def to_left(block):
        return lax.ppermute(block, ALONG, [((i + 1) % across, i) for i in range(across)])

    def other_half(block):
        return lax.ppermute(block, "gz", [(0, 1), (1, 0)])

    def like(*shape):
        return jax.ShapeDtypeStruct(shape, f32)

    exact = hartley_table(columns)
    upper = exact.astype(np.float32).astype(jnp.bfloat16)
    table_hi = jnp.asarray(upper)
    table_lo = jnp.asarray((exact - upper.astype(np.float64)).astype(jnp.bfloat16))
    waves = jnp.asarray(
        (2.0 - 2.0 * np.cos(np.arange(columns) * (2.0 * math.pi / columns))).astype(np.float32)
    ).reshape(1, columns)

    right, left = call(
        pack_kernel,
        [like(11, levels, columns), like(6, levels, columns)],
        head, t, s, lt, ls,
        scratch=[pltpu.SemaphoreType.DMA((8,))],
        away=range(5),
        out_away=range(2),
        us=2.0,
        name="pack",
    )
    before, after = to_right(right), to_left(left)

    spec, coeff, sums, flow_right, flow_left = call(
        lambda *refs: moments_kernel(rows, blocks, *refs),
        [
            like(n, levels, columns),
            like(3, modes, columns),
            like(chunks, 2, rows, width),
            like(10, levels, columns),
            like(11, levels, columns),
        ],
        head, table_hi, table_lo, depth_into_eigenbasis,
        spectral_magnitudes.reshape(1, modes), waves, u, c, df,
        scratch=[pltpu.SemaphoreType.DMA((6,))],
        away=(6, 7, 8),
        out_away=(3, 4),
        us=5.0,
        name="block_moments",
    )
    gathered = lax.all_to_all(sums, GROUP_ALL, 0, 0, tiled=True)
    gathered, late, flow_right, flow_left = lax.optimization_barrier(
        (gathered, spec, flow_right, flow_left)
    )
    gathered = gathered.reshape(places, chunks // places, 2, rows, width)
    edge = call(
        halo_kernel,
        like(5, levels, columns),
        before, after, table_hi, table_lo,
        scratch=[pltpu.VMEM((5, levels, columns), f32), pltpu.SemaphoreType.DMA((2,))],
        away=(0, 1),
        us=2.0,
        name="edge_spectrum",
    )
    spec_other = other_half(late)
    edge_other = other_half(edge)
    flow_before, flow_after = to_right(flow_right), to_left(flow_left)

    t_base, s_base, c_base, to_left_part, to_right_part = by_rows(
        tracer_kernel,
        [like(n, levels, columns)] * 3 + [like(6, levels, columns), like(4, levels, columns)],
        t, s, c, lt, ls, before, after,
        us=9.0,
        name="tracers",
        counts={5: 8, 6: 4},
    )
    from_right = to_left(to_left_part)
    from_left = to_right(to_right_part)

    ring = call(
        lambda *refs: group_kernel(rows, blocks, n, *refs),
        like(rings, 2, rows, width),
        gathered, coeff,
        us=1.0,
        name="group_moments",
    )
    ring = lax.all_to_all(ring, "z", 0, 0, tiled=True)
    carries = call(
        lambda *refs: carry_kernel(rows, blocks, n, *refs),
        like(places, chunks // places, 2, rows, width),
        gathered, ring, coeff,
        us=1.0,
        name="group_carries",
    )
    carries = lax.all_to_all(carries.reshape(chunks, 2, rows, width), GROUP_ALL, 0, 0, tiled=True)

    source = call(
        source_kernel,
        like(n + 5, modes, columns),
        spec, edge, spec_other, edge_other, depth_into_eigenbasis,
        us=4.0,
        name="mode_source",
    )
    phi, phi_edge = call(
        lambda *refs: solve_kernel(rows, blocks, *refs),
        [like(n, levels, columns), like(7, levels, columns)],
        source, carries, coeff, eigenbasis_into_depth, table_hi, table_lo,
        scratch=[pltpu.VMEM((n + 7, modes, columns), f32)]
        + [pltpu.VMEM(((n + 7) * levels, columns), bf16)] * 2,
        us=7.0,
        name="pressure",
    )
    t_bar, s_bar, u_bar, c_bar = by_rows(
        flow_kernel,
        [like(n, levels, columns)] * 4,
        u, c, df, flow_before, flow_after, phi, phi_edge,
        t_base, s_base, c_base, from_left, from_right,
        us=7.0,
        name="flow",
    )
    return tuple(jnp.transpose(a, (1, 0, 2)) for a in (t_bar, s_bar, u_bar, c_bar, phi))


def solution(mesh):
    gx, gz = mesh.shape["gx"], mesh.shape["gz"]
    inner = Mesh(mesh.devices.reshape(SPLIT[gx] + (gz,)), ALONG + ("gz",))
    field = P("gz", ALONG, None)
    return jax.shard_map(
        shards,
        mesh=inner,
        in_specs=(field,) * 8 + (P(),) * 3,
        out_specs=(field,) * 5,
        check_vma=False,
    )
```

```python
import math

import jax
import jax.numpy as jnp
import numpy as np
from jax import lax
from jax.experimental import pallas as pl
from jax.experimental.pallas import tpu as pltpu
from jax.sharding import Mesh, PartitionSpec as P

f32 = jnp.float32
bf16 = jnp.bfloat16
LANES = 128
ROWS = 8
SPLIT = {128: (8, 2, 4, 2)}
ALONG = ("z", "yh", "x", "c")
GROUP = ("yh", "x", "c")
GROUP_ALL = ("yh", "x", "c", "gz")


def hartley_table(length):
    numbers = np.arange(length)
    angle = (numbers[:, None] * numbers[None, :] % length) * (2.0 * math.pi / length)
    return np.cos(angle) + np.sin(angle)


def halves(value):
    upper = value.astype(bf16)
    return upper, (value - upper.astype(f32)).astype(bf16)


def thrice_left(pair):
    return jnp.concatenate([pair[0], pair[0], pair[1]], axis=1)


def thrice_right(pair):
    return jnp.concatenate([pair[0], pair[1], pair[0]], axis=0)


def split_dot(a, b):
    (a_hi, a_lo), (b_hi, b_lo) = a, b

    def dot(p, q):
        return jnp.dot(p, q, preferred_element_type=f32)

    return dot(a_hi, b_hi) + (dot(a_hi, b_lo) + dot(a_lo, b_hi))


def face_terms(edges, ratio):
    positive = ratio >= 0.0
    d1 = jnp.where(positive, edges[0], edges[4])
    d2 = jnp.where(positive, edges[1], edges[3])
    d3 = edges[2]
    d4 = jnp.where(positive, edges[3], edges[1])
    s1, s2, s3 = d2 - d1, d3 - d2, d4 - d3
    e0, e1, e2 = (d2 + d2) + s1, d2 + d3, (d3 + d3) - s3
    t0, t1, t2 = (13.0 / 3.0) * s1, (13.0 / 3.0) * s2, (13.0 / 3.0) * s3
    r0 = 1.0 / (t0 * s1 + (e0 * e0 + 0.04))
    r1 = 1.0 / (t1 * s2 + (e1 * e1 + 0.04))
    r2 = 1.0 / (t2 * s3 + (e2 * e2 + 0.04))
    u0, u1, u2 = (1.0 / 6.0) * (r0 * r0), r1 * r1, 0.5 * (r2 * r2)
    norm = 1.0 / (u0 + u1 + u2)
    w0, w1, w2 = u0 * norm, u1 * norm, u2 * norm
    bend = s1 - s2
    a2, cc = bend + bend, s2 - s3
    z = w0 * a2 + w2 * cc
    total = (e1 + d3) + z
    n0, n1, n2 = w0 * r0 * (z - a2), w1 * r1 * z, w2 * r2 * (z - cc)
    p0, q0 = n0 * t0, n0 * e0
    p1, q1 = n1 * t1, n1 * e1
    p2, q2 = n2 * t2, n2 * e2
    h0, h2 = 0.5 * w0, 0.25 * w2
    lean = h0 - h2
    m1, m4 = h0 + (p0 + q0), h2 + (q2 - p2)
    g2 = ((0.25 + lean) + m1) + ((q0 + q0) + (q1 - p1))
    g3 = ((0.5 - lean) + m4) + ((q2 + q2) + (p1 + q1))
    return positive, total, (m1, g2, g3, m4)


def weno_tile(field, ratio, cotangent, faces, cells, owned):
    edge_of, edge_bar, cell_bar, ratio_bar = {}, {}, {}, {}

    def edge(x):
        if x not in edge_of:
            edge_of[x] = field(x + 1) - field(x)
        return edge_of[x]

    def add(store, key, value, less=False):
        if key in store:
            store[key] = store[key] - value if less else store[key] + value
        else:
            store[key] = -value if less else value

    for f in faces:
        c, e = ratio(f), cotangent(f)
        positive, total, (m1, g2, g3, m4) = face_terms([edge(f - 3 + k) for k in range(5)], c)
        gain = (2.0 / 3.0) * (jnp.abs(c) * e)
        m1, g2, g3, m4 = gain * m1, gain * g2, gain * g3, gain * m4
        zero = jnp.zeros_like(m1)
        add(edge_bar, f - 3, jnp.where(positive, m1, zero), True)
        add(edge_bar, f - 2, jnp.where(positive, g2, -m4))
        add(edge_bar, f - 1, g3)
        add(edge_bar, f, jnp.where(positive, -m4, g2))
        add(edge_bar, f + 1, jnp.where(positive, zero, m1), True)
        add(cell_bar, f - 1, jnp.maximum(c, 0.0) * e)
        add(cell_bar, f, jnp.minimum(c, 0.0) * e)
        if f in owned:
            center = jnp.where(positive, field(f - 1), field(f))
            sixth = total * (1.0 / 6.0)
            ratio_bar[f] = e * (center + jnp.where(positive, sixth, -sixth))
    bars = {}
    for x in cells:
        parts = []
        if x - 1 in edge_bar:
            parts.append(edge_bar[x - 1])
        if x in edge_bar:
            parts.append(-edge_bar[x])
        if x in cell_bar:
            parts.append(cell_bar[x])
        bars[x] = sum(parts[1:], parts[0])
    return bars, ratio_bar


def planes(own, before, after, own_count, before_at, before_count, after_at, lanes):
    def read(x):
        if x < 0:
            return before[before_at + before_count + x, :, lanes]
        if x >= own_count:
            return after[after_at + x - own_count, :, lanes]
        return own[x, :, lanes]

    return read


def tracer_kernel(t, s, c, lt, ls, before, after, t_out, s_out, c_out, left_out, right_out):
    n, _, width = t.shape

    def tile(l, carry):
        lanes = pl.ds(pl.multiple_of(l * LANES, LANES), LANES)
        sums = {}
        for k, (own, dual, out) in enumerate(((t, lt, t_out), (s, ls, s_out))):
            field = planes(own, before, after, n, 3 * k, 3, 2 * k, lanes)
            lam = planes(dual, before, after, n, 6 + k, 1, 0, lanes)
            bars, ratio_bar = weno_tile(
                field,
                lambda f: c[f, :, lanes],
                lambda f: lam(f) - lam(f - 1),
                range(n),
                range(-3, n + 2),
                range(n),
            )
            for x in range(n):
                out[x, :, lanes] = dual[x, :, lanes] + bars[x]
                sums[x] = sums[x] + ratio_bar[x] if x in sums else ratio_bar[x]
            for x in range(3):
                left_out[3 * k + x, :, lanes] = bars[x - 3]
            for x in range(2):
                right_out[2 * k + x, :, lanes] = bars[n + x]
        for x in range(n):
            c_out[x, :, lanes] = sums[x]
        return carry

    lax.fori_loop(0, width // LANES, tile, 0)


def flow_kernel(
    u, c, df, before, after, phi, phi_edge, t_in, s_in, c_in, from_left, from_right,
    t_out, s_out, u_out, c_out,
):
    n, _, width = u.shape

    def tile(l, carry):
        lanes = pl.ds(pl.multiple_of(l * LANES, LANES), LANES)
        field = planes(u, before, after, n, 0, 5, 0, lanes)
        ratio = planes(c, before, after, n, 5, 2, 5, lanes)
        dual = planes(df, before, after, n, 7, 3, 8, lanes)
        head = planes(phi, phi_edge, phi_edge, n, 0, 3, 3, lanes)
        step = {x: head(x) - head(x - 1) for x in range(-2, n + 2)}

        def bend(x):
            if x == -3:
                return phi_edge[5, :, lanes]
            if x == n + 1:
                return phi_edge[6, :, lanes]
            return step[x] - step[x + 1]

        bars, ratio_bar = weno_tile(
            field,
            ratio,
            lambda f: (dual(f) - dual(f - 1)) + bend(f - 1),
            range(-2, n + 3),
            range(n),
            range(n),
        )
        for x in range(n):
            u_out[x, :, lanes] = (df[x, :, lanes] - step[x]) + bars[x]
            c_out[x, :, lanes] = c_in[x, :, lanes] + ratio_bar[x]
        for k, (base, out) in enumerate(((t_in, t_out), (s_in, s_out))):
            for x in range(n):
                value = base[x, :, lanes]
                if x < 2:
                    value = value + from_left[2 * k + x, :, lanes]
                if x >= n - 3:
                    value = value + from_right[3 * k + x - (n - 3), :, lanes]
                out[x, :, lanes] = value
        return carry

    lax.fori_loop(0, width // LANES, tile, 0)


def moments_kernel(rows, blocks, head, table_hi, table_lo, depth, rates, waves, u, c, df, spec, coeff, sums, flow_right, flow_left, sems):
    n, levels, columns = head.shape
    width = columns // blocks
    copies = [
        pltpu.make_async_copy(source, target, sems.at[k])
        for k, (source, target) in enumerate(
            (
                (u.at[n - 5 : n], flow_right.at[0:5]),
                (c.at[n - 2 : n], flow_right.at[5:7]),
                (df.at[n - 3 : n], flow_right.at[7:10]),
                (u.at[0:5], flow_left.at[0:5]),
                (c.at[0:3], flow_left.at[5:8]),
                (df.at[0:3], flow_left.at[8:11]),
            )
        )
    ]
    for copy in copies:
        copy.start()
    a = jnp.transpose(jnp.broadcast_to(rates[...], (columns, rates.shape[1]))) + waves[...]
    root = jnp.sqrt(a * (1.0 + 0.25 * a))
    rho = 1.0 / ((1.0 + 0.5 * a) + root)
    coeff[0] = rho
    coeff[1] = 0.5 / root
    coeff[2] = a
    values = head[...].reshape(n * levels, columns)
    values = split_dot(halves(values), (table_hi[...], table_lo[...]))
    spec[...] = values.reshape(n, levels, columns)
    first = lax.axis_index("gz") == 0
    share = jnp.where(first, depth[:, :levels], depth[:, levels:])
    share = thrice_left(halves(share * (-1.0 / columns)))
    for j in range(n):
        part = jnp.dot(share, thrice_right(halves(spec[j])), preferred_element_type=f32)
        if j == 0:
            forward, backward, power = part, part, coeff[0]
        else:
            forward = forward * coeff[0] + part
            backward = backward + power * part
            power = power * coeff[0]
    for i in range(sums.shape[0]):
        m, r = i // blocks * rows, i % blocks * width
        sums[i, 0] = forward[m : m + rows, r : r + width]
        sums[i, 1] = backward[m : m + rows, r : r + width]
    for copy in copies:
        copy.wait()


def pack_kernel(head, t, s, lt, ls, right, left, sems):
    n = head.shape[0]
    copies = [
        pltpu.make_async_copy(source, target, sems.at[k])
        for k, (source, target) in enumerate(
            (
                (t.at[n - 3 : n], right.at[0:3]),
                (s.at[n - 3 : n], right.at[3:6]),
                (lt.at[n - 1 : n], right.at[6:7]),
                (ls.at[n - 1 : n], right.at[7:8]),
                (head.at[n - 3 : n], right.at[8:11]),
                (t.at[0:2], left.at[0:2]),
                (s.at[0:2], left.at[2:4]),
                (head.at[0:2], left.at[4:6]),
            )
        )
    ]
    for copy in copies:
        copy.start()
    for copy in copies:
        copy.wait()


def halo_kernel(before, after, table_hi, table_lo, spec, planes, sems):
    copies = [
        pltpu.make_async_copy(before.at[8:11], planes.at[0:3], sems.at[0]),
        pltpu.make_async_copy(after.at[4:6], planes.at[3:5], sems.at[1]),
    ]
    for copy in copies:
        copy.start()
    for copy in copies:
        copy.wait()
    count, levels, columns = planes.shape
    value = planes[...].reshape(count * levels, columns)
    spec[...] = split_dot(halves(value), (table_hi[...], table_lo[...])).reshape(planes.shape)


def chunk_decay(rows, blocks, coeff, chunk, sem, sheets):
    n = lax.axis_index("yh")
    for name in GROUP_ALL[1:]:
        n = n * lax.axis_size(name) + lax.axis_index(name)
    width = chunk.shape[1]
    m = pl.multiple_of(n // blocks * rows, rows)
    r = pl.multiple_of(n % blocks * width, width)
    copy = pltpu.make_async_copy(coeff.at[0, pl.ds(m, rows), pl.ds(r, width)], chunk, sem)
    copy.start()
    copy.wait()
    return repeated(chunk[...], sheets)


def repeated(value, times):
    result, power = None, value
    while times:
        if times & 1:
            result = power if result is None else result * power
        power, times = power * power, times >> 1
    return result


def group_kernel(rows, blocks, sheets, got, coeff, out, chunk, sem):
    decay = chunk_decay(rows, blocks, coeff, chunk, sem, sheets)
    places, rings = got.shape[0], out.shape[0]
    forward, backward = None, None
    for p in range(places):
        a, b = got[p, 0, 0] + got[p, 1, 0], got[places - 1 - p, 0, 1] + got[places - 1 - p, 1, 1]
        forward = a if forward is None else forward * decay + a
        backward = b if backward is None else backward * decay + b
    mine = lax.axis_index("z")
    factor = repeated(decay, places)
    for k in range(rings):
        out[lax.rem(mine + 1 + k, rings), 0] = forward
        out[lax.rem(mine + 2 * rings - 1 - k, rings), 1] = backward
        forward, backward = forward * factor, backward * factor


def carry_kernel(rows, blocks, sheets, got, rings, coeff, out, chunk, sem):
    decay = chunk_decay(rows, blocks, coeff, chunk, sem, sheets)
    places, around = got.shape[0], rings.shape[0]
    closing = 1.0 / (1.0 - repeated(decay, places * around))
    left, right = rings[0, 0], rings[0, 1]
    for k in range(1, around):
        left, right = left + rings[k, 0], right + rings[k, 1]
    left, right = left * closing, right * closing
    for p in range(places):
        q = places - 1 - p
        for g in range(2):
            out[p, g, 0] = left
            out[q, g, 1] = right
        left = left * decay + (got[p, 0, 0] + got[p, 1, 0])
        right = right * decay + (got[q, 0, 1] + got[q, 1, 1])


def source_kernel(own, edge, own_other, edge_other, depth, out):
    half = own.shape[1]
    n = own.shape[0]
    first = lax.axis_index("gz") == 0
    matrix = depth[...] * (-1.0 / own.shape[2])
    here = jnp.where(first, matrix[:, :half], matrix[:, half:])
    there = jnp.where(first, matrix[:, half:], matrix[:, :half])
    matrix = thrice_left(halves(jnp.concatenate([here, there], axis=1)))

    def product(mine, other):
        full = halves(jnp.concatenate([mine, other], axis=0))
        return jnp.dot(matrix, thrice_right(full), preferred_element_type=f32)

    for j in range(n):
        out[3 + j] = product(own[j], own_other[j])
    for j in range(5):
        out[j if j < 3 else j + n] = product(edge[j], edge_other[j])


def solve_kernel(rows, blocks, source, carries, coeff_at, basis_at, hi_at, lo_at, phi, phi_edge, solved, levels_hi, levels_lo, coeff, basis, table_hi, table_lo, sems):
    pairs = ((coeff_at, coeff), (basis_at, basis), (hi_at, table_hi), (lo_at, table_lo))
    copies = [pltpu.make_async_copy(p, q, sems.at[k]) for k, (p, q) in enumerate(pairs)]
    for copy in copies:
        copy.start()
    copies[0].wait()
    count = source.shape[0]
    n = count - 5
    columns = source.shape[2]
    width = columns // blocks
    half = basis.shape[0] // 2

    def chunk(i, carry):
        m = pl.ds(pl.multiple_of(i // blocks * rows, rows), rows)
        r = pl.ds(pl.multiple_of(i % blocks * width, width), width)
        rho, kappa, a = coeff[0, m, r], coeff[1, m, r], coeff[2, m, r]
        growth = (2.0 + a) - rho
        f = [source[j, m, r] for j in range(count)]
        c, b = [None] * count, [None] * count
        c[2] = carries[i, 0]
        c[1] = (c[2] - f[2]) * growth
        c[0] = (c[1] - f[1]) * growth
        for j in range(3, count):
            c[j] = f[j] + rho * c[j - 1]
        b[n + 3] = carries[i, 1]
        b[n + 4] = (b[n + 3] - f[n + 3]) * growth
        for j in range(n + 2, -1, -1):
            b[j] = f[j] + rho * b[j + 1]
        values = [kappa * ((c[j] - f[j]) + b[j]) for j in range(count)]
        values.append(f[0] - a * values[0])
        values.append(f[count - 1] - a * values[count - 1])
        for j, value in enumerate(values):
            solved[j, m, r] = value
        return carry

    lax.fori_loop(0, carries.shape[0], chunk, 0)
    for copy in copies[1:]:
        copy.wait()
    first = lax.axis_index("gz") == 0
    share = thrice_left(halves(jnp.where(first, basis[:half, :], basis[half:, :])))

    def plane(j, carry):
        value = jnp.dot(share, thrice_right(halves(solved[j])), preferred_element_type=f32)
        here = pl.ds(pl.multiple_of(j * half, half), half)
        levels_hi[here, :], levels_lo[here, :] = halves(value)
        return carry

    lax.fori_loop(0, count + 2, plane, 0)
    result = split_dot((levels_hi[...], levels_lo[...]), (table_hi[...], table_lo[...]))
    result = result.reshape(count + 2, half, columns)
    phi[...] = result[3 : 3 + n]
    phi_edge[0:3] = result[0:3]
    phi_edge[3:7] = result[3 + n :]


AWAY = pl.BlockSpec(memory_space=pl.ANY)


def params():
    return pltpu.CompilerParams(vmem_limit_bytes=63 * 1024 * 1024)


def cost(us):
    return pl.CostEstimate(flops=int(us * 1e6), bytes_accessed=int(us * 3e6), transcendentals=0)


def call(kernel, outs, *args, scratch=(), us=2.0, name, away=(), out_away=()):
    many = isinstance(outs, (list, tuple))

    def whole(a):
        return pl.BlockSpec(a.shape, lambda i: (0,) * len(a.shape), pipeline_mode=pl.Buffered(1))

    return pl.pallas_call(
        kernel,
        grid=(1,),
        out_shape=outs,
        in_specs=[AWAY if k in away else whole(a) for k, a in enumerate(args)],
        out_specs=[AWAY if k in out_away else whole(a) for k, a in enumerate(outs)]
        if many
        else whole(outs),
        scratch_shapes=list(scratch),
        compiler_params=params(),
        cost_estimate=cost(us),
        name=name,
    )(*args)


def by_rows(kernel, outs, *args, us, name, counts={}):
    levels, columns = args[0].shape[1:]

    def spec(a, count=None):
        return pl.BlockSpec((count or a.shape[0], ROWS, columns), lambda i: (0, i, 0))

    return pl.pallas_call(
        kernel,
        grid=(levels // ROWS,),
        out_shape=outs,
        in_specs=[spec(a, counts.get(k)) for k, a in enumerate(args)],
        out_specs=[spec(o) for o in outs],
        compiler_params=params(),
        cost_estimate=cost(us),
        name=name,
    )(*args)


def shards(
    thermal_anomaly,
    saltiness_anomaly,
    eastward_flow,
    advective_ratio,
    dual_thermal_final,
    dual_saltiness_final,
    dual_flow_final,
    dual_kinematic_head,
    depth_into_eigenbasis,
    eigenbasis_into_depth,
    spectral_magnitudes,
):
    t, s, u, c, lt, ls, df, head = (
        jnp.transpose(a, (1, 0, 2))
        for a in (
            thermal_anomaly,
            saltiness_anomaly,
            eastward_flow,
            advective_ratio,
            dual_thermal_final,
            dual_saltiness_final,
            dual_flow_final,
            dual_kinematic_head,
        )
    )
    n, levels, columns = t.shape
    modes = depth_into_eigenbasis.shape[0]
    across = lax.axis_size(ALONG)
    places = lax.axis_size(GROUP)
    rings = lax.axis_size("z")
    chunks = places * lax.axis_size("gz")
    rows = max(ROWS, modes // chunks)
    blocks = chunks * rows // modes
    width = columns // blocks

    def to_right(block):
        return lax.ppermute(block, ALONG, [(i, (i + 1) % across) for i in range(across)])

    def to_left(block):
        return lax.ppermute(block, ALONG, [((i + 1) % across, i) for i in range(across)])

    def other_half(block):
        return lax.ppermute(block, "gz", [(0, 1), (1, 0)])

    def like(*shape):
        return jax.ShapeDtypeStruct(shape, f32)

    exact = hartley_table(columns)
    upper = exact.astype(np.float32).astype(jnp.bfloat16)
    table_hi = jnp.asarray(upper)
    table_lo = jnp.asarray((exact - upper.astype(np.float64)).astype(jnp.bfloat16))
    waves = jnp.asarray(
        (2.0 - 2.0 * np.cos(np.arange(columns) * (2.0 * math.pi / columns))).astype(np.float32)
    ).reshape(1, columns)

    right, left = call(
        pack_kernel,
        [like(11, levels, columns), like(6, levels, columns)],
        head, t, s, lt, ls,
        scratch=[pltpu.SemaphoreType.DMA((8,))],
        away=range(5),
        us=2.0,
        name="pack",
    )
    before, after = to_right(right), to_left(left)

    spec, coeff, sums, flow_right, flow_left = call(
        lambda *refs: moments_kernel(rows, blocks, *refs),
        [
            like(n, levels, columns),
            like(3, modes, columns),
            like(chunks, 2, rows, width),
            like(10, levels, columns),
            like(11, levels, columns),
        ],
        head, table_hi, table_lo, depth_into_eigenbasis,
        spectral_magnitudes.reshape(1, modes), waves, u, c, df,
        scratch=[pltpu.SemaphoreType.DMA((6,))],
        away=(6, 7, 8),
        us=5.0,
        name="block_moments",
    )
    gathered = lax.all_to_all(sums, GROUP_ALL, 0, 0, tiled=True)
    gathered, late, flow_right, flow_left = lax.optimization_barrier(
        (gathered, spec, flow_right, flow_left)
    )
    gathered = gathered.reshape(places, chunks // places, 2, rows, width)
    edge = call(
        halo_kernel,
        like(5, levels, columns),
        before, after, table_hi, table_lo,
        scratch=[pltpu.VMEM((5, levels, columns), f32), pltpu.SemaphoreType.DMA((2,))],
        away=(0, 1),
        us=2.0,
        name="edge_spectrum",
    )
    spec_other = other_half(late)
    edge_other = other_half(edge)
    flow_before, flow_after = to_right(flow_right), to_left(flow_left)

    t_base, s_base, c_base, to_left_part, to_right_part = by_rows(
        tracer_kernel,
        [like(n, levels, columns)] * 3 + [like(6, levels, columns), like(4, levels, columns)],
        t, s, c, lt, ls, before, after,
        us=9.0,
        name="tracers",
        counts={5: 8, 6: 4},
    )
    from_right = to_left(to_left_part)
    from_left = to_right(to_right_part)

    decay_scratch = [pltpu.VMEM((rows, width), f32), pltpu.SemaphoreType.DMA]
    ring = call(
        lambda *refs: group_kernel(rows, blocks, n, *refs),
        like(rings, 2, rows, width),
        gathered, coeff,
        scratch=decay_scratch,
        away=(1,),
        us=1.0,
        name="group_moments",
    )
    ring = lax.all_to_all(ring, "z", 0, 0, tiled=True)
    ring, t_base = lax.optimization_barrier((ring, t_base))
    carries = call(
        lambda *refs: carry_kernel(rows, blocks, n, *refs),
        like(places, chunks // places, 2, rows, width),
        gathered, ring, coeff,
        scratch=decay_scratch,
        away=(2,),
        us=1.0,
        name="group_carries",
    )
    carries = lax.all_to_all(carries.reshape(chunks, 2, rows, width), GROUP_ALL, 0, 0, tiled=True)

    source = call(
        source_kernel,
        like(n + 5, modes, columns),
        spec, edge, spec_other, edge_other, depth_into_eigenbasis,
        us=4.0,
        name="mode_source",
    )
    phi, phi_edge = call(
        lambda *refs: solve_kernel(rows, blocks, *refs),
        [like(n, levels, columns), like(7, levels, columns)],
        source, carries, coeff, eigenbasis_into_depth, table_hi, table_lo,
        scratch=[pltpu.VMEM((n + 7, modes, columns), f32)]
        + [pltpu.VMEM(((n + 7) * levels, columns), bf16)] * 2
        + [
            pltpu.VMEM((3, modes, columns), f32),
            pltpu.VMEM((modes, modes), f32),
            pltpu.VMEM((columns, columns), bf16),
            pltpu.VMEM((columns, columns), bf16),
            pltpu.SemaphoreType.DMA((4,)),
        ],
        away=(2, 3, 4, 5),
        us=7.0,
        name="pressure",
    )
    t_bar, s_bar, u_bar, c_bar = by_rows(
        flow_kernel,
        [like(n, levels, columns)] * 4,
        u, c, df, flow_before, flow_after, phi, phi_edge,
        t_base, s_base, c_base, from_left, from_right,
        us=7.0,
        name="flow",
    )
    return tuple(jnp.transpose(a, (1, 0, 2)) for a in (t_bar, s_bar, u_bar, c_bar, phi))


def solution(mesh):
    gx, gz = mesh.shape["gx"], mesh.shape["gz"]
    inner = Mesh(mesh.devices.reshape(SPLIT[gx] + (gz,)), ALONG + ("gz",))
    field = P("gz", ALONG, None)
    return jax.shard_map(
        shards,
        mesh=inner,
        in_specs=(field,) * 8 + (P(),) * 3,
        out_specs=(field,) * 5,
        check_vma=False,
    )
```

```python
import math

import jax
import jax.numpy as jnp
import numpy as np
from jax import lax
from jax.experimental import pallas as pl
from jax.experimental.pallas import tpu as pltpu
from jax.sharding import Mesh, PartitionSpec as P

f32 = jnp.float32
bf16 = jnp.bfloat16
LANES = 128
ROWS = 8
SPLIT = {128: (8, 2, 4, 2)}
ALONG = ("z", "yh", "x", "c")
GROUP = ("yh", "x", "c")
GROUP_ALL = ("yh", "x", "c", "gz")


def hartley_table(length):
    numbers = np.arange(length)
    angle = (numbers[:, None] * numbers[None, :] % length) * (2.0 * math.pi / length)
    return np.cos(angle) + np.sin(angle)


def halves(value):
    upper = value.astype(bf16)
    return upper, (value - upper.astype(f32)).astype(bf16)


def stacked_left(pair):
    upper = jnp.concatenate([pair[0], pair[0]], axis=1)
    lower = jnp.concatenate([pair[1], jnp.zeros_like(pair[1])], axis=1)
    return jnp.concatenate([upper, lower], axis=0)


def stacked_dot(left, pair):
    both = jnp.dot(left, jnp.concatenate(pair, axis=0), preferred_element_type=f32)
    half = both.shape[0] // 2
    return both[:half] + both[half:]


def thrice_left(pair):
    return jnp.concatenate([pair[0], pair[0], pair[1]], axis=1)


def thrice_right(pair):
    return jnp.concatenate([pair[0], pair[1], pair[0]], axis=0)


def split_dot(a, b):
    (a_hi, a_lo), (b_hi, b_lo) = a, b

    def dot(p, q):
        return jnp.dot(p, q, preferred_element_type=f32)

    return dot(a_hi, b_hi) + (dot(a_hi, b_lo) + dot(a_lo, b_hi))


def face_terms(edges, ratio):
    positive = ratio >= 0.0
    d1 = jnp.where(positive, edges[0], edges[4])
    d2 = jnp.where(positive, edges[1], edges[3])
    d3 = edges[2]
    d4 = jnp.where(positive, edges[3], edges[1])
    s1, s2, s3 = d2 - d1, d3 - d2, d4 - d3
    e0, e1, e2 = (d2 + d2) + s1, d2 + d3, (d3 + d3) - s3
    t0, t1, t2 = (13.0 / 3.0) * s1, (13.0 / 3.0) * s2, (13.0 / 3.0) * s3
    r0 = 1.0 / (t0 * s1 + (e0 * e0 + 0.04))
    r1 = 1.0 / (t1 * s2 + (e1 * e1 + 0.04))
    r2 = 1.0 / (t2 * s3 + (e2 * e2 + 0.04))
    u0, u1, u2 = (1.0 / 6.0) * (r0 * r0), r1 * r1, 0.5 * (r2 * r2)
    norm = 1.0 / (u0 + u1 + u2)
    w0, w1, w2 = u0 * norm, u1 * norm, u2 * norm
    bend = s1 - s2
    a2, cc = bend + bend, s2 - s3
    z = w0 * a2 + w2 * cc
    total = (e1 + d3) + z
    n0, n1, n2 = w0 * r0 * (z - a2), w1 * r1 * z, w2 * r2 * (z - cc)
    p0, q0 = n0 * t0, n0 * e0
    p1, q1 = n1 * t1, n1 * e1
    p2, q2 = n2 * t2, n2 * e2
    h0, h2 = 0.5 * w0, 0.25 * w2
    lean = h0 - h2
    m1, m4 = h0 + (p0 + q0), h2 + (q2 - p2)
    g2 = ((0.25 + lean) + m1) + ((q0 + q0) + (q1 - p1))
    g3 = ((0.5 - lean) + m4) + ((q2 + q2) + (p1 + q1))
    return positive, total, (m1, g2, g3, m4)


def weno_tile(field, ratio, cotangent, faces, cells, owned):
    edge_of, edge_bar, cell_bar, ratio_bar = {}, {}, {}, {}

    def edge(x):
        if x not in edge_of:
            edge_of[x] = field(x + 1) - field(x)
        return edge_of[x]

    def add(store, key, value, less=False):
        if key in store:
            store[key] = store[key] - value if less else store[key] + value
        else:
            store[key] = -value if less else value

    for f in faces:
        c, e = ratio(f), cotangent(f)
        positive, total, (m1, g2, g3, m4) = face_terms([edge(f - 3 + k) for k in range(5)], c)
        gain = (2.0 / 3.0) * (jnp.abs(c) * e)
        m1, g2, g3, m4 = gain * m1, gain * g2, gain * g3, gain * m4
        zero = jnp.zeros_like(m1)
        add(edge_bar, f - 3, jnp.where(positive, m1, zero), True)
        add(edge_bar, f - 2, jnp.where(positive, g2, -m4))
        add(edge_bar, f - 1, g3)
        add(edge_bar, f, jnp.where(positive, -m4, g2))
        add(edge_bar, f + 1, jnp.where(positive, zero, m1), True)
        add(cell_bar, f - 1, jnp.maximum(c, 0.0) * e)
        add(cell_bar, f, jnp.minimum(c, 0.0) * e)
        if f in owned:
            center = jnp.where(positive, field(f - 1), field(f))
            sixth = total * (1.0 / 6.0)
            ratio_bar[f] = e * (center + jnp.where(positive, sixth, -sixth))
    bars = {}
    for x in cells:
        parts = []
        if x - 1 in edge_bar:
            parts.append(edge_bar[x - 1])
        if x in edge_bar:
            parts.append(-edge_bar[x])
        if x in cell_bar:
            parts.append(cell_bar[x])
        bars[x] = sum(parts[1:], parts[0])
    return bars, ratio_bar


def planes(own, before, after, own_count, before_at, before_count, after_at, lanes):
    def read(x):
        if x < 0:
            return before[before_at + before_count + x, :, lanes]
        if x >= own_count:
            return after[after_at + x - own_count, :, lanes]
        return own[x, :, lanes]

    return read


def tracer_kernel(t, s, c, lt, ls, before, after, t_out, s_out, c_out, left_out, right_out):
    n, _, width = t.shape

    def tile(l, carry):
        lanes = pl.ds(pl.multiple_of(l * LANES, LANES), LANES)
        sums = {}
        for k, (own, dual, out) in enumerate(((t, lt, t_out), (s, ls, s_out))):
            field = planes(own, before, after, n, 3 * k, 3, 2 * k, lanes)
            lam = planes(dual, before, after, n, 6 + k, 1, 0, lanes)
            bars, ratio_bar = weno_tile(
                field,
                lambda f: c[f, :, lanes],
                lambda f: lam(f) - lam(f - 1),
                range(n),
                range(-3, n + 2),
                range(n),
            )
            for x in range(n):
                out[x, :, lanes] = dual[x, :, lanes] + bars[x]
                sums[x] = sums[x] + ratio_bar[x] if x in sums else ratio_bar[x]
            for x in range(3):
                left_out[3 * k + x, :, lanes] = bars[x - 3]
            for x in range(2):
                right_out[2 * k + x, :, lanes] = bars[n + x]
        for x in range(n):
            c_out[x, :, lanes] = sums[x]
        return carry

    lax.fori_loop(0, width // LANES, tile, 0)


def flow_kernel(
    u, c, df, before, after, phi, phi_edge, t_in, s_in, c_in, from_left, from_right,
    t_out, s_out, u_out, c_out,
):
    n, _, width = u.shape

    def tile(l, carry):
        lanes = pl.ds(pl.multiple_of(l * LANES, LANES), LANES)
        field = planes(u, before, after, n, 0, 5, 0, lanes)
        ratio = planes(c, before, after, n, 5, 2, 5, lanes)
        dual = planes(df, before, after, n, 7, 3, 8, lanes)
        head = planes(phi, phi_edge, phi_edge, n, 0, 3, 3, lanes)
        step = {x: head(x) - head(x - 1) for x in range(-2, n + 2)}

        def bend(x):
            if x == -3:
                return phi_edge[5, :, lanes]
            if x == n + 1:
                return phi_edge[6, :, lanes]
            return step[x] - step[x + 1]

        bars, ratio_bar = weno_tile(
            field,
            ratio,
            lambda f: (dual(f) - dual(f - 1)) + bend(f - 1),
            range(-2, n + 3),
            range(n),
            range(n),
        )
        for x in range(n):
            u_out[x, :, lanes] = (df[x, :, lanes] - step[x]) + bars[x]
            c_out[x, :, lanes] = c_in[x, :, lanes] + ratio_bar[x]
        for k, (base, out) in enumerate(((t_in, t_out), (s_in, s_out))):
            for x in range(n):
                value = base[x, :, lanes]
                if x < 2:
                    value = value + from_left[2 * k + x, :, lanes]
                if x >= n - 3:
                    value = value + from_right[3 * k + x - (n - 3), :, lanes]
                out[x, :, lanes] = value
        return carry

    lax.fori_loop(0, width // LANES, tile, 0)


def moments_kernel(rows, blocks, head, table_hi, table_lo, depth, rates, waves, u, c, df, spec, coeff, sums, decay, flow_right, flow_left, sems):
    n, levels, columns = head.shape
    width = columns // blocks
    copies = [
        pltpu.make_async_copy(source, target, sems.at[k])
        for k, (source, target) in enumerate(
            (
                (u.at[n - 5 : n], flow_right.at[0:5]),
                (c.at[n - 2 : n], flow_right.at[5:7]),
                (df.at[n - 3 : n], flow_right.at[7:10]),
                (u.at[0:5], flow_left.at[0:5]),
                (c.at[0:3], flow_left.at[5:8]),
                (df.at[0:3], flow_left.at[8:11]),
            )
        )
    ]
    for copy in copies:
        copy.start()
    a = jnp.transpose(jnp.broadcast_to(rates[...], (columns, rates.shape[1]))) + waves[...]
    root = jnp.sqrt(a * (1.0 + 0.25 * a))
    rho = 1.0 / ((1.0 + 0.5 * a) + root)
    coeff[0] = rho
    coeff[1] = 0.5 / root
    coeff[2] = a
    values = head[...].reshape(n * levels, columns)
    values = split_dot(halves(values), (table_hi[...], table_lo[...]))
    spec[...] = values.reshape(n, levels, columns)
    first = lax.axis_index("gz") == 0
    share = jnp.where(first, depth[:, :levels], depth[:, levels:])
    share = thrice_left(halves(share * (-1.0 / columns)))
    for j in range(n):
        part = jnp.dot(share, thrice_right(halves(spec[j])), preferred_element_type=f32)
        if j == 0:
            forward, backward, power = part, part, coeff[0]
        else:
            forward = forward * coeff[0] + part
            backward = backward + power * part
            power = power * coeff[0]
    for i in range(sums.shape[0]):
        m, r = i // blocks * rows, i % blocks * width
        sums[i, 0] = forward[m : m + rows, r : r + width]
        sums[i, 1] = backward[m : m + rows, r : r + width]
    m, r = my_chunk(rows, blocks, width)
    decay[...] = repeated(coeff[0, m, r], n)
    for copy in copies:
        copy.wait()


def pack_kernel(head, t, s, lt, ls, right, left, sems):
    n = head.shape[0]
    copies = [
        pltpu.make_async_copy(source, target, sems.at[k])
        for k, (source, target) in enumerate(
            (
                (t.at[n - 3 : n], right.at[0:3]),
                (s.at[n - 3 : n], right.at[3:6]),
                (lt.at[n - 1 : n], right.at[6:7]),
                (ls.at[n - 1 : n], right.at[7:8]),
                (head.at[n - 3 : n], right.at[8:11]),
                (t.at[0:2], left.at[0:2]),
                (s.at[0:2], left.at[2:4]),
                (head.at[0:2], left.at[4:6]),
            )
        )
    ]
    for copy in copies:
        copy.start()
    for copy in copies:
        copy.wait()


def halo_kernel(before, after, table_hi, table_lo, spec, planes, sems):
    copies = [
        pltpu.make_async_copy(before.at[8:11], planes.at[0:3], sems.at[0]),
        pltpu.make_async_copy(after.at[4:6], planes.at[3:5], sems.at[1]),
    ]
    for copy in copies:
        copy.start()
    for copy in copies:
        copy.wait()
    count, levels, columns = planes.shape
    value = planes[...].reshape(count * levels, columns)
    spec[...] = split_dot(halves(value), (table_hi[...], table_lo[...])).reshape(planes.shape)


def my_chunk(rows, blocks, width):
    n = lax.axis_index("yh")
    for name in GROUP_ALL[1:]:
        n = n * lax.axis_size(name) + lax.axis_index(name)
    m = pl.multiple_of(n // blocks * rows, rows)
    r = pl.multiple_of(n % blocks * width, width)
    return pl.ds(m, rows), pl.ds(r, width)


def repeated(value, times):
    result, power = None, value
    while times:
        if times & 1:
            result = power if result is None else result * power
        power, times = power * power, times >> 1
    return result


def group_kernel(got, decay, out):
    decay = decay[...]
    places, rings = got.shape[0], out.shape[0]
    forward, backward = None, None
    for p in range(places):
        a, b = got[p, 0, 0] + got[p, 1, 0], got[places - 1 - p, 0, 1] + got[places - 1 - p, 1, 1]
        forward = a if forward is None else forward * decay + a
        backward = b if backward is None else backward * decay + b
    mine = lax.axis_index("z")
    factor = repeated(decay, places)
    for k in range(rings):
        out[lax.rem(mine + 1 + k, rings), 0] = forward
        out[lax.rem(mine + 2 * rings - 1 - k, rings), 1] = backward
        forward, backward = forward * factor, backward * factor


def carry_kernel(got, rings, decay, out):
    decay = decay[...]
    places, around = got.shape[0], rings.shape[0]
    closing = 1.0 / (1.0 - repeated(decay, places * around))
    left, right = rings[0, 0], rings[0, 1]
    for k in range(1, around):
        left, right = left + rings[k, 0], right + rings[k, 1]
    left, right = left * closing, right * closing
    for p in range(places):
        q = places - 1 - p
        for g in range(2):
            out[p, g, 0] = left
            out[q, g, 1] = right
        left = left * decay + (got[p, 0, 0] + got[p, 1, 0])
        right = right * decay + (got[q, 0, 1] + got[q, 1, 1])


def source_kernel(own_at, edge_at, own_other_at, edge_other_at, depth_at, out_at, own, edge, own_other, edge_other, depth, out, sems):
    pairs = (
        (depth_at, depth),
        (own_at, own),
        (own_other_at, own_other),
        (edge_at, edge),
        (edge_other_at, edge_other),
    )
    copies = [pltpu.make_async_copy(p, q, sems.at[k]) for k, (p, q) in enumerate(pairs)]
    for copy in copies:
        copy.start()
    half = own.shape[1]
    n = own.shape[0]
    copies[0].wait()
    first = lax.axis_index("gz") == 0
    matrix = depth[...] * (-1.0 / own.shape[2])
    here = jnp.where(first, matrix[:, :half], matrix[:, half:])
    there = jnp.where(first, matrix[:, half:], matrix[:, :half])
    matrix = stacked_left(halves(jnp.concatenate([here, there], axis=1)))

    def product(mine, other):
        return stacked_dot(matrix, halves(jnp.concatenate([mine, other], axis=0)))

    copies[1].wait()
    copies[2].wait()
    for j in range(n):
        out[3 + j] = product(own[j], own_other[j])
    copies.append(pltpu.make_async_copy(out.at[3 : 3 + n], out_at.at[3 : 3 + n], sems.at[5]))
    copies[5].start()
    copies[3].wait()
    copies[4].wait()
    for j in range(5):
        out[j if j < 3 else j + n] = product(edge[j], edge_other[j])
    for k, (first, count) in enumerate(((0, 3), (3 + n, 2))):
        part = pl.ds(first, count)
        copies.append(pltpu.make_async_copy(out.at[part], out_at.at[part], sems.at[6 + k]))
        copies[6 + k].start()
    for copy in copies[5:]:
        copy.wait()


def solve_kernel(rows, blocks, source_at, carries_at, coeff_at, basis_at, hi_at, lo_at, phi, phi_edge, solved, levels_hi, levels_lo, source, carries, coeff, basis, table_hi, table_lo, heads, sems):
    pairs = (
        (carries_at, carries),
        (coeff_at, coeff),
        (source_at, source),
        (basis_at, basis),
        (hi_at, table_hi),
        (lo_at, table_lo),
    )
    copies = [pltpu.make_async_copy(p, q, sems.at[k]) for k, (p, q) in enumerate(pairs)]
    for copy in copies:
        copy.start()
    for copy in copies[:3]:
        copy.wait()
    count = source.shape[0]
    n = count - 5
    columns = source.shape[2]
    width = columns // blocks
    half = basis.shape[0] // 2

    def chunk(i, carry):
        m = pl.ds(pl.multiple_of(i // blocks * rows, rows), rows)
        r = pl.ds(pl.multiple_of(i % blocks * width, width), width)
        rho, kappa, a = coeff[0, m, r], coeff[1, m, r], coeff[2, m, r]
        growth = (2.0 + a) - rho
        f = [source[j, m, r] for j in range(count)]
        c, b = [None] * count, [None] * count
        c[2] = carries[i, 0]
        c[1] = (c[2] - f[2]) * growth
        c[0] = (c[1] - f[1]) * growth
        for j in range(3, count):
            c[j] = f[j] + rho * c[j - 1]
        b[n + 3] = carries[i, 1]
        b[n + 4] = (b[n + 3] - f[n + 3]) * growth
        for j in range(n + 2, -1, -1):
            b[j] = f[j] + rho * b[j + 1]
        values = [kappa * ((c[j] - f[j]) + b[j]) for j in range(count)]
        values.append(f[0] - a * values[0])
        values.append(f[count - 1] - a * values[count - 1])
        for j, value in enumerate(values):
            solved[j, m, r] = value
        return carry

    lax.fori_loop(0, carries.shape[0], chunk, 0)
    for copy in copies[3:]:
        copy.wait()
    first = lax.axis_index("gz") == 0
    share = stacked_left(halves(jnp.where(first, basis[:half, :], basis[half:, :])))

    def plane(j, carry):
        value = stacked_dot(share, halves(solved[j]))
        here = pl.ds(pl.multiple_of(j * half, half), half)
        levels_hi[here, :], levels_lo[here, :] = halves(value)
        return carry

    lax.fori_loop(0, count + 2, plane, 0)
    result = split_dot((levels_hi[...], levels_lo[...]), (table_hi[...], table_lo[...]))
    heads[...] = result.reshape(count + 2, half, columns)
    pairs = (
        (heads.at[3 : 3 + n], phi),
        (heads.at[0:3], phi_edge.at[0:3]),
        (heads.at[3 + n : count + 2], phi_edge.at[3:7]),
    )
    copies = [pltpu.make_async_copy(p, q, sems.at[6 + k]) for k, (p, q) in enumerate(pairs)]
    for copy in copies:
        copy.start()
    for copy in copies:
        copy.wait()


AWAY = pl.BlockSpec(memory_space=pltpu.HBM)


def params():
    return pltpu.CompilerParams(vmem_limit_bytes=63 * 1024 * 1024)


def cost(us):
    return pl.CostEstimate(flops=int(us * 1e6), bytes_accessed=int(us * 3e6), transcendentals=0)


def call(kernel, outs, *args, scratch=(), us=2.0, name, away=(), out_away=()):
    many = isinstance(outs, (list, tuple))

    def whole(a):
        return pl.BlockSpec(a.shape, lambda i: (0,) * len(a.shape), pipeline_mode=pl.Buffered(1))

    return pl.pallas_call(
        kernel,
        grid=(1,),
        out_shape=outs,
        in_specs=[AWAY if k in away else whole(a) for k, a in enumerate(args)],
        out_specs=[AWAY if k in out_away else whole(a) for k, a in enumerate(outs)]
        if many
        else whole(outs),
        scratch_shapes=list(scratch),
        compiler_params=params(),
        cost_estimate=cost(us),
        name=name,
    )(*args)


def near(kernel, outs, *args, us, name, scratch=(), away=(), out_away=(), limit=48):
    where = pl.BlockSpec(memory_space=pltpu.VMEM)
    return pl.pallas_call(
        kernel,
        out_shape=outs,
        in_specs=[AWAY if k in away else where for k in range(len(args))],
        out_specs=[AWAY if k in out_away else where for k in range(len(outs))]
        if isinstance(outs, list)
        else where,
        scratch_shapes=list(scratch),
        compiler_params=pltpu.CompilerParams(vmem_limit_bytes=limit * 1024 * 1024),
        cost_estimate=cost(us),
        name=name,
    )(*args)


def by_rows(kernel, outs, *args, us, name, counts={}):
    levels, columns = args[0].shape[1:]

    def spec(a, count=None):
        return pl.BlockSpec((count or a.shape[0], ROWS, columns), lambda i: (0, i, 0))

    return pl.pallas_call(
        kernel,
        grid=(levels // ROWS,),
        out_shape=outs,
        in_specs=[spec(a, counts.get(k)) for k, a in enumerate(args)],
        out_specs=[spec(o) for o in outs],
        compiler_params=params(),
        cost_estimate=cost(us),
        name=name,
    )(*args)


def shards(
    thermal_anomaly,
    saltiness_anomaly,
    eastward_flow,
    advective_ratio,
    dual_thermal_final,
    dual_saltiness_final,
    dual_flow_final,
    dual_kinematic_head,
    depth_into_eigenbasis,
    eigenbasis_into_depth,
    spectral_magnitudes,
):
    t, s, u, c, lt, ls, df, head = (
        jnp.transpose(a, (1, 0, 2))
        for a in (
            thermal_anomaly,
            saltiness_anomaly,
            eastward_flow,
            advective_ratio,
            dual_thermal_final,
            dual_saltiness_final,
            dual_flow_final,
            dual_kinematic_head,
        )
    )
    n, levels, columns = t.shape
    modes = depth_into_eigenbasis.shape[0]
    across = lax.axis_size(ALONG)
    places = lax.axis_size(GROUP)
    rings = lax.axis_size("z")
    chunks = places * lax.axis_size("gz")
    rows = max(ROWS, modes // chunks)
    blocks = chunks * rows // modes
    width = columns // blocks

    def to_right(block):
        return lax.ppermute(block, ALONG, [(i, (i + 1) % across) for i in range(across)])

    def to_left(block):
        return lax.ppermute(block, ALONG, [((i + 1) % across, i) for i in range(across)])

    def other_half(block):
        return lax.ppermute(block, "gz", [(0, 1), (1, 0)])

    def like(*shape):
        return jax.ShapeDtypeStruct(shape, f32)

    exact = hartley_table(columns)
    upper = exact.astype(np.float32).astype(jnp.bfloat16)
    table_hi = jnp.asarray(upper)
    table_lo = jnp.asarray((exact - upper.astype(np.float64)).astype(jnp.bfloat16))
    waves = jnp.asarray(
        (2.0 - 2.0 * np.cos(np.arange(columns) * (2.0 * math.pi / columns))).astype(np.float32)
    ).reshape(1, columns)

    right, left = call(
        pack_kernel,
        [like(11, levels, columns), like(6, levels, columns)],
        head, t, s, lt, ls,
        scratch=[pltpu.SemaphoreType.DMA((8,))],
        away=range(5),
        us=2.0,
        name="pack",
    )
    before, after = to_right(right), to_left(left)

    spec, coeff, sums, decay, flow_right, flow_left = call(
        lambda *refs: moments_kernel(rows, blocks, *refs),
        [
            like(n, levels, columns),
            like(3, modes, columns),
            like(chunks, 2, rows, width),
            like(rows, width),
            like(10, levels, columns),
            like(11, levels, columns),
        ],
        head, table_hi, table_lo, depth_into_eigenbasis,
        spectral_magnitudes.reshape(1, modes), waves, u, c, df,
        scratch=[pltpu.SemaphoreType.DMA((6,))],
        away=(6, 7, 8),
        us=5.0,
        name="block_moments",
    )
    gathered = lax.all_to_all(sums, GROUP_ALL, 0, 0, tiled=True)
    t_base, s_base, c_base, to_left_part, to_right_part = by_rows(
        tracer_kernel,
        [like(n, levels, columns)] * 3 + [like(6, levels, columns), like(4, levels, columns)],
        t, s, c, lt, ls, before, after,
        us=9.0,
        name="tracers",
        counts={5: 8, 6: 4},
    )
    gathered, late, flow_right, flow_left, t_base = lax.optimization_barrier(
        (gathered, spec, flow_right, flow_left, t_base)
    )
    gathered = gathered.reshape(places, chunks // places, 2, rows, width)
    spec_other = other_half(late)
    flow_before, flow_after = to_right(flow_right), to_left(flow_left)
    edge = call(
        halo_kernel,
        like(5, levels, columns),
        before, after, table_hi, table_lo,
        scratch=[pltpu.VMEM((5, levels, columns), f32), pltpu.SemaphoreType.DMA((2,))],
        away=(0, 1),
        us=2.0,
        name="edge_spectrum",
    )
    edge_other = other_half(edge)

    ring = near(
        group_kernel,
        like(rings, 2, rows, width),
        gathered, decay,
        us=1.0,
        name="group_moments",
    )
    ring = lax.all_to_all(ring, "z", 0, 0, tiled=True)
    carries = near(
        carry_kernel,
        like(places, chunks // places, 2, rows, width),
        gathered, ring, decay,
        us=1.0,
        name="group_carries",
    )
    carries, to_left_part, to_right_part = lax.optimization_barrier(
        (carries, to_left_part, to_right_part)
    )
    carries = lax.all_to_all(carries.reshape(chunks, 2, rows, width), GROUP_ALL, 0, 0, tiled=True)
    from_right = to_left(to_left_part)
    from_left = to_right(to_right_part)

    (source,) = near(
        source_kernel,
        [like(n + 5, modes, columns)],
        spec, edge, spec_other, edge_other, depth_into_eigenbasis,
        scratch=[
            pltpu.VMEM((n, levels, columns), f32),
            pltpu.VMEM((5, levels, columns), f32),
            pltpu.VMEM((n, levels, columns), f32),
            pltpu.VMEM((5, levels, columns), f32),
            pltpu.VMEM((modes, modes), f32),
            pltpu.VMEM((n + 5, modes, columns), f32),
            pltpu.SemaphoreType.DMA((8,)),
        ],
        away=range(5),
        out_away=(0,),
        us=4.0,
        limit=63,
        name="mode_source",
    )
    phi, phi_edge = near(
        lambda *refs: solve_kernel(rows, blocks, *refs),
        [like(n, levels, columns), like(7, levels, columns)],
        source, carries, coeff, eigenbasis_into_depth, table_hi, table_lo,
        scratch=[pltpu.VMEM((n + 7, modes, columns), f32)]
        + [pltpu.VMEM(((n + 7) * levels, columns), bf16)] * 2
        + [
            pltpu.VMEM((n + 5, modes, columns), f32),
            pltpu.VMEM((chunks, 2, rows, width), f32),
            pltpu.VMEM((3, modes, columns), f32),
            pltpu.VMEM((modes, modes), f32),
            pltpu.VMEM((columns, columns), bf16),
            pltpu.VMEM((columns, columns), bf16),
            pltpu.VMEM((n + 7, levels, columns), f32),
            pltpu.SemaphoreType.DMA((9,)),
        ],
        away=range(6),
        out_away=(0, 1),
        us=7.0,
        limit=63,
        name="pressure",
    )
    t_bar, s_bar, u_bar, c_bar = by_rows(
        flow_kernel,
        [like(n, levels, columns)] * 4,
        u, c, df, flow_before, flow_after, phi, phi_edge,
        t_base, s_base, c_base, from_left, from_right,
        us=7.0,
        name="flow",
    )
    return tuple(jnp.transpose(a, (1, 0, 2)) for a in (t_bar, s_bar, u_bar, c_bar, phi))


def solution(mesh):
    gx, gz = mesh.shape["gx"], mesh.shape["gz"]
    inner = Mesh(mesh.devices.reshape(SPLIT[gx] + (gz,)), ALONG + ("gz",))
    field = P("gz", ALONG, None)
    return jax.shard_map(
        shards,
        mesh=inner,
        in_specs=(field,) * 8 + (P(),) * 3,
        out_specs=(field,) * 5,
        check_vma=False,
    )
```

```python
import math

import jax
import jax.numpy as jnp
import numpy as np
from jax import lax
from jax.experimental import pallas as pl
from jax.experimental.pallas import tpu as pltpu
from jax.sharding import Mesh, PartitionSpec as P

f32 = jnp.float32
bf16 = jnp.bfloat16
LANES = 128
ROWS = 8
SPLIT = {128: (8, 2, 4, 2)}
ALONG = ("z", "yh", "x", "c")
GROUP = ("yh", "x", "c")
GROUP_ALL = ("yh", "x", "c", "gz")


def hartley_table(length):
    numbers = np.arange(length)
    angle = (numbers[:, None] * numbers[None, :] % length) * (2.0 * math.pi / length)
    return np.cos(angle) + np.sin(angle)


def halves(value):
    upper = value.astype(bf16)
    return upper, (value - upper.astype(f32)).astype(bf16)


def stacked_left(pair):
    upper = jnp.concatenate([pair[0], pair[0]], axis=1)
    lower = jnp.concatenate([pair[1], jnp.zeros_like(pair[1])], axis=1)
    return jnp.concatenate([upper, lower], axis=0)


def stacked_dot(left, pair):
    both = jnp.dot(left, jnp.concatenate(pair, axis=0), preferred_element_type=f32)
    half = both.shape[0] // 2
    return both[:half] + both[half:]


def thrice_left(pair):
    return jnp.concatenate([pair[0], pair[0], pair[1]], axis=1)


def thrice_right(pair):
    return jnp.concatenate([pair[0], pair[1], pair[0]], axis=0)


def split_dot(a, b):
    (a_hi, a_lo), (b_hi, b_lo) = a, b

    def dot(p, q):
        return jnp.dot(p, q, preferred_element_type=f32)

    return dot(a_hi, b_hi) + (dot(a_hi, b_lo) + dot(a_lo, b_hi))


def face_terms(edges, ratio):
    positive = ratio >= 0.0
    d1 = jnp.where(positive, edges[0], edges[4])
    d2 = jnp.where(positive, edges[1], edges[3])
    d3 = edges[2]
    d4 = jnp.where(positive, edges[3], edges[1])
    s1, s2, s3 = d2 - d1, d3 - d2, d4 - d3
    e0, e1, e2 = (d2 + d2) + s1, d2 + d3, (d3 + d3) - s3
    t0, t1, t2 = (13.0 / 3.0) * s1, (13.0 / 3.0) * s2, (13.0 / 3.0) * s3
    r0 = 1.0 / (t0 * s1 + (e0 * e0 + 0.04))
    r1 = 1.0 / (t1 * s2 + (e1 * e1 + 0.04))
    r2 = 1.0 / (t2 * s3 + (e2 * e2 + 0.04))
    u0, u1, u2 = (1.0 / 6.0) * (r0 * r0), r1 * r1, 0.5 * (r2 * r2)
    norm = 1.0 / (u0 + u1 + u2)
    w0, w1, w2 = u0 * norm, u1 * norm, u2 * norm
    bend = s1 - s2
    a2, cc = bend + bend, s2 - s3
    z = w0 * a2 + w2 * cc
    total = (e1 + d3) + z
    n0, n1, n2 = w0 * r0 * (z - a2), w1 * r1 * z, w2 * r2 * (z - cc)
    p0, q0 = n0 * t0, n0 * e0
    p1, q1 = n1 * t1, n1 * e1
    p2, q2 = n2 * t2, n2 * e2
    h0, h2 = 0.5 * w0, 0.25 * w2
    lean = h0 - h2
    m1, m4 = h0 + (p0 + q0), h2 + (q2 - p2)
    g2 = ((0.25 + lean) + m1) + ((q0 + q0) + (q1 - p1))
    g3 = ((0.5 - lean) + m4) + ((q2 + q2) + (p1 + q1))
    return positive, total, (m1, g2, g3, m4)


def weno_tile(field, ratio, cotangent, faces, cells, owned):
    edge_of, edge_bar, cell_bar, ratio_bar = {}, {}, {}, {}

    def edge(x):
        if x not in edge_of:
            edge_of[x] = field(x + 1) - field(x)
        return edge_of[x]

    def add(store, key, value, less=False):
        if key in store:
            store[key] = store[key] - value if less else store[key] + value
        else:
            store[key] = -value if less else value

    for f in faces:
        c, e = ratio(f), cotangent(f)
        positive, total, (m1, g2, g3, m4) = face_terms([edge(f - 3 + k) for k in range(5)], c)
        gain = (2.0 / 3.0) * (jnp.abs(c) * e)
        m1, g2, g3, m4 = gain * m1, gain * g2, gain * g3, gain * m4
        zero = jnp.zeros_like(m1)
        add(edge_bar, f - 3, jnp.where(positive, m1, zero), True)
        add(edge_bar, f - 2, jnp.where(positive, g2, -m4))
        add(edge_bar, f - 1, g3)
        add(edge_bar, f, jnp.where(positive, -m4, g2))
        add(edge_bar, f + 1, jnp.where(positive, zero, m1), True)
        add(cell_bar, f - 1, jnp.maximum(c, 0.0) * e)
        add(cell_bar, f, jnp.minimum(c, 0.0) * e)
        if f in owned:
            center = jnp.where(positive, field(f - 1), field(f))
            sixth = total * (1.0 / 6.0)
            ratio_bar[f] = e * (center + jnp.where(positive, sixth, -sixth))
    bars = {}
    for x in cells:
        parts = []
        if x - 1 in edge_bar:
            parts.append(edge_bar[x - 1])
        if x in edge_bar:
            parts.append(-edge_bar[x])
        if x in cell_bar:
            parts.append(cell_bar[x])
        bars[x] = sum(parts[1:], parts[0])
    return bars, ratio_bar


def planes(own, before, after, own_count, before_at, before_count, after_at, lanes):
    def read(x):
        if x < 0:
            return before[before_at + before_count + x, :, lanes]
        if x >= own_count:
            return after[after_at + x - own_count, :, lanes]
        return own[x, :, lanes]

    return read


def tracer_kernel(t, s, c, lt, ls, before, after, t_out, s_out, c_out, left_out, right_out):
    n, _, width = t.shape

    def tile(l, carry):
        lanes = pl.ds(pl.multiple_of(l * LANES, LANES), LANES)
        sums = {}
        for k, (own, dual, out) in enumerate(((t, lt, t_out), (s, ls, s_out))):
            field = planes(own, before, after, n, 3 * k, 3, 2 * k, lanes)
            lam = planes(dual, before, after, n, 6 + k, 1, 0, lanes)
            bars, ratio_bar = weno_tile(
                field,
                lambda f: c[f, :, lanes],
                lambda f: lam(f) - lam(f - 1),
                range(n),
                range(-3, n + 2),
                range(n),
            )
            for x in range(n):
                out[x, :, lanes] = dual[x, :, lanes] + bars[x]
                sums[x] = sums[x] + ratio_bar[x] if x in sums else ratio_bar[x]
            for x in range(3):
                left_out[3 * k + x, :, lanes] = bars[x - 3]
            for x in range(2):
                right_out[2 * k + x, :, lanes] = bars[n + x]
        for x in range(n):
            c_out[x, :, lanes] = sums[x]
        return carry

    lax.fori_loop(0, width // LANES, tile, 0)


def flow_kernel(
    u, c, df, before, after, phi, phi_edge, t_in, s_in, c_in, from_left, from_right,
    t_out, s_out, u_out, c_out,
):
    n, _, width = u.shape

    def tile(l, carry):
        lanes = pl.ds(pl.multiple_of(l * LANES, LANES), LANES)
        field = planes(u, before, after, n, 0, 5, 0, lanes)
        ratio = planes(c, before, after, n, 5, 2, 5, lanes)
        dual = planes(df, before, after, n, 7, 3, 8, lanes)
        head = planes(phi, phi_edge, phi_edge, n, 0, 3, 3, lanes)
        step = {x: head(x) - head(x - 1) for x in range(-2, n + 2)}

        def bend(x):
            if x == -3:
                return phi_edge[5, :, lanes]
            if x == n + 1:
                return phi_edge[6, :, lanes]
            return step[x] - step[x + 1]

        bars, ratio_bar = weno_tile(
            field,
            ratio,
            lambda f: (dual(f) - dual(f - 1)) + bend(f - 1),
            range(-2, n + 3),
            range(n),
            range(n),
        )
        for x in range(n):
            u_out[x, :, lanes] = (df[x, :, lanes] - step[x]) + bars[x]
            c_out[x, :, lanes] = c_in[x, :, lanes] + ratio_bar[x]
        for k, (base, out) in enumerate(((t_in, t_out), (s_in, s_out))):
            for x in range(n):
                value = base[x, :, lanes]
                if x < 2:
                    value = value + from_left[2 * k + x, :, lanes]
                if x >= n - 3:
                    value = value + from_right[3 * k + x - (n - 3), :, lanes]
                out[x, :, lanes] = value
        return carry

    lax.fori_loop(0, width // LANES, tile, 0)


def moments_kernel(rows, blocks, head, table_hi, table_lo, depth, rates, waves, u, c, df, spec, coeff, sums, decay, flow_right, flow_left, sems):
    n, levels, columns = head.shape
    width = columns // blocks
    copies = [
        pltpu.make_async_copy(source, target, sems.at[k])
        for k, (source, target) in enumerate(
            (
                (u.at[n - 5 : n], flow_right.at[0:5]),
                (c.at[n - 2 : n], flow_right.at[5:7]),
                (df.at[n - 3 : n], flow_right.at[7:10]),
                (u.at[0:5], flow_left.at[0:5]),
                (c.at[0:3], flow_left.at[5:8]),
                (df.at[0:3], flow_left.at[8:11]),
            )
        )
    ]
    for copy in copies:
        copy.start()
    a = jnp.transpose(jnp.broadcast_to(rates[...], (columns, rates.shape[1]))) + waves[...]
    root = jnp.sqrt(a * (1.0 + 0.25 * a))
    rho = 1.0 / ((1.0 + 0.5 * a) + root)
    coeff[0] = rho
    coeff[1] = 0.5 / root
    coeff[2] = a
    values = head[...].reshape(n * levels, columns)
    values = split_dot(halves(values), (table_hi[...], table_lo[...]))
    spec[...] = values.reshape(n, levels, columns)
    first = lax.axis_index("gz") == 0
    share = jnp.where(first, depth[:, :levels], depth[:, levels:])
    share = thrice_left(halves(share * (-1.0 / columns)))
    for j in range(n):
        part = jnp.dot(share, thrice_right(halves(spec[j])), preferred_element_type=f32)
        if j == 0:
            forward, backward, power = part, part, coeff[0]
        else:
            forward = forward * coeff[0] + part
            backward = backward + power * part
            power = power * coeff[0]
    for i in range(sums.shape[0]):
        m, r = i // blocks * rows, i % blocks * width
        sums[i, 0] = forward[m : m + rows, r : r + width]
        sums[i, 1] = backward[m : m + rows, r : r + width]
    m, r = my_chunk(rows, blocks, width)
    decay[...] = repeated(coeff[0, m, r], n)
    for copy in copies:
        copy.wait()


def pack_kernel(head, t, s, lt, ls, right, left, sems):
    n = head.shape[0]
    copies = [
        pltpu.make_async_copy(source, target, sems.at[k])
        for k, (source, target) in enumerate(
            (
                (t.at[n - 3 : n], right.at[0:3]),
                (s.at[n - 3 : n], right.at[3:6]),
                (lt.at[n - 1 : n], right.at[6:7]),
                (ls.at[n - 1 : n], right.at[7:8]),
                (head.at[n - 3 : n], right.at[8:11]),
                (t.at[0:2], left.at[0:2]),
                (s.at[0:2], left.at[2:4]),
                (head.at[0:2], left.at[4:6]),
            )
        )
    ]
    for copy in copies:
        copy.start()
    for copy in copies:
        copy.wait()


def halo_kernel(before, after, table_hi, table_lo, spec, planes, sems):
    copies = [
        pltpu.make_async_copy(before.at[8:11], planes.at[0:3], sems.at[0]),
        pltpu.make_async_copy(after.at[4:6], planes.at[3:5], sems.at[1]),
    ]
    for copy in copies:
        copy.start()
    for copy in copies:
        copy.wait()
    count, levels, columns = planes.shape
    value = planes[...].reshape(count * levels, columns)
    spec[...] = split_dot(halves(value), (table_hi[...], table_lo[...])).reshape(planes.shape)


def my_chunk(rows, blocks, width):
    n = lax.axis_index("yh")
    for name in GROUP_ALL[1:]:
        n = n * lax.axis_size(name) + lax.axis_index(name)
    m = pl.multiple_of(n // blocks * rows, rows)
    r = pl.multiple_of(n % blocks * width, width)
    return pl.ds(m, rows), pl.ds(r, width)


def repeated(value, times):
    result, power = None, value
    while times:
        if times & 1:
            result = power if result is None else result * power
        power, times = power * power, times >> 1
    return result


def group_kernel(got, decay, out):
    decay = decay[...]
    places, rings = got.shape[0], out.shape[0]
    forward, backward = None, None
    for p in range(places):
        a, b = got[p, 0, 0] + got[p, 1, 0], got[places - 1 - p, 0, 1] + got[places - 1 - p, 1, 1]
        forward = a if forward is None else forward * decay + a
        backward = b if backward is None else backward * decay + b
    mine = lax.axis_index("z")
    factor = repeated(decay, places)
    for k in range(rings):
        out[lax.rem(mine + 1 + k, rings), 0] = forward
        out[lax.rem(mine + 2 * rings - 1 - k, rings), 1] = backward
        forward, backward = forward * factor, backward * factor


def carry_kernel(got, rings, decay, out):
    decay = decay[...]
    places, around = got.shape[0], rings.shape[0]
    closing = 1.0 / (1.0 - repeated(decay, places * around))
    left, right = rings[0, 0], rings[0, 1]
    for k in range(1, around):
        left, right = left + rings[k, 0], right + rings[k, 1]
    left, right = left * closing, right * closing
    for p in range(places):
        q = places - 1 - p
        for g in range(2):
            out[p, g, 0] = left
            out[q, g, 1] = right
        left = left * decay + (got[p, 0, 0] + got[p, 1, 0])
        right = right * decay + (got[q, 0, 1] + got[q, 1, 1])


def source_kernel(own_at, edge_at, own_other_at, edge_other_at, depth_at, out_at, own, edge, own_other, edge_other, depth, out, sems):
    pairs = (
        (depth_at, depth),
        (own_at, own),
        (own_other_at, own_other),
        (edge_at, edge),
        (edge_other_at, edge_other),
    )
    copies = [pltpu.make_async_copy(p, q, sems.at[k]) for k, (p, q) in enumerate(pairs)]
    for copy in copies:
        copy.start()
    half = own.shape[1]
    n = own.shape[0]
    copies[0].wait()
    first = lax.axis_index("gz") == 0
    matrix = depth[...] * (-1.0 / own.shape[2])
    here = jnp.where(first, matrix[:, :half], matrix[:, half:])
    there = jnp.where(first, matrix[:, half:], matrix[:, :half])
    matrix = stacked_left(halves(jnp.concatenate([here, there], axis=1)))

    def product(mine, other):
        return stacked_dot(matrix, halves(jnp.concatenate([mine, other], axis=0)))

    copies[1].wait()
    copies[2].wait()
    for j in range(n):
        out[3 + j] = product(own[j], own_other[j])
    copies.append(pltpu.make_async_copy(out.at[3 : 3 + n], out_at.at[3 : 3 + n], sems.at[5]))
    copies[5].start()
    copies[3].wait()
    copies[4].wait()
    for j in range(5):
        out[j if j < 3 else j + n] = product(edge[j], edge_other[j])
    for k, (first, count) in enumerate(((0, 3), (3 + n, 2))):
        part = pl.ds(first, count)
        copies.append(pltpu.make_async_copy(out.at[part], out_at.at[part], sems.at[6 + k]))
        copies[6 + k].start()
    for copy in copies[5:]:
        copy.wait()


def solve_kernel(rows, blocks, source_at, carries_at, coeff_at, basis_at, hi_at, lo_at, phi, phi_edge, solved, levels_hi, levels_lo, source, carries, coeff, basis, table_hi, table_lo, heads, sems):
    pairs = (
        (carries_at, carries),
        (coeff_at, coeff),
        (source_at, source),
        (basis_at, basis),
        (hi_at, table_hi),
        (lo_at, table_lo),
    )
    copies = [pltpu.make_async_copy(p, q, sems.at[k]) for k, (p, q) in enumerate(pairs)]
    for copy in copies:
        copy.start()
    for copy in copies[:3]:
        copy.wait()
    count = source.shape[0]
    n = count - 5
    columns = source.shape[2]
    width = columns // blocks
    half = basis.shape[0] // 2

    def chunk(i, carry):
        m = pl.ds(pl.multiple_of(i // blocks * rows, rows), rows)
        r = pl.ds(pl.multiple_of(i % blocks * width, width), width)
        rho, kappa, a = coeff[0, m, r], coeff[1, m, r], coeff[2, m, r]
        growth = (2.0 + a) - rho
        f = [source[j, m, r] for j in range(count)]
        c, b = [None] * count, [None] * count
        c[2] = carries[i, 0]
        c[1] = (c[2] - f[2]) * growth
        c[0] = (c[1] - f[1]) * growth
        for j in range(3, count):
            c[j] = f[j] + rho * c[j - 1]
        b[n + 3] = carries[i, 1]
        b[n + 4] = (b[n + 3] - f[n + 3]) * growth
        for j in range(n + 2, -1, -1):
            b[j] = f[j] + rho * b[j + 1]
        values = [kappa * ((c[j] - f[j]) + b[j]) for j in range(count)]
        values.append(f[0] - a * values[0])
        values.append(f[count - 1] - a * values[count - 1])
        for j, value in enumerate(values):
            solved[j, m, r] = value
        return carry

    lax.fori_loop(0, carries.shape[0], chunk, 0)
    for copy in copies[3:]:
        copy.wait()
    first = lax.axis_index("gz") == 0
    share = stacked_left(halves(jnp.where(first, basis[:half, :], basis[half:, :])))

    def plane(j, carry):
        value = stacked_dot(share, halves(solved[j]))
        here = pl.ds(pl.multiple_of(j * half, half), half)
        levels_hi[here, :], levels_lo[here, :] = halves(value)
        return carry

    lax.fori_loop(0, count + 2, plane, 0)
    result = split_dot((levels_hi[...], levels_lo[...]), (table_hi[...], table_lo[...]))
    heads[...] = result.reshape(count + 2, half, columns)
    pairs = (
        (heads.at[3 : 3 + n], phi),
        (heads.at[0:3], phi_edge.at[0:3]),
        (heads.at[3 + n : count + 2], phi_edge.at[3:7]),
    )
    copies = [pltpu.make_async_copy(p, q, sems.at[6 + k]) for k, (p, q) in enumerate(pairs)]
    for copy in copies:
        copy.start()
    for copy in copies:
        copy.wait()


AWAY = pl.BlockSpec(memory_space=pltpu.HBM)


def params():
    return pltpu.CompilerParams(vmem_limit_bytes=63 * 1024 * 1024)


def cost(us):
    return pl.CostEstimate(flops=int(us * 1e6), bytes_accessed=int(us * 3e6), transcendentals=0)


def call(kernel, outs, *args, scratch=(), us=2.0, name, away=(), out_away=()):
    many = isinstance(outs, (list, tuple))

    def whole(a):
        return pl.BlockSpec(a.shape, lambda i: (0,) * len(a.shape), pipeline_mode=pl.Buffered(1))

    return pl.pallas_call(
        kernel,
        grid=(1,),
        out_shape=outs,
        in_specs=[AWAY if k in away else whole(a) for k, a in enumerate(args)],
        out_specs=[AWAY if k in out_away else whole(a) for k, a in enumerate(outs)]
        if many
        else whole(outs),
        scratch_shapes=list(scratch),
        compiler_params=params(),
        cost_estimate=cost(us),
        name=name,
    )(*args)


def near(kernel, outs, *args, us, name, scratch=(), away=(), out_away=(), limit=48):
    where = pl.BlockSpec(memory_space=pltpu.VMEM)
    return pl.pallas_call(
        kernel,
        out_shape=outs,
        in_specs=[AWAY if k in away else where for k in range(len(args))],
        out_specs=[AWAY if k in out_away else where for k in range(len(outs))]
        if isinstance(outs, list)
        else where,
        scratch_shapes=list(scratch),
        compiler_params=pltpu.CompilerParams(vmem_limit_bytes=limit * 1024 * 1024),
        cost_estimate=cost(us),
        name=name,
    )(*args)


def by_rows(kernel, outs, *args, us, name, counts={}):
    levels, columns = args[0].shape[1:]

    def spec(a, count=None):
        return pl.BlockSpec((count or a.shape[0], ROWS, columns), lambda i: (0, i, 0))

    return pl.pallas_call(
        kernel,
        grid=(levels // ROWS,),
        out_shape=outs,
        in_specs=[spec(a, counts.get(k)) for k, a in enumerate(args)],
        out_specs=[spec(o) for o in outs],
        compiler_params=params(),
        cost_estimate=cost(us),
        name=name,
    )(*args)


def shards(
    thermal_anomaly,
    saltiness_anomaly,
    eastward_flow,
    advective_ratio,
    dual_thermal_final,
    dual_saltiness_final,
    dual_flow_final,
    dual_kinematic_head,
    depth_into_eigenbasis,
    eigenbasis_into_depth,
    spectral_magnitudes,
):
    t, s, u, c, lt, ls, df, head = (
        jnp.transpose(a, (1, 0, 2))
        for a in (
            thermal_anomaly,
            saltiness_anomaly,
            eastward_flow,
            advective_ratio,
            dual_thermal_final,
            dual_saltiness_final,
            dual_flow_final,
            dual_kinematic_head,
        )
    )
    n, levels, columns = t.shape
    modes = depth_into_eigenbasis.shape[0]
    across = lax.axis_size(ALONG)
    places = lax.axis_size(GROUP)
    rings = lax.axis_size("z")
    chunks = places * lax.axis_size("gz")
    rows = max(ROWS, modes // chunks)
    blocks = chunks * rows // modes
    width = columns // blocks

    def to_right(block):
        return lax.ppermute(block, ALONG, [(i, (i + 1) % across) for i in range(across)])

    def to_left(block):
        return lax.ppermute(block, ALONG, [((i + 1) % across, i) for i in range(across)])

    def other_half(block):
        return lax.ppermute(block, "gz", [(0, 1), (1, 0)])

    def like(*shape):
        return jax.ShapeDtypeStruct(shape, f32)

    exact = hartley_table(columns)
    upper = exact.astype(np.float32).astype(jnp.bfloat16)
    table_hi = jnp.asarray(upper)
    table_lo = jnp.asarray((exact - upper.astype(np.float64)).astype(jnp.bfloat16))
    waves = jnp.asarray(
        (2.0 - 2.0 * np.cos(np.arange(columns) * (2.0 * math.pi / columns))).astype(np.float32)
    ).reshape(1, columns)

    right, left = call(
        pack_kernel,
        [like(11, levels, columns), like(6, levels, columns)],
        head, t, s, lt, ls,
        scratch=[pltpu.SemaphoreType.DMA((8,))],
        away=range(5),
        us=2.0,
        name="pack",
    )
    before, after = to_right(right), to_left(left)

    spec, coeff, sums, decay, flow_right, flow_left = call(
        lambda *refs: moments_kernel(rows, blocks, *refs),
        [
            like(n, levels, columns),
            like(3, modes, columns),
            like(chunks, 2, rows, width),
            like(rows, width),
            like(10, levels, columns),
            like(11, levels, columns),
        ],
        head, table_hi, table_lo, depth_into_eigenbasis,
        spectral_magnitudes.reshape(1, modes), waves, u, c, df,
        scratch=[pltpu.SemaphoreType.DMA((6,))],
        away=(6, 7, 8),
        us=5.0,
        name="block_moments",
    )
    gathered = lax.all_to_all(sums, GROUP_ALL, 0, 0, tiled=True)
    t_base, s_base, c_base, to_left_part, to_right_part = by_rows(
        tracer_kernel,
        [like(n, levels, columns)] * 3 + [like(6, levels, columns), like(4, levels, columns)],
        t, s, c, lt, ls, before, after,
        us=9.0,
        name="tracers",
        counts={5: 8, 6: 4},
    )
    spec_other = other_half(spec)
    gathered, t_base, spec_other = lax.optimization_barrier((gathered, t_base, spec_other))
    gathered = gathered.reshape(places, chunks // places, 2, rows, width)
    edge = call(
        halo_kernel,
        like(5, levels, columns),
        before, after, table_hi, table_lo,
        scratch=[pltpu.VMEM((5, levels, columns), f32), pltpu.SemaphoreType.DMA((2,))],
        away=(0, 1),
        us=2.0,
        name="edge_spectrum",
    )
    edge_other = other_half(edge)

    ring = near(
        group_kernel,
        like(rings, 2, rows, width),
        gathered, decay,
        us=1.0,
        name="group_moments",
    )
    ring, flow_right, flow_left = lax.optimization_barrier((ring, flow_right, flow_left))
    ring = lax.all_to_all(ring, "z", 0, 0, tiled=True)
    flow_before, flow_after = to_right(flow_right), to_left(flow_left)
    carries = near(
        carry_kernel,
        like(places, chunks // places, 2, rows, width),
        gathered, ring, decay,
        us=1.0,
        name="group_carries",
    )
    carries = lax.all_to_all(carries.reshape(chunks, 2, rows, width), GROUP_ALL, 0, 0, tiled=True)
    from_right = to_left(to_left_part)
    from_left = to_right(to_right_part)

    (source,) = near(
        source_kernel,
        [like(n + 5, modes, columns)],
        spec, edge, spec_other, edge_other, depth_into_eigenbasis,
        scratch=[
            pltpu.VMEM((n, levels, columns), f32),
            pltpu.VMEM((5, levels, columns), f32),
            pltpu.VMEM((n, levels, columns), f32),
            pltpu.VMEM((5, levels, columns), f32),
            pltpu.VMEM((modes, modes), f32),
            pltpu.VMEM((n + 5, modes, columns), f32),
            pltpu.SemaphoreType.DMA((8,)),
        ],
        away=range(5),
        out_away=(0,),
        us=4.0,
        limit=63,
        name="mode_source",
    )
    phi, phi_edge = near(
        lambda *refs: solve_kernel(rows, blocks, *refs),
        [like(n, levels, columns), like(7, levels, columns)],
        source, carries, coeff, eigenbasis_into_depth, table_hi, table_lo,
        scratch=[pltpu.VMEM((n + 7, modes, columns), f32)]
        + [pltpu.VMEM(((n + 7) * levels, columns), bf16)] * 2
        + [
            pltpu.VMEM((n + 5, modes, columns), f32),
            pltpu.VMEM((chunks, 2, rows, width), f32),
            pltpu.VMEM((3, modes, columns), f32),
            pltpu.VMEM((modes, modes), f32),
            pltpu.VMEM((columns, columns), bf16),
            pltpu.VMEM((columns, columns), bf16),
            pltpu.VMEM((n + 7, levels, columns), f32),
            pltpu.SemaphoreType.DMA((9,)),
        ],
        away=range(6),
        out_away=(0, 1),
        us=7.0,
        limit=63,
        name="pressure",
    )
    t_bar, s_bar, u_bar, c_bar = by_rows(
        flow_kernel,
        [like(n, levels, columns)] * 4,
        u, c, df, flow_before, flow_after, phi, phi_edge,
        t_base, s_base, c_base, from_left, from_right,
        us=7.0,
        name="flow",
    )
    return tuple(jnp.transpose(a, (1, 0, 2)) for a in (t_bar, s_bar, u_bar, c_bar, phi))


def solution(mesh):
    gx, gz = mesh.shape["gx"], mesh.shape["gz"]
    inner = Mesh(mesh.devices.reshape(SPLIT[gx] + (gz,)), ALONG + ("gz",))
    field = P("gz", ALONG, None)
    return jax.shard_map(
        shards,
        mesh=inner,
        in_specs=(field,) * 8 + (P(),) * 3,
        out_specs=(field,) * 5,
        check_vma=False,
    )
```

```python
import math

import jax
import jax.numpy as jnp
import numpy as np
from jax import lax
from jax.experimental import pallas as pl
from jax.experimental.pallas import tpu as pltpu
from jax.sharding import Mesh, PartitionSpec as P

f32 = jnp.float32
bf16 = jnp.bfloat16
LANES = 128
ROWS = 8
SPLIT = {128: (8, 2, 4, 2)}
ALONG = ("z", "yh", "x", "c")
GROUP = ("yh", "x", "c")
GROUP_ALL = ("yh", "x", "c", "gz")


def hartley_table(length):
    numbers = np.arange(length)
    angle = (numbers[:, None] * numbers[None, :] % length) * (2.0 * math.pi / length)
    return np.cos(angle) + np.sin(angle)


def halves(value):
    upper = value.astype(bf16)
    return upper, (value - upper.astype(f32)).astype(bf16)


def stacked_left(pair):
    upper = jnp.concatenate([pair[0], pair[0]], axis=1)
    lower = jnp.concatenate([pair[1], jnp.zeros_like(pair[1])], axis=1)
    return jnp.concatenate([upper, lower], axis=0)


def stacked_dot(left, pair):
    both = jnp.dot(left, jnp.concatenate(pair, axis=0), preferred_element_type=f32)
    half = both.shape[0] // 2
    return both[:half] + both[half:]


def thrice_left(pair):
    return jnp.concatenate([pair[0], pair[0], pair[1]], axis=1)


def thrice_right(pair):
    return jnp.concatenate([pair[0], pair[1], pair[0]], axis=0)


def split_dot(a, b):
    (a_hi, a_lo), (b_hi, b_lo) = a, b

    def dot(p, q):
        return jnp.dot(p, q, preferred_element_type=f32)

    return dot(a_hi, b_hi) + (dot(a_hi, b_lo) + dot(a_lo, b_hi))


def face_terms(edges, ratio, side=None):
    positive = ratio >= 0.0
    if side == "left":
        d1, d2, d3, d4 = edges[0], edges[1], edges[2], edges[3]
    elif side == "right":
        d1, d2, d3, d4 = edges[4], edges[3], edges[2], edges[1]
    else:
        d1 = jnp.where(positive, edges[0], edges[4])
        d2 = jnp.where(positive, edges[1], edges[3])
        d3 = edges[2]
        d4 = jnp.where(positive, edges[3], edges[1])
    s1, s2, s3 = d2 - d1, d3 - d2, d4 - d3
    e0, e1, e2 = (d2 + d2) + s1, d2 + d3, (d3 + d3) - s3
    t0, t1, t2 = (13.0 / 3.0) * s1, (13.0 / 3.0) * s2, (13.0 / 3.0) * s3
    r0 = 1.0 / (t0 * s1 + (e0 * e0 + 0.04))
    r1 = 1.0 / (t1 * s2 + (e1 * e1 + 0.04))
    r2 = 1.0 / (t2 * s3 + (e2 * e2 + 0.04))
    u0, u1, u2 = (1.0 / 6.0) * (r0 * r0), r1 * r1, 0.5 * (r2 * r2)
    norm = 1.0 / (u0 + u1 + u2)
    w0, w1, w2 = u0 * norm, u1 * norm, u2 * norm
    bend = s1 - s2
    a2, cc = bend + bend, s2 - s3
    z = w0 * a2 + w2 * cc
    total = (e1 + d3) + z
    n0, n1, n2 = w0 * r0 * (z - a2), w1 * r1 * z, w2 * r2 * (z - cc)
    p0, q0 = n0 * t0, n0 * e0
    p1, q1 = n1 * t1, n1 * e1
    p2, q2 = n2 * t2, n2 * e2
    h0, h2 = 0.5 * w0, 0.25 * w2
    lean = h0 - h2
    m1, m4 = h0 + (p0 + q0), h2 + (q2 - p2)
    g2 = ((0.25 + lean) + m1) + ((q0 + q0) + (q1 - p1))
    g3 = ((0.5 - lean) + m4) + ((q2 + q2) + (p1 + q1))
    return positive, total, (m1, g2, g3, m4)


def weno_tile(field, ratio, cotangent, faces, cells, owned, ends=()):
    edge_of, edge_bar, cell_bar, ratio_bar = {}, {}, {}, {}

    def edge(x):
        if x not in edge_of:
            edge_of[x] = field(x + 1) - field(x)
        return edge_of[x]

    def add(store, key, value, less=False):
        if key in store:
            store[key] = store[key] - value if less else store[key] + value
        else:
            store[key] = -value if less else value

    for f in faces:
        c, e = ratio(f), cotangent(f)
        side = ("right" if f == ends[0] else "left" if f == ends[1] else None) if ends else None
        skip = {"right": 0, "left": 4}.get(side)
        five = [None if k == skip else edge(f - 3 + k) for k in range(5)]
        positive, total, (m1, g2, g3, m4) = face_terms(five, c, side)
        gain = (2.0 / 3.0) * (jnp.abs(c) * e)
        m1, g2, g3, m4 = gain * m1, gain * g2, gain * g3, gain * m4
        zero = jnp.zeros_like(m1)
        add(edge_bar, f - 3, jnp.where(positive, m1, zero), True)
        add(edge_bar, f - 2, jnp.where(positive, g2, -m4))
        add(edge_bar, f - 1, g3)
        add(edge_bar, f, jnp.where(positive, -m4, g2))
        add(edge_bar, f + 1, jnp.where(positive, zero, m1), True)
        add(cell_bar, f - 1, jnp.maximum(c, 0.0) * e)
        add(cell_bar, f, jnp.minimum(c, 0.0) * e)
        if f in owned:
            center = jnp.where(positive, field(f - 1), field(f))
            sixth = total * (1.0 / 6.0)
            ratio_bar[f] = e * (center + jnp.where(positive, sixth, -sixth))
    bars = {}
    for x in cells:
        parts = []
        if x - 1 in edge_bar:
            parts.append(edge_bar[x - 1])
        if x in edge_bar:
            parts.append(-edge_bar[x])
        if x in cell_bar:
            parts.append(cell_bar[x])
        bars[x] = sum(parts[1:], parts[0])
    return bars, ratio_bar


def planes(own, before, after, own_count, before_at, before_count, after_at, lanes):
    def read(x):
        if x < 0:
            return before[before_at + before_count + x, :, lanes]
        if x >= own_count:
            return after[after_at + x - own_count, :, lanes]
        return own[x, :, lanes]

    return read


def tracer_kernel(t, s, c, lt, ls, before, after, t_out, s_out, c_out, left_out, right_out):
    n, _, width = t.shape

    def tile(l, carry):
        lanes = pl.ds(pl.multiple_of(l * LANES, LANES), LANES)
        sums = {}
        for k, (own, dual, out) in enumerate(((t, lt, t_out), (s, ls, s_out))):
            field = planes(own, before, after, n, 3 * k, 3, 2 * k, lanes)
            lam = planes(dual, before, after, n, 6 + k, 1, 0, lanes)
            bars, ratio_bar = weno_tile(
                field,
                lambda f: c[f, :, lanes],
                lambda f: lam(f) - lam(f - 1),
                range(n),
                range(-3, n + 2),
                range(n),
            )
            for x in range(n):
                out[x, :, lanes] = dual[x, :, lanes] + bars[x]
                sums[x] = sums[x] + ratio_bar[x] if x in sums else ratio_bar[x]
            for x in range(3):
                left_out[3 * k + x, :, lanes] = bars[x - 3]
            for x in range(2):
                right_out[2 * k + x, :, lanes] = bars[n + x]
        for x in range(n):
            c_out[x, :, lanes] = sums[x]
        return carry

    lax.fori_loop(0, width // LANES, tile, 0)


def flow_kernel(
    u, c, df, before, after, phi, phi_edge, t_in, s_in, c_in, from_left, from_right,
    t_out, s_out, u_out, c_out,
):
    n, _, width = u.shape

    def tile(l, carry):
        lanes = pl.ds(pl.multiple_of(l * LANES, LANES), LANES)
        field = planes(u, before, after, n, 0, 4, 0, lanes)
        ratio = planes(c, before, after, n, 4, 2, 4, lanes)
        dual = planes(df, before, after, n, 6, 3, 7, lanes)
        head = planes(phi, phi_edge, phi_edge, n, 0, 3, 3, lanes)
        step = {x: head(x) - head(x - 1) for x in range(-2, n + 2)}

        def bend(x):
            if x == -3:
                return phi_edge[5, :, lanes]
            if x == n + 1:
                return phi_edge[6, :, lanes]
            return step[x] - step[x + 1]

        bars, ratio_bar = weno_tile(
            field,
            ratio,
            lambda f: (dual(f) - dual(f - 1)) + bend(f - 1),
            range(-2, n + 3),
            range(n),
            range(n),
            (-2, n + 2),
        )
        for x in range(n):
            u_out[x, :, lanes] = (df[x, :, lanes] - step[x]) + bars[x]
            c_out[x, :, lanes] = c_in[x, :, lanes] + ratio_bar[x]
        for k, (base, out) in enumerate(((t_in, t_out), (s_in, s_out))):
            for x in range(n):
                value = base[x, :, lanes]
                if x < 2:
                    value = value + from_left[2 * k + x, :, lanes]
                if x >= n - 3:
                    value = value + from_right[3 * k + x - (n - 3), :, lanes]
                out[x, :, lanes] = value
        return carry

    lax.fori_loop(0, width // LANES, tile, 0)


def moments_kernel(rows, blocks, head, table_hi, table_lo, depth, rates, waves, u, c, df, spec, coeff, sums, decay, flow_right, flow_left, sems):
    n, levels, columns = head.shape
    width = columns // blocks
    copies = [
        pltpu.make_async_copy(source, target, sems.at[k])
        for k, (source, target) in enumerate(
            (
                (u.at[n - 4 : n], flow_right.at[0:4]),
                (c.at[n - 2 : n], flow_right.at[4:6]),
                (df.at[n - 3 : n], flow_right.at[6:9]),
                (u.at[0:4], flow_left.at[0:4]),
                (c.at[0:3], flow_left.at[4:7]),
                (df.at[0:3], flow_left.at[7:10]),
            )
        )
    ]
    for copy in copies:
        copy.start()
    a = jnp.transpose(jnp.broadcast_to(rates[...], (columns, rates.shape[1]))) + waves[...]
    root = jnp.sqrt(a * (1.0 + 0.25 * a))
    rho = 1.0 / ((1.0 + 0.5 * a) + root)
    coeff[0] = rho
    coeff[1] = 0.5 / root
    coeff[2] = a
    values = head[...].reshape(n * levels, columns)
    values = split_dot(halves(values), (table_hi[...], table_lo[...]))
    spec[...] = values.reshape(n, levels, columns)
    first = lax.axis_index("gz") == 0
    share = jnp.where(first, depth[:, :levels], depth[:, levels:])
    share = thrice_left(halves(share * (-1.0 / columns)))
    for j in range(n):
        part = jnp.dot(share, thrice_right(halves(spec[j])), preferred_element_type=f32)
        if j == 0:
            forward, backward, power = part, part, coeff[0]
        else:
            forward = forward * coeff[0] + part
            backward = backward + power * part
            power = power * coeff[0]
    for i in range(sums.shape[0]):
        m, r = i // blocks * rows, i % blocks * width
        sums[i, 0] = forward[m : m + rows, r : r + width]
        sums[i, 1] = backward[m : m + rows, r : r + width]
    m, r = my_chunk(rows, blocks, width)
    decay[...] = repeated(coeff[0, m, r], n)
    for copy in copies:
        copy.wait()


def pack_kernel(head, t, s, lt, ls, right, left, sems):
    n = head.shape[0]
    copies = [
        pltpu.make_async_copy(source, target, sems.at[k])
        for k, (source, target) in enumerate(
            (
                (t.at[n - 3 : n], right.at[0:3]),
                (s.at[n - 3 : n], right.at[3:6]),
                (lt.at[n - 1 : n], right.at[6:7]),
                (ls.at[n - 1 : n], right.at[7:8]),
                (head.at[n - 3 : n], right.at[8:11]),
                (t.at[0:2], left.at[0:2]),
                (s.at[0:2], left.at[2:4]),
                (head.at[0:2], left.at[4:6]),
            )
        )
    ]
    for copy in copies:
        copy.start()
    for copy in copies:
        copy.wait()


def halo_kernel(before, after, table_hi, table_lo, spec, planes, sems):
    copies = [
        pltpu.make_async_copy(before.at[8:11], planes.at[0:3], sems.at[0]),
        pltpu.make_async_copy(after.at[4:6], planes.at[3:5], sems.at[1]),
    ]
    for copy in copies:
        copy.start()
    for copy in copies:
        copy.wait()
    count, levels, columns = planes.shape
    value = planes[...].reshape(count * levels, columns)
    spec[...] = split_dot(halves(value), (table_hi[...], table_lo[...])).reshape(planes.shape)


def my_chunk(rows, blocks, width):
    n = lax.axis_index("yh")
    for name in GROUP_ALL[1:]:
        n = n * lax.axis_size(name) + lax.axis_index(name)
    m = pl.multiple_of(n // blocks * rows, rows)
    r = pl.multiple_of(n % blocks * width, width)
    return pl.ds(m, rows), pl.ds(r, width)


def repeated(value, times):
    result, power = None, value
    while times:
        if times & 1:
            result = power if result is None else result * power
        power, times = power * power, times >> 1
    return result


def group_kernel(got, decay, out):
    decay = decay[...]
    places, rings = got.shape[0], out.shape[0]
    forward, backward = None, None
    for p in range(places):
        a, b = got[p, 0, 0] + got[p, 1, 0], got[places - 1 - p, 0, 1] + got[places - 1 - p, 1, 1]
        forward = a if forward is None else forward * decay + a
        backward = b if backward is None else backward * decay + b
    mine = lax.axis_index("z")
    factor = repeated(decay, places)
    for k in range(rings):
        out[lax.rem(mine + 1 + k, rings), 0] = forward
        out[lax.rem(mine + 2 * rings - 1 - k, rings), 1] = backward
        forward, backward = forward * factor, backward * factor


def carry_kernel(got, rings, decay, out):
    decay = decay[...]
    places, around = got.shape[0], rings.shape[0]
    closing = 1.0 / (1.0 - repeated(decay, places * around))
    left, right = rings[0, 0], rings[0, 1]
    for k in range(1, around):
        left, right = left + rings[k, 0], right + rings[k, 1]
    left, right = left * closing, right * closing
    for p in range(places):
        q = places - 1 - p
        for g in range(2):
            out[p, g, 0] = left
            out[q, g, 1] = right
        left = left * decay + (got[p, 0, 0] + got[p, 1, 0])
        right = right * decay + (got[q, 0, 1] + got[q, 1, 1])


def source_kernel(own_at, edge_at, own_other_at, edge_other_at, depth_at, out_at, own, edge, own_other, edge_other, depth, out, sems):
    pairs = (
        (depth_at, depth),
        (own_at, own),
        (own_other_at, own_other),
        (edge_at, edge),
        (edge_other_at, edge_other),
    )
    copies = [pltpu.make_async_copy(p, q, sems.at[k]) for k, (p, q) in enumerate(pairs)]
    for copy in copies:
        copy.start()
    half = own.shape[1]
    n = own.shape[0]
    copies[0].wait()
    first = lax.axis_index("gz") == 0
    matrix = depth[...] * (-1.0 / own.shape[2])
    here = jnp.where(first, matrix[:, :half], matrix[:, half:])
    there = jnp.where(first, matrix[:, half:], matrix[:, :half])
    matrix = stacked_left(halves(jnp.concatenate([here, there], axis=1)))

    def product(mine, other):
        return stacked_dot(matrix, halves(jnp.concatenate([mine, other], axis=0)))

    copies[1].wait()
    copies[2].wait()
    for j in range(n):
        out[3 + j] = product(own[j], own_other[j])
    copies.append(pltpu.make_async_copy(out.at[3 : 3 + n], out_at.at[3 : 3 + n], sems.at[5]))
    copies[5].start()
    copies[3].wait()
    copies[4].wait()
    for j in range(5):
        out[j if j < 3 else j + n] = product(edge[j], edge_other[j])
    for k, (first, count) in enumerate(((0, 3), (3 + n, 2))):
        part = pl.ds(first, count)
        copies.append(pltpu.make_async_copy(out.at[part], out_at.at[part], sems.at[6 + k]))
        copies[6 + k].start()
    for copy in copies[5:]:
        copy.wait()


def solve_kernel(rows, blocks, source_at, carries_at, coeff_at, basis_at, hi_at, lo_at, phi, phi_edge, solved, levels_hi, levels_lo, source, carries, coeff, basis, table_hi, table_lo, heads, sems):
    pairs = (
        (carries_at, carries),
        (coeff_at, coeff),
        (source_at, source),
        (basis_at, basis),
        (hi_at, table_hi),
        (lo_at, table_lo),
    )
    copies = [pltpu.make_async_copy(p, q, sems.at[k]) for k, (p, q) in enumerate(pairs)]
    for copy in copies:
        copy.start()
    for copy in copies[:3]:
        copy.wait()
    count = source.shape[0]
    n = count - 5
    columns = source.shape[2]
    width = columns // blocks
    half = basis.shape[0] // 2

    def chunk(i, carry):
        m = pl.ds(pl.multiple_of(i // blocks * rows, rows), rows)
        r = pl.ds(pl.multiple_of(i % blocks * width, width), width)
        rho, kappa, a = coeff[0, m, r], coeff[1, m, r], coeff[2, m, r]
        growth = (2.0 + a) - rho
        f = [source[j, m, r] for j in range(count)]
        c, b = [None] * count, [None] * count
        c[2] = carries[i, 0]
        c[1] = (c[2] - f[2]) * growth
        c[0] = (c[1] - f[1]) * growth
        for j in range(3, count):
            c[j] = f[j] + rho * c[j - 1]
        b[n + 3] = carries[i, 1]
        b[n + 4] = (b[n + 3] - f[n + 3]) * growth
        for j in range(n + 2, -1, -1):
            b[j] = f[j] + rho * b[j + 1]
        values = [kappa * ((c[j] - f[j]) + b[j]) for j in range(count)]
        values.append(f[0] - a * values[0])
        values.append(f[count - 1] - a * values[count - 1])
        for j, value in enumerate(values):
            solved[j, m, r] = value
        return carry

    lax.fori_loop(0, carries.shape[0], chunk, 0)
    for copy in copies[3:]:
        copy.wait()
    first = lax.axis_index("gz") == 0
    share = stacked_left(halves(jnp.where(first, basis[:half, :], basis[half:, :])))

    def plane(j, carry):
        value = stacked_dot(share, halves(solved[j]))
        here = pl.ds(pl.multiple_of(j * half, half), half)
        levels_hi[here, :], levels_lo[here, :] = halves(value)
        return carry

    lax.fori_loop(0, count + 2, plane, 0)
    result = split_dot((levels_hi[...], levels_lo[...]), (table_hi[...], table_lo[...]))
    heads[...] = result.reshape(count + 2, half, columns)
    pairs = (
        (heads.at[3 : 3 + n], phi),
        (heads.at[0:3], phi_edge.at[0:3]),
        (heads.at[3 + n : count + 2], phi_edge.at[3:7]),
    )
    copies = [pltpu.make_async_copy(p, q, sems.at[6 + k]) for k, (p, q) in enumerate(pairs)]
    for copy in copies:
        copy.start()
    for copy in copies:
        copy.wait()


AWAY = pl.BlockSpec(memory_space=pltpu.HBM)


def params():
    return pltpu.CompilerParams(vmem_limit_bytes=63 * 1024 * 1024)


def cost(us):
    return pl.CostEstimate(flops=int(us * 1e6), bytes_accessed=int(us * 3e6), transcendentals=0)


def call(kernel, outs, *args, scratch=(), us=2.0, name, away=(), out_away=()):
    many = isinstance(outs, (list, tuple))

    def whole(a):
        return pl.BlockSpec(a.shape, lambda i: (0,) * len(a.shape), pipeline_mode=pl.Buffered(1))

    return pl.pallas_call(
        kernel,
        grid=(1,),
        out_shape=outs,
        in_specs=[AWAY if k in away else whole(a) for k, a in enumerate(args)],
        out_specs=[AWAY if k in out_away else whole(a) for k, a in enumerate(outs)]
        if many
        else whole(outs),
        scratch_shapes=list(scratch),
        compiler_params=params(),
        cost_estimate=cost(us),
        name=name,
    )(*args)


def near(kernel, outs, *args, us, name, scratch=(), away=(), out_away=(), limit=48):
    where = pl.BlockSpec(memory_space=pltpu.VMEM)
    return pl.pallas_call(
        kernel,
        out_shape=outs,
        in_specs=[AWAY if k in away else where for k in range(len(args))],
        out_specs=[AWAY if k in out_away else where for k in range(len(outs))]
        if isinstance(outs, list)
        else where,
        scratch_shapes=list(scratch),
        compiler_params=pltpu.CompilerParams(vmem_limit_bytes=limit * 1024 * 1024),
        cost_estimate=cost(us),
        name=name,
    )(*args)


def by_rows(kernel, outs, *args, us, name, counts={}):
    levels, columns = args[0].shape[1:]

    def spec(a, count=None):
        return pl.BlockSpec((count or a.shape[0], ROWS, columns), lambda i: (0, i, 0))

    return pl.pallas_call(
        kernel,
        grid=(levels // ROWS,),
        out_shape=outs,
        in_specs=[spec(a, counts.get(k)) for k, a in enumerate(args)],
        out_specs=[spec(o) for o in outs],
        compiler_params=params(),
        cost_estimate=cost(us),
        name=name,
    )(*args)


def shards(
    thermal_anomaly,
    saltiness_anomaly,
    eastward_flow,
    advective_ratio,
    dual_thermal_final,
    dual_saltiness_final,
    dual_flow_final,
    dual_kinematic_head,
    depth_into_eigenbasis,
    eigenbasis_into_depth,
    spectral_magnitudes,
):
    t, s, u, c, lt, ls, df, head = (
        jnp.transpose(a, (1, 0, 2))
        for a in (
            thermal_anomaly,
            saltiness_anomaly,
            eastward_flow,
            advective_ratio,
            dual_thermal_final,
            dual_saltiness_final,
            dual_flow_final,
            dual_kinematic_head,
        )
    )
    n, levels, columns = t.shape
    modes = depth_into_eigenbasis.shape[0]
    across = lax.axis_size(ALONG)
    places = lax.axis_size(GROUP)
    rings = lax.axis_size("z")
    chunks = places * lax.axis_size("gz")
    rows = max(ROWS, modes // chunks)
    blocks = chunks * rows // modes
    width = columns // blocks

    def to_right(block):
        return lax.ppermute(block, ALONG, [(i, (i + 1) % across) for i in range(across)])

    def to_left(block):
        return lax.ppermute(block, ALONG, [((i + 1) % across, i) for i in range(across)])

    def other_half(block):
        return lax.ppermute(block, "gz", [(0, 1), (1, 0)])

    def like(*shape):
        return jax.ShapeDtypeStruct(shape, f32)

    exact = hartley_table(columns)
    upper = exact.astype(np.float32).astype(jnp.bfloat16)
    table_hi = jnp.asarray(upper)
    table_lo = jnp.asarray((exact - upper.astype(np.float64)).astype(jnp.bfloat16))
    waves = jnp.asarray(
        (2.0 - 2.0 * np.cos(np.arange(columns) * (2.0 * math.pi / columns))).astype(np.float32)
    ).reshape(1, columns)

    right, left = call(
        pack_kernel,
        [like(11, levels, columns), like(6, levels, columns)],
        head, t, s, lt, ls,
        scratch=[pltpu.SemaphoreType.DMA((8,))],
        away=range(5),
        us=2.0,
        name="pack",
    )
    before, after = to_right(right), to_left(left)

    spec, coeff, sums, decay, flow_right, flow_left = call(
        lambda *refs: moments_kernel(rows, blocks, *refs),
        [
            like(n, levels, columns),
            like(3, modes, columns),
            like(chunks, 2, rows, width),
            like(rows, width),
            like(9, levels, columns),
            like(10, levels, columns),
        ],
        head, table_hi, table_lo, depth_into_eigenbasis,
        spectral_magnitudes.reshape(1, modes), waves, u, c, df,
        scratch=[pltpu.SemaphoreType.DMA((6,))],
        away=(6, 7, 8),
        us=5.0,
        name="block_moments",
    )
    gathered = lax.all_to_all(sums, GROUP_ALL, 0, 0, tiled=True)
    t_base, s_base, c_base, to_left_part, to_right_part = by_rows(
        tracer_kernel,
        [like(n, levels, columns)] * 3 + [like(6, levels, columns), like(4, levels, columns)],
        t, s, c, lt, ls, before, after,
        us=9.0,
        name="tracers",
        counts={5: 8, 6: 4},
    )
    gathered, t_base, late, edge_before, edge_after = lax.optimization_barrier(
        (gathered, t_base, spec, before, after)
    )
    spec_other = other_half(late)
    gathered = gathered.reshape(places, chunks // places, 2, rows, width)
    edge = call(
        halo_kernel,
        like(5, levels, columns),
        edge_before, edge_after, table_hi, table_lo,
        scratch=[pltpu.VMEM((5, levels, columns), f32), pltpu.SemaphoreType.DMA((2,))],
        away=(0, 1),
        us=2.0,
        name="edge_spectrum",
    )
    edge_other = other_half(edge)

    ring = near(
        group_kernel,
        like(rings, 2, rows, width),
        gathered, decay,
        us=1.0,
        name="group_moments",
    )
    ring, flow_right, flow_left = lax.optimization_barrier((ring, flow_right, flow_left))
    ring = lax.all_to_all(ring, "z", 0, 0, tiled=True)
    flow_before, flow_after = to_right(flow_right), to_left(flow_left)
    ring, spec_other = lax.optimization_barrier((ring, spec_other))
    carries = near(
        carry_kernel,
        like(places, chunks // places, 2, rows, width),
        gathered, ring, decay,
        us=1.0,
        name="group_carries",
    )
    carries = lax.all_to_all(carries.reshape(chunks, 2, rows, width), GROUP_ALL, 0, 0, tiled=True)
    from_right = to_left(to_left_part)
    from_left = to_right(to_right_part)

    (source,) = near(
        source_kernel,
        [like(n + 5, modes, columns)],
        spec, edge, spec_other, edge_other, depth_into_eigenbasis,
        scratch=[
            pltpu.VMEM((n, levels, columns), f32),
            pltpu.VMEM((5, levels, columns), f32),
            pltpu.VMEM((n, levels, columns), f32),
            pltpu.VMEM((5, levels, columns), f32),
            pltpu.VMEM((modes, modes), f32),
            pltpu.VMEM((n + 5, modes, columns), f32),
            pltpu.SemaphoreType.DMA((8,)),
        ],
        away=range(5),
        out_away=(0,),
        us=4.0,
        limit=63,
        name="mode_source",
    )
    phi, phi_edge = near(
        lambda *refs: solve_kernel(rows, blocks, *refs),
        [like(n, levels, columns), like(7, levels, columns)],
        source, carries, coeff, eigenbasis_into_depth, table_hi, table_lo,
        scratch=[pltpu.VMEM((n + 7, modes, columns), f32)]
        + [pltpu.VMEM(((n + 7) * levels, columns), bf16)] * 2
        + [
            pltpu.VMEM((n + 5, modes, columns), f32),
            pltpu.VMEM((chunks, 2, rows, width), f32),
            pltpu.VMEM((3, modes, columns), f32),
            pltpu.VMEM((modes, modes), f32),
            pltpu.VMEM((columns, columns), bf16),
            pltpu.VMEM((columns, columns), bf16),
            pltpu.VMEM((n + 7, levels, columns), f32),
            pltpu.SemaphoreType.DMA((9,)),
        ],
        away=range(6),
        out_away=(0, 1),
        us=7.0,
        limit=63,
        name="pressure",
    )
    t_bar, s_bar, u_bar, c_bar = by_rows(
        flow_kernel,
        [like(n, levels, columns)] * 4,
        u, c, df, flow_before, flow_after, phi, phi_edge,
        t_base, s_base, c_base, from_left, from_right,
        us=7.0,
        name="flow",
    )
    return tuple(jnp.transpose(a, (1, 0, 2)) for a in (t_bar, s_bar, u_bar, c_bar, phi))


def solution(mesh):
    gx, gz = mesh.shape["gx"], mesh.shape["gz"]
    inner = Mesh(mesh.devices.reshape(SPLIT[gx] + (gz,)), ALONG + ("gz",))
    field = P("gz", ALONG, None)
    return jax.shard_map(
        shards,
        mesh=inner,
        in_specs=(field,) * 8 + (P(),) * 3,
        out_specs=(field,) * 5,
        check_vma=False,
    )
```

```python
import math

import jax
import jax.numpy as jnp
import numpy as np
from jax import lax
from jax.experimental import pallas as pl
from jax.experimental.pallas import tpu as pltpu
from jax.sharding import Mesh, PartitionSpec as P

f32 = jnp.float32
bf16 = jnp.bfloat16
LANES = 128
ROWS = 8
SPLIT = {128: (8, 2, 4, 2)}
ALONG = ("z", "yh", "x", "c")
GROUP = ("yh", "x", "c")
GROUP_ALL = ("yh", "x", "c", "gz")


def hartley_table(length):
    numbers = np.arange(length)
    angle = (numbers[:, None] * numbers[None, :] % length) * (2.0 * math.pi / length)
    return np.cos(angle) + np.sin(angle)


def halves(value):
    upper = value.astype(bf16)
    return upper, (value - upper.astype(f32)).astype(bf16)


def stacked_left(pair):
    upper = jnp.concatenate([pair[0], pair[0]], axis=1)
    lower = jnp.concatenate([pair[1], jnp.zeros_like(pair[1])], axis=1)
    return jnp.concatenate([upper, lower], axis=0)


def stacked_dot(left, pair):
    both = jnp.dot(left, jnp.concatenate(pair, axis=0), preferred_element_type=f32)
    half = both.shape[0] // 2
    return both[:half] + both[half:]


def thrice_left(pair):
    return jnp.concatenate([pair[0], pair[0], pair[1]], axis=1)


def thrice_right(pair):
    return jnp.concatenate([pair[0], pair[1], pair[0]], axis=0)


def split_dot(a, b):
    (a_hi, a_lo), (b_hi, b_lo) = a, b

    def dot(p, q):
        return jnp.dot(p, q, preferred_element_type=f32)

    return dot(a_hi, b_hi) + (dot(a_hi, b_lo) + dot(a_lo, b_hi))


def face_terms(edges, ratio, side=None):
    positive = ratio >= 0.0
    if side == "left":
        d1, d2, d3, d4 = edges[0], edges[1], edges[2], edges[3]
    elif side == "right":
        d1, d2, d3, d4 = edges[4], edges[3], edges[2], edges[1]
    else:
        d1 = jnp.where(positive, edges[0], edges[4])
        d2 = jnp.where(positive, edges[1], edges[3])
        d3 = edges[2]
        d4 = jnp.where(positive, edges[3], edges[1])
    s1, s2, s3 = d2 - d1, d3 - d2, d4 - d3
    e0, e1, e2 = (d2 + d2) + s1, d2 + d3, (d3 + d3) - s3
    t0, t1, t2 = (13.0 / 3.0) * s1, (13.0 / 3.0) * s2, (13.0 / 3.0) * s3
    r0 = 1.0 / (t0 * s1 + (e0 * e0 + 0.04))
    r1 = 1.0 / (t1 * s2 + (e1 * e1 + 0.04))
    r2 = 1.0 / (t2 * s3 + (e2 * e2 + 0.04))
    u0, u1, u2 = (1.0 / 6.0) * (r0 * r0), r1 * r1, 0.5 * (r2 * r2)
    norm = 1.0 / (u0 + u1 + u2)
    w0, w1, w2 = u0 * norm, u1 * norm, u2 * norm
    bend = s1 - s2
    a2, cc = bend + bend, s2 - s3
    z = w0 * a2 + w2 * cc
    total = (e1 + d3) + z
    n0, n1, n2 = w0 * r0 * (z - a2), w1 * r1 * z, w2 * r2 * (z - cc)
    p0, q0 = n0 * t0, n0 * e0
    p1, q1 = n1 * t1, n1 * e1
    p2, q2 = n2 * t2, n2 * e2
    h0, h2 = 0.5 * w0, 0.25 * w2
    lean = h0 - h2
    m1, m4 = h0 + (p0 + q0), h2 + (q2 - p2)
    g2 = ((0.25 + lean) + m1) + ((q0 + q0) + (q1 - p1))
    g3 = ((0.5 - lean) + m4) + ((q2 + q2) + (p1 + q1))
    return positive, total, (m1, g2, g3, m4)


def weno_tile(field, ratio, cotangent, faces, cells, owned, ends=()):
    edge_of, edge_bar, cell_bar, ratio_bar = {}, {}, {}, {}

    def edge(x):
        if x not in edge_of:
            edge_of[x] = field(x + 1) - field(x)
        return edge_of[x]

    def add(store, key, value, less=False):
        if key in store:
            store[key] = store[key] - value if less else store[key] + value
        else:
            store[key] = -value if less else value

    for f in faces:
        c, e = ratio(f), cotangent(f)
        side = ("right" if f == ends[0] else "left" if f == ends[1] else None) if ends else None
        skip = {"right": 0, "left": 4}.get(side)
        five = [None if k == skip else edge(f - 3 + k) for k in range(5)]
        positive, total, (m1, g2, g3, m4) = face_terms(five, c, side)
        gain = (2.0 / 3.0) * (jnp.abs(c) * e)
        m1, g2, g3, m4 = gain * m1, gain * g2, gain * g3, gain * m4
        zero = jnp.zeros_like(m1)
        add(edge_bar, f - 3, jnp.where(positive, m1, zero), True)
        add(edge_bar, f - 2, jnp.where(positive, g2, -m4))
        add(edge_bar, f - 1, g3)
        add(edge_bar, f, jnp.where(positive, -m4, g2))
        add(edge_bar, f + 1, jnp.where(positive, zero, m1), True)
        add(cell_bar, f - 1, jnp.maximum(c, 0.0) * e)
        add(cell_bar, f, jnp.minimum(c, 0.0) * e)
        if f in owned:
            center = jnp.where(positive, field(f - 1), field(f))
            sixth = total * (1.0 / 6.0)
            ratio_bar[f] = e * (center + jnp.where(positive, sixth, -sixth))
    bars = {}
    for x in cells:
        parts = []
        if x - 1 in edge_bar:
            parts.append(edge_bar[x - 1])
        if x in edge_bar:
            parts.append(-edge_bar[x])
        if x in cell_bar:
            parts.append(cell_bar[x])
        bars[x] = sum(parts[1:], parts[0])
    return bars, ratio_bar


def planes(own, before, after, own_count, before_at, before_count, after_at, lanes):
    def read(x):
        if x < 0:
            return before[before_at + before_count + x, :, lanes]
        if x >= own_count:
            return after[after_at + x - own_count, :, lanes]
        return own[x, :, lanes]

    return read


def tracer_kernel(t, s, c, lt, ls, before, after, t_out, s_out, c_out, left_out, right_out):
    n, _, width = t.shape

    def tile(l, carry):
        lanes = pl.ds(pl.multiple_of(l * LANES, LANES), LANES)
        sums = {}
        for k, (own, dual, out) in enumerate(((t, lt, t_out), (s, ls, s_out))):
            field = planes(own, before, after, n, 3 * k, 3, 2 * k, lanes)
            lam = planes(dual, before, after, n, 6 + k, 1, 0, lanes)
            bars, ratio_bar = weno_tile(
                field,
                lambda f: c[f, :, lanes],
                lambda f: lam(f) - lam(f - 1),
                range(n),
                range(-3, n + 2),
                range(n),
            )
            for x in range(n):
                out[x, :, lanes] = dual[x, :, lanes] + bars[x]
                sums[x] = sums[x] + ratio_bar[x] if x in sums else ratio_bar[x]
            for x in range(3):
                left_out[3 * k + x, :, lanes] = bars[x - 3]
            for x in range(2):
                right_out[2 * k + x, :, lanes] = bars[n + x]
        for x in range(n):
            c_out[x, :, lanes] = sums[x]
        return carry

    lax.fori_loop(0, width // LANES, tile, 0)


def flow_kernel(
    u, c, df, before, after, phi, phi_edge, t_in, s_in, c_in, from_left, from_right,
    t_out, s_out, u_out, c_out,
):
    n, _, width = u.shape

    def tile(l, carry):
        lanes = pl.ds(pl.multiple_of(l * LANES, LANES), LANES)
        field = planes(u, before, after, n, 0, 4, 0, lanes)
        ratio = planes(c, before, after, n, 4, 2, 4, lanes)
        dual = planes(df, before, after, n, 6, 3, 7, lanes)
        head = planes(phi, phi_edge, phi_edge, n, 0, 3, 3, lanes)
        step = {x: head(x) - head(x - 1) for x in range(-2, n + 2)}

        def bend(x):
            if x == -3:
                return phi_edge[5, :, lanes]
            if x == n + 1:
                return phi_edge[6, :, lanes]
            return step[x] - step[x + 1]

        bars, ratio_bar = weno_tile(
            field,
            ratio,
            lambda f: (dual(f) - dual(f - 1)) + bend(f - 1),
            range(-2, n + 3),
            range(n),
            range(n),
            (-2, n + 2),
        )
        for x in range(n):
            u_out[x, :, lanes] = (df[x, :, lanes] - step[x]) + bars[x]
            c_out[x, :, lanes] = c_in[x, :, lanes] + ratio_bar[x]
        for k, (base, out) in enumerate(((t_in, t_out), (s_in, s_out))):
            for x in range(n):
                value = base[x, :, lanes]
                if x < 2:
                    value = value + from_left[2 * k + x, :, lanes]
                if x >= n - 3:
                    value = value + from_right[3 * k + x - (n - 3), :, lanes]
                out[x, :, lanes] = value
        return carry

    lax.fori_loop(0, width // LANES, tile, 0)


def moments_kernel(rows, blocks, head, table_hi, table_lo, depth, rates, waves, u, c, df, spec, coeff, sums, decay, flow_right, flow_left, sems):
    n, levels, columns = head.shape
    width = columns // blocks
    copies = [
        pltpu.make_async_copy(source, target, sems.at[k])
        for k, (source, target) in enumerate(
            (
                (u.at[n - 4 : n], flow_right.at[0:4]),
                (c.at[n - 2 : n], flow_right.at[4:6]),
                (df.at[n - 3 : n], flow_right.at[6:9]),
                (u.at[0:4], flow_left.at[0:4]),
                (c.at[0:3], flow_left.at[4:7]),
                (df.at[0:3], flow_left.at[7:10]),
            )
        )
    ]
    for copy in copies:
        copy.start()
    a = jnp.transpose(jnp.broadcast_to(rates[...], (columns, rates.shape[1]))) + waves[...]
    root = jnp.sqrt(a * (1.0 + 0.25 * a))
    rho = 1.0 / ((1.0 + 0.5 * a) + root)
    coeff[0] = rho
    coeff[1] = 0.5 / root
    coeff[2] = a
    values = head[...].reshape(n * levels, columns)
    values = split_dot(halves(values), (table_hi[...], table_lo[...]))
    spec[...] = values.reshape(n, levels, columns)
    first = lax.axis_index("gz") == 0
    share = jnp.where(first, depth[:, :levels], depth[:, levels:])
    share = thrice_left(halves(share * (-1.0 / columns)))
    for j in range(n):
        part = jnp.dot(share, thrice_right(halves(spec[j])), preferred_element_type=f32)
        if j == 0:
            forward, backward, power = part, part, coeff[0]
        else:
            forward = forward * coeff[0] + part
            backward = backward + power * part
            power = power * coeff[0]
    for i in range(sums.shape[0]):
        m, r = i // blocks * rows, i % blocks * width
        sums[i, 0] = forward[m : m + rows, r : r + width]
        sums[i, 1] = backward[m : m + rows, r : r + width]
    m, r = my_chunk(rows, blocks, width)
    decay[...] = repeated(coeff[0, m, r], n)
    for copy in copies:
        copy.wait()


def pack_kernel(head, t, s, lt, ls, right, left, sems):
    n = head.shape[0]
    copies = [
        pltpu.make_async_copy(source, target, sems.at[k])
        for k, (source, target) in enumerate(
            (
                (t.at[n - 3 : n], right.at[0:3]),
                (s.at[n - 3 : n], right.at[3:6]),
                (lt.at[n - 1 : n], right.at[6:7]),
                (ls.at[n - 1 : n], right.at[7:8]),
                (head.at[n - 3 : n], right.at[8:11]),
                (t.at[0:2], left.at[0:2]),
                (s.at[0:2], left.at[2:4]),
                (head.at[0:2], left.at[4:6]),
            )
        )
    ]
    for copy in copies:
        copy.start()
    for copy in copies:
        copy.wait()


def halo_kernel(before, after, table_hi, table_lo, spec, planes, sems):
    copies = [
        pltpu.make_async_copy(before.at[8:11], planes.at[0:3], sems.at[0]),
        pltpu.make_async_copy(after.at[4:6], planes.at[3:5], sems.at[1]),
    ]
    for copy in copies:
        copy.start()
    for copy in copies:
        copy.wait()
    count, levels, columns = planes.shape
    value = planes[...].reshape(count * levels, columns)
    spec[...] = split_dot(halves(value), (table_hi[...], table_lo[...])).reshape(planes.shape)


def my_chunk(rows, blocks, width):
    n = lax.axis_index("yh")
    for name in GROUP_ALL[1:]:
        n = n * lax.axis_size(name) + lax.axis_index(name)
    m = pl.multiple_of(n // blocks * rows, rows)
    r = pl.multiple_of(n % blocks * width, width)
    return pl.ds(m, rows), pl.ds(r, width)


def repeated(value, times):
    result, power = None, value
    while times:
        if times & 1:
            result = power if result is None else result * power
        power, times = power * power, times >> 1
    return result


def group_kernel(got, decay, out):
    decay = decay[...]
    places, rings = got.shape[0], out.shape[0]
    forward, backward = None, None
    for p in range(places):
        a, b = got[p, 0, 0] + got[p, 1, 0], got[places - 1 - p, 0, 1] + got[places - 1 - p, 1, 1]
        forward = a if forward is None else forward * decay + a
        backward = b if backward is None else backward * decay + b
    mine = lax.axis_index("z")
    factor = repeated(decay, places)
    for k in range(rings):
        out[lax.rem(mine + 1 + k, rings), 0] = forward
        out[lax.rem(mine + 2 * rings - 1 - k, rings), 1] = backward
        forward, backward = forward * factor, backward * factor


def carry_kernel(got, rings, decay, out):
    decay = decay[...]
    places, around = got.shape[0], rings.shape[0]
    closing = 1.0 / (1.0 - repeated(decay, places * around))
    left, right = rings[0, 0], rings[0, 1]
    for k in range(1, around):
        left, right = left + rings[k, 0], right + rings[k, 1]
    left, right = left * closing, right * closing
    for p in range(places):
        q = places - 1 - p
        for g in range(2):
            out[p, g, 0] = left
            out[q, g, 1] = right
        left = left * decay + (got[p, 0, 0] + got[p, 1, 0])
        right = right * decay + (got[q, 0, 1] + got[q, 1, 1])


def source_kernel(own_at, edge_at, own_other_at, edge_other_at, depth_at, out_at, own, edge, own_other, edge_other, depth, out, sems):
    pairs = (
        (depth_at, depth),
        (own_at, own),
        (own_other_at, own_other),
        (edge_at, edge),
        (edge_other_at, edge_other),
    )
    copies = [pltpu.make_async_copy(p, q, sems.at[k]) for k, (p, q) in enumerate(pairs)]
    for copy in copies:
        copy.start()
    half = own.shape[1]
    n = own.shape[0]
    copies[0].wait()
    first = lax.axis_index("gz") == 0
    matrix = depth[...] * (-1.0 / own.shape[2])
    here = jnp.where(first, matrix[:, :half], matrix[:, half:])
    there = jnp.where(first, matrix[:, half:], matrix[:, :half])
    matrix = stacked_left(halves(jnp.concatenate([here, there], axis=1)))

    def product(mine, other):
        return stacked_dot(matrix, halves(jnp.concatenate([mine, other], axis=0)))

    copies[1].wait()
    copies[2].wait()
    for j in range(n):
        out[3 + j] = product(own[j], own_other[j])
    copies.append(pltpu.make_async_copy(out.at[3 : 3 + n], out_at.at[3 : 3 + n], sems.at[5]))
    copies[5].start()
    copies[3].wait()
    copies[4].wait()
    for j in range(5):
        out[j if j < 3 else j + n] = product(edge[j], edge_other[j])
    for k, (first, count) in enumerate(((0, 3), (3 + n, 2))):
        part = pl.ds(first, count)
        copies.append(pltpu.make_async_copy(out.at[part], out_at.at[part], sems.at[6 + k]))
        copies[6 + k].start()
    for copy in copies[5:]:
        copy.wait()


def solve_kernel(rows, blocks, source_at, carries_at, coeff_at, basis_at, hi_at, lo_at, phi, phi_edge, solved, levels_hi, levels_lo, source, carries, coeff, basis, table_hi, table_lo, heads, sems):
    pairs = (
        (carries_at, carries),
        (coeff_at, coeff),
        (source_at, source),
        (basis_at, basis),
        (hi_at, table_hi),
        (lo_at, table_lo),
    )
    copies = [pltpu.make_async_copy(p, q, sems.at[k]) for k, (p, q) in enumerate(pairs)]
    for copy in copies:
        copy.start()
    for copy in copies[:3]:
        copy.wait()
    count = source.shape[0]
    n = count - 5
    columns = source.shape[2]
    width = columns // blocks
    half = basis.shape[0] // 2

    def chunk(i, carry):
        m = pl.ds(pl.multiple_of(i // blocks * rows, rows), rows)
        r = pl.ds(pl.multiple_of(i % blocks * width, width), width)
        rho, kappa, a = coeff[0, m, r], coeff[1, m, r], coeff[2, m, r]
        growth = (2.0 + a) - rho
        f = [source[j, m, r] for j in range(count)]
        c, b = [None] * count, [None] * count
        c[2] = carries[i, 0]
        c[1] = (c[2] - f[2]) * growth
        c[0] = (c[1] - f[1]) * growth
        for j in range(3, count):
            c[j] = f[j] + rho * c[j - 1]
        b[n + 3] = carries[i, 1]
        b[n + 4] = (b[n + 3] - f[n + 3]) * growth
        for j in range(n + 2, -1, -1):
            b[j] = f[j] + rho * b[j + 1]
        values = [kappa * ((c[j] - f[j]) + b[j]) for j in range(count)]
        values.append(f[0] - a * values[0])
        values.append(f[count - 1] - a * values[count - 1])
        for j, value in enumerate(values):
            solved[j, m, r] = value
        return carry

    lax.fori_loop(0, carries.shape[0], chunk, 0)
    for copy in copies[3:]:
        copy.wait()
    first = lax.axis_index("gz") == 0
    share = stacked_left(halves(jnp.where(first, basis[:half, :], basis[half:, :])))

    def plane(j, carry):
        value = stacked_dot(share, halves(solved[j]))
        here = pl.ds(pl.multiple_of(j * half, half), half)
        levels_hi[here, :], levels_lo[here, :] = halves(value)
        return carry

    lax.fori_loop(0, count + 2, plane, 0)
    result = split_dot((levels_hi[...], levels_lo[...]), (table_hi[...], table_lo[...]))
    heads[...] = result.reshape(count + 2, half, columns)
    pairs = (
        (heads.at[3 : 3 + n], phi),
        (heads.at[0:3], phi_edge.at[0:3]),
        (heads.at[3 + n : count + 2], phi_edge.at[3:7]),
    )
    copies = [pltpu.make_async_copy(p, q, sems.at[6 + k]) for k, (p, q) in enumerate(pairs)]
    for copy in copies:
        copy.start()
    for copy in copies:
        copy.wait()


AWAY = pl.BlockSpec(memory_space=pltpu.HBM)


def params():
    return pltpu.CompilerParams(vmem_limit_bytes=63 * 1024 * 1024)


def cost(us):
    return pl.CostEstimate(flops=int(us * 1e6), bytes_accessed=int(us * 3e6), transcendentals=0)


def call(kernel, outs, *args, scratch=(), us=2.0, name, away=(), out_away=()):
    many = isinstance(outs, (list, tuple))

    def whole(a):
        return pl.BlockSpec(a.shape, lambda i: (0,) * len(a.shape), pipeline_mode=pl.Buffered(1))

    return pl.pallas_call(
        kernel,
        grid=(1,),
        out_shape=outs,
        in_specs=[AWAY if k in away else whole(a) for k, a in enumerate(args)],
        out_specs=[AWAY if k in out_away else whole(a) for k, a in enumerate(outs)]
        if many
        else whole(outs),
        scratch_shapes=list(scratch),
        compiler_params=params(),
        cost_estimate=cost(us),
        name=name,
    )(*args)


def near(kernel, outs, *args, us, name, scratch=(), away=(), out_away=(), limit=48):
    where = pl.BlockSpec(memory_space=pltpu.VMEM)
    return pl.pallas_call(
        kernel,
        out_shape=outs,
        in_specs=[AWAY if k in away else where for k in range(len(args))],
        out_specs=[AWAY if k in out_away else where for k in range(len(outs))]
        if isinstance(outs, list)
        else where,
        scratch_shapes=list(scratch),
        compiler_params=pltpu.CompilerParams(vmem_limit_bytes=limit * 1024 * 1024),
        cost_estimate=cost(us),
        name=name,
    )(*args)


def by_rows(kernel, outs, *args, us, name, counts={}):
    levels, columns = args[0].shape[1:]

    def spec(a, count=None):
        return pl.BlockSpec((count or a.shape[0], ROWS, columns), lambda i: (0, i, 0))

    return pl.pallas_call(
        kernel,
        grid=(levels // ROWS,),
        out_shape=outs,
        in_specs=[spec(a, counts.get(k)) for k, a in enumerate(args)],
        out_specs=[spec(o) for o in outs],
        compiler_params=params(),
        cost_estimate=cost(us),
        name=name,
    )(*args)


def shards(
    thermal_anomaly,
    saltiness_anomaly,
    eastward_flow,
    advective_ratio,
    dual_thermal_final,
    dual_saltiness_final,
    dual_flow_final,
    dual_kinematic_head,
    depth_into_eigenbasis,
    eigenbasis_into_depth,
    spectral_magnitudes,
):
    t, s, u, c, lt, ls, df, head = (
        jnp.transpose(a, (1, 0, 2))
        for a in (
            thermal_anomaly,
            saltiness_anomaly,
            eastward_flow,
            advective_ratio,
            dual_thermal_final,
            dual_saltiness_final,
            dual_flow_final,
            dual_kinematic_head,
        )
    )
    n, levels, columns = t.shape
    modes = depth_into_eigenbasis.shape[0]
    across = lax.axis_size(ALONG)
    places = lax.axis_size(GROUP)
    rings = lax.axis_size("z")
    chunks = places * lax.axis_size("gz")
    rows = max(ROWS, modes // chunks)
    blocks = chunks * rows // modes
    width = columns // blocks

    def to_right(block):
        return lax.ppermute(block, ALONG, [(i, (i + 1) % across) for i in range(across)])

    def to_left(block):
        return lax.ppermute(block, ALONG, [((i + 1) % across, i) for i in range(across)])

    def other_half(block):
        return lax.ppermute(block, "gz", [(0, 1), (1, 0)])

    def like(*shape):
        return jax.ShapeDtypeStruct(shape, f32)

    exact = hartley_table(columns)
    upper = exact.astype(np.float32).astype(jnp.bfloat16)
    table_hi = jnp.asarray(upper)
    table_lo = jnp.asarray((exact - upper.astype(np.float64)).astype(jnp.bfloat16))
    waves = jnp.asarray(
        (2.0 - 2.0 * np.cos(np.arange(columns) * (2.0 * math.pi / columns))).astype(np.float32)
    ).reshape(1, columns)

    right, left = call(
        pack_kernel,
        [like(11, levels, columns), like(6, levels, columns)],
        head, t, s, lt, ls,
        scratch=[pltpu.SemaphoreType.DMA((8,))],
        away=range(5),
        us=2.0,
        name="pack",
    )
    before, after = to_right(right), to_left(left)

    spec, coeff, sums, decay, flow_right, flow_left = call(
        lambda *refs: moments_kernel(rows, blocks, *refs),
        [
            like(n, levels, columns),
            like(3, modes, columns),
            like(chunks, 2, rows, width),
            like(rows, width),
            like(9, levels, columns),
            like(10, levels, columns),
        ],
        head, table_hi, table_lo, depth_into_eigenbasis,
        spectral_magnitudes.reshape(1, modes), waves, u, c, df,
        scratch=[pltpu.SemaphoreType.DMA((6,))],
        away=(6, 7, 8),
        us=5.0,
        name="block_moments",
    )
    gathered = lax.all_to_all(sums, GROUP_ALL, 0, 0, tiled=True)
    t_base, s_base, c_base, to_left_part, to_right_part = by_rows(
        tracer_kernel,
        [like(n, levels, columns)] * 3 + [like(6, levels, columns), like(4, levels, columns)],
        t, s, c, lt, ls, before, after,
        us=9.0,
        name="tracers",
        counts={5: 8, 6: 4},
    )
    gathered, t_base, late, edge_before, edge_after = lax.optimization_barrier(
        (gathered, t_base, spec, before, after)
    )
    spec_other = other_half(late)
    gathered = gathered.reshape(places, chunks // places, 2, rows, width)
    edge = call(
        halo_kernel,
        like(5, levels, columns),
        edge_before, edge_after, table_hi, table_lo,
        scratch=[pltpu.VMEM((5, levels, columns), f32), pltpu.SemaphoreType.DMA((2,))],
        away=(0, 1),
        us=2.0,
        name="edge_spectrum",
    )
    edge_other = other_half(edge)

    ring = near(
        group_kernel,
        like(rings, 2, rows, width),
        gathered, decay,
        us=1.0,
        name="group_moments",
    )
    ring = lax.all_to_all(ring, "z", 0, 0, tiled=True)
    from_right = to_left(to_left_part)
    from_left = to_right(to_right_part)
    ring, spec_other, flow_right, flow_left, from_right, from_left = lax.optimization_barrier(
        (ring, spec_other, flow_right, flow_left, from_right, from_left)
    )
    flow_before, flow_after = to_right(flow_right), to_left(flow_left)
    carries = near(
        carry_kernel,
        like(places, chunks // places, 2, rows, width),
        gathered, ring, decay,
        us=1.0,
        name="group_carries",
    )
    carries = lax.all_to_all(carries.reshape(chunks, 2, rows, width), GROUP_ALL, 0, 0, tiled=True)

    (source,) = near(
        source_kernel,
        [like(n + 5, modes, columns)],
        spec, edge, spec_other, edge_other, depth_into_eigenbasis,
        scratch=[
            pltpu.VMEM((n, levels, columns), f32),
            pltpu.VMEM((5, levels, columns), f32),
            pltpu.VMEM((n, levels, columns), f32),
            pltpu.VMEM((5, levels, columns), f32),
            pltpu.VMEM((modes, modes), f32),
            pltpu.VMEM((n + 5, modes, columns), f32),
            pltpu.SemaphoreType.DMA((8,)),
        ],
        away=range(5),
        out_away=(0,),
        us=4.0,
        limit=63,
        name="mode_source",
    )
    phi, phi_edge = near(
        lambda *refs: solve_kernel(rows, blocks, *refs),
        [like(n, levels, columns), like(7, levels, columns)],
        source, carries, coeff, eigenbasis_into_depth, table_hi, table_lo,
        scratch=[pltpu.VMEM((n + 7, modes, columns), f32)]
        + [pltpu.VMEM(((n + 7) * levels, columns), bf16)] * 2
        + [
            pltpu.VMEM((n + 5, modes, columns), f32),
            pltpu.VMEM((chunks, 2, rows, width), f32),
            pltpu.VMEM((3, modes, columns), f32),
            pltpu.VMEM((modes, modes), f32),
            pltpu.VMEM((columns, columns), bf16),
            pltpu.VMEM((columns, columns), bf16),
            pltpu.VMEM((n + 7, levels, columns), f32),
            pltpu.SemaphoreType.DMA((9,)),
        ],
        away=range(6),
        out_away=(0, 1),
        us=7.0,
        limit=63,
        name="pressure",
    )
    t_bar, s_bar, u_bar, c_bar = by_rows(
        flow_kernel,
        [like(n, levels, columns)] * 4,
        u, c, df, flow_before, flow_after, phi, phi_edge,
        t_base, s_base, c_base, from_left, from_right,
        us=7.0,
        name="flow",
    )
    return tuple(jnp.transpose(a, (1, 0, 2)) for a in (t_bar, s_bar, u_bar, c_bar, phi))


def solution(mesh):
    gx, gz = mesh.shape["gx"], mesh.shape["gz"]
    inner = Mesh(mesh.devices.reshape(SPLIT[gx] + (gz,)), ALONG + ("gz",))
    field = P("gz", ALONG, None)
    return jax.shard_map(
        shards,
        mesh=inner,
        in_specs=(field,) * 8 + (P(),) * 3,
        out_specs=(field,) * 5,
        check_vma=False,
    )
```

```python
import math

import jax
import jax.numpy as jnp
import numpy as np
from jax import lax
from jax.experimental import pallas as pl
from jax.experimental.pallas import tpu as pltpu
from jax.sharding import Mesh, PartitionSpec as P

f32 = jnp.float32
bf16 = jnp.bfloat16
LANES = 128
ROWS = 8
SPLIT = {128: (8, 2, 4, 2)}
ALONG = ("z", "yh", "x", "c")
GROUP = ("yh", "x", "c")
GROUP_ALL = ("yh", "x", "c", "gz")


def hartley_table(length):
    numbers = np.arange(length)
    angle = (numbers[:, None] * numbers[None, :] % length) * (2.0 * math.pi / length)
    return np.cos(angle) + np.sin(angle)


def halves(value):
    upper = value.astype(bf16)
    return upper, (value - upper.astype(f32)).astype(bf16)


def stacked_left(pair):
    upper = jnp.concatenate([pair[0], pair[0]], axis=1)
    lower = jnp.concatenate([pair[1], jnp.zeros_like(pair[1])], axis=1)
    return jnp.concatenate([upper, lower], axis=0)


def stacked_dot(left, pair):
    both = jnp.dot(left, jnp.concatenate(pair, axis=0), preferred_element_type=f32)
    half = both.shape[0] // 2
    return both[:half] + both[half:]


def thrice_left(pair):
    return jnp.concatenate([pair[0], pair[0], pair[1]], axis=1)


def thrice_right(pair):
    return jnp.concatenate([pair[0], pair[1], pair[0]], axis=0)


def split_dot(a, b):
    (a_hi, a_lo), (b_hi, b_lo) = a, b

    def dot(p, q):
        return jnp.dot(p, q, preferred_element_type=f32)

    return dot(a_hi, b_hi) + (dot(a_hi, b_lo) + dot(a_lo, b_hi))


def face_terms(edges, ratio, side=None):
    positive = ratio >= 0.0
    if side == "left":
        d1, d2, d3, d4 = edges[0], edges[1], edges[2], edges[3]
    elif side == "right":
        d1, d2, d3, d4 = edges[4], edges[3], edges[2], edges[1]
    else:
        d1 = jnp.where(positive, edges[0], edges[4])
        d2 = jnp.where(positive, edges[1], edges[3])
        d3 = edges[2]
        d4 = jnp.where(positive, edges[3], edges[1])
    s1, s2, s3 = d2 - d1, d3 - d2, d4 - d3
    e0, e1, e2 = (d2 + d2) + s1, d2 + d3, (d3 + d3) - s3
    t0, t1, t2 = (13.0 / 3.0) * s1, (13.0 / 3.0) * s2, (13.0 / 3.0) * s3
    r0 = 1.0 / (t0 * s1 + (e0 * e0 + 0.04))
    r1 = 1.0 / (t1 * s2 + (e1 * e1 + 0.04))
    r2 = 1.0 / (t2 * s3 + (e2 * e2 + 0.04))
    u0, u1, u2 = (1.0 / 6.0) * (r0 * r0), r1 * r1, 0.5 * (r2 * r2)
    norm = 1.0 / (u0 + u1 + u2)
    w0, w1, w2 = u0 * norm, u1 * norm, u2 * norm
    bend = s1 - s2
    a2, cc = bend + bend, s2 - s3
    z = w0 * a2 + w2 * cc
    total = (e1 + d3) + z
    n0, n1, n2 = w0 * r0 * (z - a2), w1 * r1 * z, w2 * r2 * (z - cc)
    p0, q0 = n0 * t0, n0 * e0
    p1, q1 = n1 * t1, n1 * e1
    p2, q2 = n2 * t2, n2 * e2
    h0, h2 = 0.5 * w0, 0.25 * w2
    lean = h0 - h2
    m1, m4 = h0 + (p0 + q0), h2 + (q2 - p2)
    g2 = ((0.25 + lean) + m1) + ((q0 + q0) + (q1 - p1))
    g3 = ((0.5 - lean) + m4) + ((q2 + q2) + (p1 + q1))
    return positive, total, (m1, g2, g3, m4)


def weno_tile(field, ratio, cotangent, faces, cells, owned, ends=()):
    edge_of, edge_bar, cell_bar, ratio_bar = {}, {}, {}, {}

    def edge(x):
        if x not in edge_of:
            edge_of[x] = field(x + 1) - field(x)
        return edge_of[x]

    def add(store, key, value, less=False):
        if key in store:
            store[key] = store[key] - value if less else store[key] + value
        else:
            store[key] = -value if less else value

    for f in faces:
        c, e = ratio(f), cotangent(f)
        side = ("right" if f == ends[0] else "left" if f == ends[1] else None) if ends else None
        skip = {"right": 0, "left": 4}.get(side)
        five = [None if k == skip else edge(f - 3 + k) for k in range(5)]
        positive, total, (m1, g2, g3, m4) = face_terms(five, c, side)
        gain = (2.0 / 3.0) * (jnp.abs(c) * e)
        m1, g2, g3, m4 = gain * m1, gain * g2, gain * g3, gain * m4
        zero = jnp.zeros_like(m1)
        add(edge_bar, f - 3, jnp.where(positive, m1, zero), True)
        add(edge_bar, f - 2, jnp.where(positive, g2, -m4))
        add(edge_bar, f - 1, g3)
        add(edge_bar, f, jnp.where(positive, -m4, g2))
        add(edge_bar, f + 1, jnp.where(positive, zero, m1), True)
        add(cell_bar, f - 1, jnp.maximum(c, 0.0) * e)
        add(cell_bar, f, jnp.minimum(c, 0.0) * e)
        if f in owned:
            center = jnp.where(positive, field(f - 1), field(f))
            sixth = total * (1.0 / 6.0)
            ratio_bar[f] = e * (center + jnp.where(positive, sixth, -sixth))
    bars = {}
    for x in cells:
        parts = []
        if x - 1 in edge_bar:
            parts.append(edge_bar[x - 1])
        if x in edge_bar:
            parts.append(-edge_bar[x])
        if x in cell_bar:
            parts.append(cell_bar[x])
        bars[x] = sum(parts[1:], parts[0])
    return bars, ratio_bar


def planes(own, before, after, own_count, before_at, before_count, after_at, lanes):
    def read(x):
        if x < 0:
            return before[before_at + before_count + x, :, lanes]
        if x >= own_count:
            return after[after_at + x - own_count, :, lanes]
        return own[x, :, lanes]

    return read


def tracer_kernel(t, s, c, lt, ls, before, after, t_out, s_out, c_out, left_out, right_out):
    n, _, width = t.shape

    def tile(l, carry):
        lanes = pl.ds(pl.multiple_of(l * LANES, LANES), LANES)
        sums = {}
        for k, (own, dual, out) in enumerate(((t, lt, t_out), (s, ls, s_out))):
            field = planes(own, before, after, n, 3 * k, 3, 2 * k, lanes)
            lam = planes(dual, before, after, n, 6 + k, 1, 0, lanes)
            bars, ratio_bar = weno_tile(
                field,
                lambda f: c[f, :, lanes],
                lambda f: lam(f) - lam(f - 1),
                range(n),
                range(-3, n + 2),
                range(n),
            )
            for x in range(n):
                out[x, :, lanes] = dual[x, :, lanes] + bars[x]
                sums[x] = sums[x] + ratio_bar[x] if x in sums else ratio_bar[x]
            for x in range(3):
                left_out[3 * k + x, :, lanes] = bars[x - 3]
            for x in range(2):
                right_out[2 * k + x, :, lanes] = bars[n + x]
        for x in range(n):
            c_out[x, :, lanes] = sums[x]
        return carry

    lax.fori_loop(0, width // LANES, tile, 0)


def flow_kernel(
    u, c, df, before, after, phi, phi_edge, t_in, s_in, c_in, from_left, from_right,
    t_out, s_out, u_out, c_out,
):
    n, _, width = u.shape

    def tile(l, carry):
        lanes = pl.ds(pl.multiple_of(l * LANES, LANES), LANES)
        field = planes(u, before, after, n, 0, 4, 0, lanes)
        ratio = planes(c, before, after, n, 4, 2, 4, lanes)
        dual = planes(df, before, after, n, 6, 3, 7, lanes)
        head = planes(phi, phi_edge, phi_edge, n, 0, 3, 3, lanes)
        step = {x: head(x) - head(x - 1) for x in range(-2, n + 2)}

        def bend(x):
            if x == -3:
                return phi_edge[5, :, lanes]
            if x == n + 1:
                return phi_edge[6, :, lanes]
            return step[x] - step[x + 1]

        bars, ratio_bar = weno_tile(
            field,
            ratio,
            lambda f: (dual(f) - dual(f - 1)) + bend(f - 1),
            range(-2, n + 3),
            range(n),
            range(n),
            (-2, n + 2),
        )
        for x in range(n):
            u_out[x, :, lanes] = (df[x, :, lanes] - step[x]) + bars[x]
            c_out[x, :, lanes] = c_in[x, :, lanes] + ratio_bar[x]
        for k, (base, out) in enumerate(((t_in, t_out), (s_in, s_out))):
            for x in range(n):
                value = base[x, :, lanes]
                if x < 2:
                    value = value + from_left[2 * k + x, :, lanes]
                if x >= n - 3:
                    value = value + from_right[3 * k + x - (n - 3), :, lanes]
                out[x, :, lanes] = value
        return carry

    lax.fori_loop(0, width // LANES, tile, 0)


def moments_kernel(rows, blocks, head, table_hi, table_lo, depth, rates, waves, u, c, df, spec, coeff, sums, decay, flow_right, flow_left, sems):
    n, levels, columns = head.shape
    width = columns // blocks
    copies = [
        pltpu.make_async_copy(source, target, sems.at[k])
        for k, (source, target) in enumerate(
            (
                (u.at[n - 4 : n], flow_right.at[0:4]),
                (c.at[n - 2 : n], flow_right.at[4:6]),
                (df.at[n - 3 : n], flow_right.at[6:9]),
                (u.at[0:4], flow_left.at[0:4]),
                (c.at[0:3], flow_left.at[4:7]),
                (df.at[0:3], flow_left.at[7:10]),
            )
        )
    ]
    for copy in copies:
        copy.start()
    a = jnp.transpose(jnp.broadcast_to(rates[...], (columns, rates.shape[1]))) + waves[...]
    root = jnp.sqrt(a * (1.0 + 0.25 * a))
    rho = 1.0 / ((1.0 + 0.5 * a) + root)
    coeff[0] = rho
    coeff[1] = 0.5 / root
    coeff[2] = a
    values = head[...].reshape(n * levels, columns)
    values = split_dot(halves(values), (table_hi[...], table_lo[...]))
    spec[...] = values.reshape(n, levels, columns)
    first = lax.axis_index("gz") == 0
    share = jnp.where(first, depth[:, :levels], depth[:, levels:])
    share = thrice_left(halves(share * (-1.0 / columns)))
    for j in range(n):
        part = jnp.dot(share, thrice_right(halves(spec[j])), preferred_element_type=f32)
        if j == 0:
            forward, backward, power = part, part, coeff[0]
        else:
            forward = forward * coeff[0] + part
            backward = backward + power * part
            power = power * coeff[0]
    for i in range(sums.shape[0]):
        m, r = i // blocks * rows, i % blocks * width
        sums[i, 0] = forward[m : m + rows, r : r + width]
        sums[i, 1] = backward[m : m + rows, r : r + width]
    m, r = my_chunk(rows, blocks, width)
    decay[...] = repeated(coeff[0, m, r], n)
    for copy in copies:
        copy.wait()


def pack_kernel(head, t, s, lt, ls, right, left, sems):
    n = head.shape[0]
    copies = [
        pltpu.make_async_copy(source, target, sems.at[k])
        for k, (source, target) in enumerate(
            (
                (t.at[n - 3 : n], right.at[0:3]),
                (s.at[n - 3 : n], right.at[3:6]),
                (lt.at[n - 1 : n], right.at[6:7]),
                (ls.at[n - 1 : n], right.at[7:8]),
                (head.at[n - 3 : n], right.at[8:11]),
                (t.at[0:2], left.at[0:2]),
                (s.at[0:2], left.at[2:4]),
                (head.at[0:2], left.at[4:6]),
            )
        )
    ]
    for copy in copies:
        copy.start()
    for copy in copies:
        copy.wait()


def halo_kernel(before, after, table_hi, table_lo, spec, planes, sems):
    copies = [
        pltpu.make_async_copy(before.at[8:11], planes.at[0:3], sems.at[0]),
        pltpu.make_async_copy(after.at[4:6], planes.at[3:5], sems.at[1]),
    ]
    for copy in copies:
        copy.start()
    for copy in copies:
        copy.wait()
    count, levels, columns = planes.shape
    value = planes[...].reshape(count * levels, columns)
    spec[...] = split_dot(halves(value), (table_hi[...], table_lo[...])).reshape(planes.shape)


def my_chunk(rows, blocks, width):
    n = lax.axis_index("yh")
    for name in GROUP_ALL[1:]:
        n = n * lax.axis_size(name) + lax.axis_index(name)
    m = pl.multiple_of(n // blocks * rows, rows)
    r = pl.multiple_of(n % blocks * width, width)
    return pl.ds(m, rows), pl.ds(r, width)


def repeated(value, times):
    result, power = None, value
    while times:
        if times & 1:
            result = power if result is None else result * power
        power, times = power * power, times >> 1
    return result


def group_kernel(got, decay, out):
    decay = decay[...]
    places, rings = got.shape[0], out.shape[0]
    forward, backward = None, None
    for p in range(places):
        a, b = got[p, 0, 0] + got[p, 1, 0], got[places - 1 - p, 0, 1] + got[places - 1 - p, 1, 1]
        forward = a if forward is None else forward * decay + a
        backward = b if backward is None else backward * decay + b
    mine = lax.axis_index("z")
    factor = repeated(decay, places)
    for k in range(rings):
        out[lax.rem(mine + 1 + k, rings), 0] = forward
        out[lax.rem(mine + 2 * rings - 1 - k, rings), 1] = backward
        forward, backward = forward * factor, backward * factor


def carry_kernel(got, rings, decay, out):
    decay = decay[...]
    places, around = got.shape[0], rings.shape[0]
    closing = 1.0 / (1.0 - repeated(decay, places * around))
    left, right = rings[0, 0], rings[0, 1]
    for k in range(1, around):
        left, right = left + rings[k, 0], right + rings[k, 1]
    left, right = left * closing, right * closing
    for p in range(places):
        q = places - 1 - p
        for g in range(2):
            out[p, g, 0] = left
            out[q, g, 1] = right
        left = left * decay + (got[p, 0, 0] + got[p, 1, 0])
        right = right * decay + (got[q, 0, 1] + got[q, 1, 1])


def source_kernel(own_at, edge_at, own_other_at, edge_other_at, depth_at, out_at, own, edge, own_other, edge_other, depth, out, sems):
    pairs = (
        (depth_at, depth),
        (own_at, own),
        (own_other_at, own_other),
        (edge_at, edge),
        (edge_other_at, edge_other),
    )
    copies = [pltpu.make_async_copy(p, q, sems.at[k]) for k, (p, q) in enumerate(pairs)]
    for copy in copies:
        copy.start()
    half = own.shape[1]
    n = own.shape[0]
    copies[0].wait()
    first = lax.axis_index("gz") == 0
    matrix = depth[...] * (-1.0 / own.shape[2])
    here = jnp.where(first, matrix[:, :half], matrix[:, half:])
    there = jnp.where(first, matrix[:, half:], matrix[:, :half])
    matrix = stacked_left(halves(jnp.concatenate([here, there], axis=1)))

    def product(mine, other):
        return stacked_dot(matrix, halves(jnp.concatenate([mine, other], axis=0)))

    copies[1].wait()
    copies[2].wait()
    for j in range(n):
        out[3 + j] = product(own[j], own_other[j])
    copies.append(pltpu.make_async_copy(out.at[3 : 3 + n], out_at.at[3 : 3 + n], sems.at[5]))
    copies[5].start()
    copies[3].wait()
    copies[4].wait()
    for j in range(5):
        out[j if j < 3 else j + n] = product(edge[j], edge_other[j])
    for k, (first, count) in enumerate(((0, 3), (3 + n, 2))):
        part = pl.ds(first, count)
        copies.append(pltpu.make_async_copy(out.at[part], out_at.at[part], sems.at[6 + k]))
        copies[6 + k].start()
    for copy in copies[5:]:
        copy.wait()


def solve_kernel(rows, blocks, source_at, carries_at, coeff_at, basis_at, hi_at, lo_at, phi, phi_edge, solved, levels_hi, levels_lo, source, carries, coeff, basis, table_hi, table_lo, heads, sems):
    pairs = (
        (carries_at, carries),
        (coeff_at, coeff),
        (source_at, source),
        (basis_at, basis),
        (hi_at, table_hi),
        (lo_at, table_lo),
    )
    copies = [pltpu.make_async_copy(p, q, sems.at[k]) for k, (p, q) in enumerate(pairs)]
    for copy in copies:
        copy.start()
    for copy in copies[:3]:
        copy.wait()
    count = source.shape[0]
    n = count - 5
    columns = source.shape[2]
    width = columns // blocks
    half = basis.shape[0] // 2

    def chunk(i, carry):
        m = pl.ds(pl.multiple_of(i // blocks * rows, rows), rows)
        r = pl.ds(pl.multiple_of(i % blocks * width, width), width)
        rho, kappa, a = coeff[0, m, r], coeff[1, m, r], coeff[2, m, r]
        growth = (2.0 + a) - rho
        f = [source[j, m, r] for j in range(count)]
        c, b = [None] * count, [None] * count
        c[2] = carries[i, 0]
        c[1] = (c[2] - f[2]) * growth
        c[0] = (c[1] - f[1]) * growth
        for j in range(3, count):
            c[j] = f[j] + rho * c[j - 1]
        b[n + 3] = carries[i, 1]
        b[n + 4] = (b[n + 3] - f[n + 3]) * growth
        for j in range(n + 2, -1, -1):
            b[j] = f[j] + rho * b[j + 1]
        values = [kappa * ((c[j] - f[j]) + b[j]) for j in range(count)]
        values.append(f[0] - a * values[0])
        values.append(f[count - 1] - a * values[count - 1])
        for j, value in enumerate(values):
            solved[j, m, r] = value
        return carry

    lax.fori_loop(0, carries.shape[0], chunk, 0)
    for copy in copies[3:]:
        copy.wait()
    first = lax.axis_index("gz") == 0
    share = stacked_left(halves(jnp.where(first, basis[:half, :], basis[half:, :])))

    def plane(j, carry):
        value = stacked_dot(share, halves(solved[j]))
        here = pl.ds(pl.multiple_of(j * half, half), half)
        levels_hi[here, :], levels_lo[here, :] = halves(value)
        return carry

    lax.fori_loop(0, count + 2, plane, 0)
    result = split_dot((levels_hi[...], levels_lo[...]), (table_hi[...], table_lo[...]))
    heads[...] = result.reshape(count + 2, half, columns)
    pairs = (
        (heads.at[3 : 3 + n], phi),
        (heads.at[0:3], phi_edge.at[0:3]),
        (heads.at[3 + n : count + 2], phi_edge.at[3:7]),
    )
    copies = [pltpu.make_async_copy(p, q, sems.at[6 + k]) for k, (p, q) in enumerate(pairs)]
    for copy in copies:
        copy.start()
    for copy in copies:
        copy.wait()


AWAY = pl.BlockSpec(memory_space=pltpu.HBM)


def params():
    return pltpu.CompilerParams(vmem_limit_bytes=63 * 1024 * 1024)


def cost(us):
    return pl.CostEstimate(flops=int(us * 1e6), bytes_accessed=int(us * 3e6), transcendentals=0)


def call(kernel, outs, *args, scratch=(), us=2.0, name, away=(), out_away=()):
    many = isinstance(outs, (list, tuple))

    def whole(a):
        return pl.BlockSpec(a.shape, lambda i: (0,) * len(a.shape), pipeline_mode=pl.Buffered(1))

    return pl.pallas_call(
        kernel,
        grid=(1,),
        out_shape=outs,
        in_specs=[AWAY if k in away else whole(a) for k, a in enumerate(args)],
        out_specs=[AWAY if k in out_away else whole(a) for k, a in enumerate(outs)]
        if many
        else whole(outs),
        scratch_shapes=list(scratch),
        compiler_params=params(),
        cost_estimate=cost(us),
        name=name,
    )(*args)


def near(kernel, outs, *args, us, name, scratch=(), away=(), out_away=(), limit=48):
    where = pl.BlockSpec(memory_space=pltpu.VMEM)
    return pl.pallas_call(
        kernel,
        out_shape=outs,
        in_specs=[AWAY if k in away else where for k in range(len(args))],
        out_specs=[AWAY if k in out_away else where for k in range(len(outs))]
        if isinstance(outs, list)
        else where,
        scratch_shapes=list(scratch),
        compiler_params=pltpu.CompilerParams(vmem_limit_bytes=limit * 1024 * 1024),
        cost_estimate=cost(us),
        name=name,
    )(*args)


def by_rows(kernel, outs, *args, us, name, counts={}):
    levels, columns = args[0].shape[1:]

    def spec(a, count=None):
        return pl.BlockSpec((count or a.shape[0], ROWS, columns), lambda i: (0, i, 0))

    return pl.pallas_call(
        kernel,
        grid=(levels // ROWS,),
        out_shape=outs,
        in_specs=[spec(a, counts.get(k)) for k, a in enumerate(args)],
        out_specs=[spec(o) for o in outs],
        compiler_params=params(),
        cost_estimate=cost(us),
        name=name,
    )(*args)


def shards(
    thermal_anomaly,
    saltiness_anomaly,
    eastward_flow,
    advective_ratio,
    dual_thermal_final,
    dual_saltiness_final,
    dual_flow_final,
    dual_kinematic_head,
    depth_into_eigenbasis,
    eigenbasis_into_depth,
    spectral_magnitudes,
):
    t, s, u, c, lt, ls, df, head = (
        jnp.transpose(a, (1, 0, 2))
        for a in (
            thermal_anomaly,
            saltiness_anomaly,
            eastward_flow,
            advective_ratio,
            dual_thermal_final,
            dual_saltiness_final,
            dual_flow_final,
            dual_kinematic_head,
        )
    )
    n, levels, columns = t.shape
    modes = depth_into_eigenbasis.shape[0]
    across = lax.axis_size(ALONG)
    places = lax.axis_size(GROUP)
    rings = lax.axis_size("z")
    chunks = places * lax.axis_size("gz")
    rows = max(ROWS, modes // chunks)
    blocks = chunks * rows // modes
    width = columns // blocks

    def to_right(block):
        return lax.ppermute(block, ALONG, [(i, (i + 1) % across) for i in range(across)])

    def to_left(block):
        return lax.ppermute(block, ALONG, [((i + 1) % across, i) for i in range(across)])

    def other_half(block):
        return lax.ppermute(block, "gz", [(0, 1), (1, 0)])

    def like(*shape):
        return jax.ShapeDtypeStruct(shape, f32)

    exact = hartley_table(columns)
    upper = exact.astype(np.float32).astype(jnp.bfloat16)
    table_hi = jnp.asarray(upper)
    table_lo = jnp.asarray((exact - upper.astype(np.float64)).astype(jnp.bfloat16))
    waves = jnp.asarray(
        (2.0 - 2.0 * np.cos(np.arange(columns) * (2.0 * math.pi / columns))).astype(np.float32)
    ).reshape(1, columns)

    right, left = call(
        pack_kernel,
        [like(11, levels, columns), like(6, levels, columns)],
        head, t, s, lt, ls,
        scratch=[pltpu.SemaphoreType.DMA((8,))],
        away=range(5),
        us=2.0,
        name="pack",
    )
    before, after = to_right(right), to_left(left)

    spec, coeff, sums, decay, flow_right, flow_left = call(
        lambda *refs: moments_kernel(rows, blocks, *refs),
        [
            like(n, levels, columns),
            like(3, modes, columns),
            like(chunks, 2, rows, width),
            like(rows, width),
            like(9, levels, columns),
            like(10, levels, columns),
        ],
        head, table_hi, table_lo, depth_into_eigenbasis,
        spectral_magnitudes.reshape(1, modes), waves, u, c, df,
        scratch=[pltpu.SemaphoreType.DMA((6,))],
        away=(6, 7, 8),
        us=5.0,
        name="block_moments",
    )
    gathered = lax.all_to_all(sums, GROUP_ALL, 0, 0, tiled=True)
    before, after, flow_right, flow_left = lax.optimization_barrier(
        (before, after, flow_right, flow_left)
    )
    flow_before, flow_after = to_right(flow_right), to_left(flow_left)
    t_base, s_base, c_base, to_left_part, to_right_part = by_rows(
        tracer_kernel,
        [like(n, levels, columns)] * 3 + [like(6, levels, columns), like(4, levels, columns)],
        t, s, c, lt, ls, before, after,
        us=9.0,
        name="tracers",
        counts={5: 8, 6: 4},
    )
    gathered, t_base, late, edge_before, edge_after = lax.optimization_barrier(
        (gathered, t_base, spec, before, after)
    )
    spec_other = other_half(late)
    gathered = gathered.reshape(places, chunks // places, 2, rows, width)
    edge = call(
        halo_kernel,
        like(5, levels, columns),
        edge_before, edge_after, table_hi, table_lo,
        scratch=[pltpu.VMEM((5, levels, columns), f32), pltpu.SemaphoreType.DMA((2,))],
        away=(0, 1),
        us=2.0,
        name="edge_spectrum",
    )
    edge_other = other_half(edge)

    ring = near(
        group_kernel,
        like(rings, 2, rows, width),
        gathered, decay,
        us=1.0,
        name="group_moments",
    )
    ring = lax.all_to_all(ring, "z", 0, 0, tiled=True)
    ring, spec_other = lax.optimization_barrier((ring, spec_other))
    carries = near(
        carry_kernel,
        like(places, chunks // places, 2, rows, width),
        gathered, ring, decay,
        us=1.0,
        name="group_carries",
    )
    carries = lax.all_to_all(carries.reshape(chunks, 2, rows, width), GROUP_ALL, 0, 0, tiled=True)
    from_right = to_left(to_left_part)
    from_left = to_right(to_right_part)

    (source,) = near(
        source_kernel,
        [like(n + 5, modes, columns)],
        spec, edge, spec_other, edge_other, depth_into_eigenbasis,
        scratch=[
            pltpu.VMEM((n, levels, columns), f32),
            pltpu.VMEM((5, levels, columns), f32),
            pltpu.VMEM((n, levels, columns), f32),
            pltpu.VMEM((5, levels, columns), f32),
            pltpu.VMEM((modes, modes), f32),
            pltpu.VMEM((n + 5, modes, columns), f32),
            pltpu.SemaphoreType.DMA((8,)),
        ],
        away=range(5),
        out_away=(0,),
        us=4.0,
        limit=63,
        name="mode_source",
    )
    phi, phi_edge = near(
        lambda *refs: solve_kernel(rows, blocks, *refs),
        [like(n, levels, columns), like(7, levels, columns)],
        source, carries, coeff, eigenbasis_into_depth, table_hi, table_lo,
        scratch=[pltpu.VMEM((n + 7, modes, columns), f32)]
        + [pltpu.VMEM(((n + 7) * levels, columns), bf16)] * 2
        + [
            pltpu.VMEM((n + 5, modes, columns), f32),
            pltpu.VMEM((chunks, 2, rows, width), f32),
            pltpu.VMEM((3, modes, columns), f32),
            pltpu.VMEM((modes, modes), f32),
            pltpu.VMEM((columns, columns), bf16),
            pltpu.VMEM((columns, columns), bf16),
            pltpu.VMEM((n + 7, levels, columns), f32),
            pltpu.SemaphoreType.DMA((9,)),
        ],
        away=range(6),
        out_away=(0, 1),
        us=7.0,
        limit=63,
        name="pressure",
    )
    t_bar, s_bar, u_bar, c_bar = by_rows(
        flow_kernel,
        [like(n, levels, columns)] * 4,
        u, c, df, flow_before, flow_after, phi, phi_edge,
        t_base, s_base, c_base, from_left, from_right,
        us=7.0,
        name="flow",
    )
    return tuple(jnp.transpose(a, (1, 0, 2)) for a in (t_bar, s_bar, u_bar, c_bar, phi))


def solution(mesh):
    gx, gz = mesh.shape["gx"], mesh.shape["gz"]
    inner = Mesh(mesh.devices.reshape(SPLIT[gx] + (gz,)), ALONG + ("gz",))
    field = P("gz", ALONG, None)
    return jax.shard_map(
        shards,
        mesh=inner,
        in_specs=(field,) * 8 + (P(),) * 3,
        out_specs=(field,) * 5,
        check_vma=False,
    )
```
